32 devices in a mesh: dp: 8 (over z, y), mp: 4 (over x, core).
Axes of the slice: x: 2, y: 2, z: 4, core: 2. Of those that a mesh axis runs over, the one named last changes fastest.
Arguments:
- patches: bfloat16 [32, 197, 768], P(('dp', 'mp')), may hold values from -6 to 6
- row_mask: int32 [32, 197], P(('dp', 'mp')), may hold values from 0 to 1, as said below
- out_grad: bfloat16 [32, 197, 768], P(('dp', 'mp')), may hold values from -6 to 6
- rel_index: int32 [197, 197], replicated, may hold values from 0 to 731
- mask_token: float32 [768], replicated, may hold values from -6 to 6
- ln1_gain: float32 [768], replicated, may hold values from 0.5 to 1.5
- ln1_bias: float32 [768], replicated, may hold values from -4 to 4
- qkv_weight: bfloat16 [768, 2304], replicated, may hold values from -0.21875 to 0.21875
- query_bias: float32 [768], replicated, may hold values from -6 to 6
- value_bias: float32 [768], replicated, may hold values from -6 to 6
- rel_table: float32 [732, 12], replicated, may hold values from -6 to 6
- proj_weight: bfloat16 [768, 768], replicated, may hold values from -0.625 to 0.625
- proj_bias: float32 [768], replicated, may hold values from -4 to 4
- gamma1: float32 [768], replicated, may hold values from 0.5 to 1.5
- ln2_gain: float32 [768], replicated, may hold values from 0.5 to 1.5
- ln2_bias: float32 [768], replicated, may hold values from -4 to 4
- fc1_weight: bfloat16 [768, 3072], P(None, 'mp'), may hold values from -0.21875 to 0.21875
- fc1_bias: bfloat16 [3072], P('mp'), may hold values from -6 to 6
- fc2_weight: bfloat16 [3072, 768], P('mp'), may hold values from -0.109375 to 0.109375
- fc2_bias: float32 [768], replicated, may hold values from -4 to 4
- gamma2: float32 [768], replicated, may hold values from 0.5 to 1.5
Outputs:
- layer_out: bfloat16 [32, 197, 768], P(('dp', 'mp'))
- patch_grad: float32 [32, 197, 768], P(('dp', 'mp'))
- mask_token_grad: float32 [768], replicated
- ln1_gain_grad: float32 [768], replicated
- ln1_bias_grad: float32 [768], replicated
- qkv_weight_grad: float32 [768, 2304], P('dp')
- query_bias_grad: float32 [768], replicated
- value_bias_grad: float32 [768], replicated
- rel_table_grad: float32 [732, 12], replicated
- proj_weight_grad: float32 [768, 768], P('dp')
- proj_bias_grad: float32 [768], replicated
- gamma1_grad: float32 [768], replicated
- ln2_gain_grad: float32 [768], replicated
- ln2_bias_grad: float32 [768], replicated
- fc1_weight_grad: float32 [768, 3072], P('dp', 'mp')
- fc1_bias_grad: float32 [3072], P('mp')
- fc2_weight_grad: float32 [3072, 768], P('mp', 'dp')
- fc2_bias_grad: float32 [768], replicated
- gamma2_grad: float32 [768], replicated
The draws below stay inside these ranges and needn't reach their ends.
Inputs may be any that keep to these rules, and one draw needn't show every extreme that they name: `row_mask`: row 0 of every image (the class row) is never masked. The number of masked rows differs widely from image to image, and in some images every one of the 196 patch rows is masked.
All inputs are finite; a program needn't handle non-finite values.
Results may differ from the reference program's by a relative error of at most 0.015.
Values may be sent and summed in bfloat16 or wider, within the bound.
No kernel may reach another device: no remote copies, remote signals or barrier semaphores. Data moves between devices by JAX's collectives and lax.ppermute only.
A program may use at most 128 MiB of HBM per device.

```python
import math
import jax
import jax.numpy as jnp
from jax import lax

D = 768
HEADS = 12
HEAD_DIM = 64
FF = 3072
ROWS = 197
REL = 732
IMAGES = 32


def draw_row_mask(key, part):
    first, second, third = jax.random.split(jax.random.fold_in(key, 71), 3)
    patch_rows = ROWS - 1
    level = jax.random.randint(first, (IMAGES,), 0, ROWS)
    cubed = level * level // ROWS * level // ROWS
    flipped = jax.random.randint(second, (IMAGES,), 0, 2)
    counts = jnp.where(flipped > 0, patch_rows - cubed, cubed)
    image_ids = jnp.arange(IMAGES, dtype=jnp.int32)
    counts = jnp.where(image_ids % 16 == 5, patch_rows, counts)
    counts = jnp.clip(counts, 0, patch_rows)
    scores = jax.random.randint(third, (IMAGES, patch_rows), 0, 1 << 20) * patch_rows
    scores = scores + jnp.arange(patch_rows, dtype=jnp.int32)[None, :]
    order = jnp.argsort(scores, axis=1)
    ranks = jnp.argsort(order, axis=1).astype(jnp.int32)
    patch_mask = (ranks < counts[:, None]).astype(jnp.int32)
    class_col = jnp.zeros((IMAGES, 1), jnp.int32)
    return jnp.concatenate([class_col, patch_mask], axis=1)


def set_ends(result, own_key, least, largest):
    longest = result.shape.index(max(result.shape))
    spots = []
    for shift in (0, 1):
        where = [jax.random.randint(jax.random.fold_in(own_key, axis), (), 0, length) for axis, length in enumerate(result.shape)]
        where[longest] = (where[longest] + shift) % result.shape[longest]
        spots.append(tuple(where))
    return result.at[spots[0]].set(least).at[spots[1]].set(largest)


def levels(stream_key, extent, shards, least, largest):
    factor_of, own = 1.0, jax.random.fold_in(stream_key, 6)
    for axis_at, parts in shards:
        draws = jnp.exp(jax.random.uniform(jax.random.fold_in(own, axis_at), (parts,), jnp.float32, least / len(shards), largest / len(shards)))
        factor_of = factor_of * jnp.repeat(draws, extent[axis_at] // parts).reshape([-1 if axis == axis_at else 1 for axis in range(len(extent))])
    return factor_of


def noise(key, dims, deviation, most, cuts=(), kind=jnp.bfloat16):
    values = jax.random.normal(key, dims, jnp.float32) * deviation
    if len(cuts) > 0:
        values = levels(key, dims, cuts, -0.22, 0.18) * values
    return jnp.clip(values, min=-most, max=most).astype(kind)


def setup_inputs(seed: int = 0) -> dict:
    key_of = jax.random.split(jax.random.key(seed), 22)
    patches = noise(key_of[0], (IMAGES, ROWS, D), 1.0, 6.0, ((0, 32),))
    row_mask = draw_row_mask(jax.random.fold_in(key_of[21], 71), 0)
    out_grad = noise(key_of[2], (IMAGES, ROWS, D), 1.0, 6.0, ((0, 32),))
    rel_index = set_ends(jax.random.randint(key_of[3], (ROWS, ROWS), 0, REL), jax.random.fold_in(key_of[3], 1), 0, REL - 1).astype(jnp.int32)
    mask_token = noise(key_of[4], (D,), 1.0, 6.0, (), jnp.float32)
    ln1_gain = jnp.clip(1.0 + 0.1 * jax.random.normal(key_of[5], (D,), jnp.float32), 0.5, 1.5)
    ln1_bias = noise(key_of[6], (D,), 0.3, 4.0, (), jnp.float32)
    qkv_weight = noise(key_of[7], (D, 3 * D), D ** -0.5, 0.21875)
    query_bias = noise(key_of[8], (D,), 0.5, 6.0, (), jnp.float32)
    value_bias = noise(key_of[9], (D,), 0.5, 6.0, (), jnp.float32)
    rel_table = noise(key_of[10], (REL, HEADS), 1.0, 6.0, (), jnp.float32)
    proj_weight = noise(key_of[11], (D, D), (D // 8) ** -0.5, 0.625)
    proj_bias = noise(key_of[12], (D,), 0.3, 4.0, (), jnp.float32)
    gamma1 = jnp.clip(1.0 + 0.1 * jax.random.normal(key_of[13], (D,), jnp.float32), 0.5, 1.5)
    ln2_gain = jnp.clip(1.0 + 0.1 * jax.random.normal(key_of[14], (D,), jnp.float32), 0.5, 1.5)
    ln2_bias = noise(key_of[15], (D,), 0.3, 4.0, (), jnp.float32)
    fc1_weight = noise(key_of[16], (D, FF), D ** -0.5, 0.21875, ((1, 4),))
    fc1_bias = noise(key_of[17], (FF,), 0.5, 6.0, ((0, 4),))
    fc2_weight = noise(key_of[18], (FF, D), FF ** -0.5, 0.109375, ((0, 4),))
    fc2_bias = noise(key_of[19], (D,), 0.3, 4.0, (), jnp.float32)
    gamma2 = jnp.clip(1.0 + 0.1 * jax.random.normal(key_of[20], (D,), jnp.float32), 0.5, 1.5)
    return {"patches": patches, "row_mask": row_mask, "out_grad": out_grad, "rel_index": rel_index, "mask_token": mask_token, "ln1_gain": ln1_gain, "ln1_bias": ln1_bias, "qkv_weight": qkv_weight, "query_bias": query_bias, "value_bias": value_bias, "rel_table": rel_table, "proj_weight": proj_weight, "proj_bias": proj_bias, "gamma1": gamma1, "ln2_gain": ln2_gain, "ln2_bias": ln2_bias, "fc1_weight": fc1_weight, "fc1_bias": fc1_bias, "fc2_weight": fc2_weight, "fc2_bias": fc2_bias, "gamma2": gamma2}


@jax.custom_vjp
def low(v):
    return lax.optimization_barrier(v.astype(jnp.bfloat16)).astype(jnp.float32)

@jax.custom_vjp
def low_back(v):
    return v

def low_keep(v):
    return (low(v), None)

def low_pass(kept, grad):
    return (grad,)

def back_keep(v):
    return (v, None)

def back_low(kept, grad):
    return (low(grad),)
low.defvjp(low_keep, low_pass)
low_back.defvjp(back_keep, back_low)
highest = lax.Precision.HIGHEST

def norm_rows(values, gain, shift):
    middle = lax.optimization_barrier(jnp.mean(values, axis=-1, keepdims=True))
    centred = values - middle
    spread = lax.optimization_barrier(jnp.mean(centred * centred, axis=-1, keepdims=True))
    return centred * lax.rsqrt(spread + 1e-06) * gain + shift

def block_forward(params, x_group, mask_group, rel_index):
    mask_token, ln1_gain, ln1_bias, qkv_weight, query_bias, value_bias, rel_table, proj_weight, proj_bias, gamma1, ln2_gain, ln2_bias, fc1_weight, fc1_bias, fc2_weight, fc2_bias, gamma2 = params
    group_size = x_group.shape[0]
    picked = (mask_group > 0)[..., None]
    start = jnp.where(picked, mask_token, x_group)
    normed = low(norm_rows(start, ln1_gain, ln1_bias))
    bias_row = jnp.concatenate([query_bias, jnp.zeros_like(query_bias), value_bias])
    qkv = low_back(jnp.einsum('bsd,de->bse', normed, qkv_weight, precision=highest) + bias_row)
    shaped = (group_size, ROWS, HEADS, HEAD_DIM)
    query_rows = low(qkv[..., :D] * HEAD_DIM ** (-0.5)).reshape(shaped)
    key_rows = low(qkv[..., D:2 * D]).reshape(shaped)
    value_rows = low(qkv[..., 2 * D:]).reshape(shaped)
    rel_bias = jnp.transpose(rel_table[rel_index], (2, 0, 1))
    scores = low_back(jnp.einsum('bqhe,bkhe->bhqk', query_rows, key_rows, precision=highest) + rel_bias)
    probs = jax.nn.softmax(scores, axis=-1)
    mixed = jnp.einsum('bhqk,bkhe->bqhe', low(probs), value_rows, precision=highest)
    mixed = low(low_back(mixed)).reshape(group_size, ROWS, D)
    attended = low_back(jnp.einsum('bsd,de->bse', mixed, proj_weight, precision=highest) + proj_bias)
    hidden = start + gamma1 * attended
    inner = low(norm_rows(hidden, ln2_gain, ln2_bias))
    pre = low_back(jnp.einsum('bsd,df->bsf', inner, fc1_weight, precision=highest) + fc1_bias)
    act = low(jax.nn.gelu(pre, approximate=False))
    branch = low_back(jnp.einsum('bsf,fd->bsd', act, fc2_weight, precision=highest) + fc2_bias)
    return hidden + gamma2 * branch

def reference(patches, row_mask, out_grad, rel_index, mask_token, ln1_gain, ln1_bias, qkv_weight, query_bias, value_bias, rel_table, proj_weight, proj_bias, gamma1, ln2_gain, ln2_bias, fc1_weight, fc1_bias, fc2_weight, fc2_bias, gamma2):
    params = tuple((item.astype(jnp.float32) for item in (mask_token, ln1_gain, ln1_bias, qkv_weight, query_bias, value_bias, rel_table, proj_weight, proj_bias, gamma1, ln2_gain, ln2_bias, fc1_weight, fc1_bias, fc2_weight, fc2_bias, gamma2)))
    group_size = math.gcd(IMAGES, 16)
    groups = IMAGES // group_size
    inputs = patches.astype(jnp.float32).reshape(groups, group_size, ROWS, D)
    masks = row_mask.reshape(groups, group_size, ROWS)
    cotangent = out_grad.astype(jnp.float32) * (row_mask > 0).astype(jnp.float32)[..., None]
    cotangent = cotangent.reshape(groups, group_size, ROWS, D)

    def one_group(totals, item):
        x_group, mask_group, cot_group = item

        def forward(param_set, start_in):
            return block_forward(param_set, start_in, mask_group, rel_index)
        layer, pull_back = jax.vjp(forward, params, x_group)
        param_grads, input_grad = pull_back(cot_group)
        totals = jax.tree.map(lambda summed, update: summed + update, totals, param_grads)
        return (totals, (layer.astype(jnp.bfloat16), input_grad))
    zeros = jax.tree.map(jnp.zeros_like, params)
    totals, (layers, input_grads) = lax.scan(one_group, zeros, (inputs, masks, cotangent))
    layer_out = layers.reshape(IMAGES, ROWS, D)
    patch_grad = input_grads.reshape(IMAGES, ROWS, D)
    return (layer_out, patch_grad, totals[0], totals[1], totals[2], totals[3], totals[4], totals[5], totals[6], totals[7], totals[8], totals[9], totals[10], totals[11], totals[12], totals[13], totals[14], totals[15], totals[16])
```

```python
import functools

import jax
import jax.numpy as jnp
from jax import lax
from jax.experimental import pallas as pl
from jax.experimental.pallas import tpu as pltpu
from jax.sharding import PartitionSpec as P

F32 = jnp.float32
BF16 = jnp.bfloat16
EPS = 1e-06
LANES = 128
VMEM_LIMIT = 56 * 1024 * 1024


def round_up(value, step):
    return -(-value // step) * step


def dot_nn(left, right):
    return lax.dot_general(left, right, (((1,), (0,)), ((), ())), preferred_element_type=F32)


def dot_nt(left, right):
    return lax.dot_general(left, right, (((1,), (1,)), ((), ())), preferred_element_type=F32)


def dot_tn(left, right):
    return lax.dot_general(left, right, (((0,), (0,)), ((), ())), preferred_element_type=F32)


def row_of(ref):
    return ref[...].reshape(1, ref.shape[0])


def norm_stats(values):
    middle = jnp.mean(values, axis=-1, keepdims=True)
    centred = values - middle
    spread = jnp.mean(centred * centred, axis=-1, keepdims=True)
    root = lax.rsqrt(spread + EPS)
    return centred * root, root


def norm_back(d_out, xhat, root, gain):
    t = d_out * gain
    mean_t = jnp.mean(t, axis=-1, keepdims=True)
    mean_tx = jnp.mean(t * xhat, axis=-1, keepdims=True)
    return root * (t - mean_t - xhat * mean_tx)


def call(body, outs, scratch=(), flops=0, moved=0):
    return pl.pallas_call(
        body,
        out_shape=outs,
        scratch_shapes=list(scratch),
        compiler_params=pltpu.CompilerParams(vmem_limit_bytes=VMEM_LIMIT),
        cost_estimate=pl.CostEstimate(flops=flops, bytes_accessed=moved, transcendentals=0),
    )


def shape(dims, kind):
    return jax.ShapeDtypeStruct(dims, kind)


def load_padded(source_ref, pad_ref):
    rows = source_ref.shape[1]
    tail = (rows // 8) * 8
    pad_ref[tail:, :] = jnp.zeros_like(pad_ref[tail:, :])
    pad_ref[0:rows, :] = source_ref[0].astype(F32)
    return pad_ref[...]


def forward_body(
    heads,
    patches_ref,
    mask_ref,
    index_ref,
    token_ref,
    gain1_ref,
    bias1_ref,
    wqkv_ref,
    qbias_ref,
    vbias_ref,
    table_ref,
    wproj_ref,
    pbias_ref,
    gamma1_ref,
    gain2_ref,
    bias2_ref,
    normed_ref,
    q_ref,
    k_ref,
    v_ref,
    probs_ref,
    mixed_ref,
    attended_ref,
    hidden_ref,
    inner_ref,
    pad_s,
    index_s,
    table_s,
    tablet_s,
):
    rows = patches_ref.shape[1]
    width = patches_ref.shape[2]
    pad = normed_ref.shape[0]
    keys = k_ref.shape[0]
    head_size = width // heads
    picked = mask_ref[...] > 0
    start = jnp.where(picked, row_of(token_ref), load_padded(patches_ref, pad_s))
    xhat, _ = norm_stats(start)
    normed = (xhat * row_of(gain1_ref) + row_of(bias1_ref)).astype(BF16)
    normed_ref[...] = normed
    qkv = dot_nn(normed, wqkv_ref[...])
    scale = head_size ** (-0.5)
    q_ref[...] = ((qkv[:, :width] + row_of(qbias_ref)) * scale).astype(BF16)
    k_ref[0:pad, :] = qkv[:, width : 2 * width].astype(BF16)
    k_ref[pad:, :] = jnp.zeros_like(k_ref[pad:, :])
    v_ref[0:pad, :] = (qkv[:, 2 * width :] + row_of(vbias_ref)).astype(BF16)
    v_ref[pad:, :] = jnp.zeros_like(v_ref[pad:, :])

    index_s[...] = jnp.zeros_like(index_s)
    index_s[0:rows, 0:rows] = index_ref[...]
    table_s[...] = jnp.zeros_like(table_s)
    table_s[0 : table_ref.shape[0], 0:heads] = table_ref[...]
    chunks = table_s.shape[0] // LANES
    for chunk in range(chunks):
        part = slice(chunk * LANES, (chunk + 1) * LANES)
        flipped = table_s[part, :].T
        for head in range(heads):
            tablet_s[head, :, part] = flipped[head : head + 1, :]
    lane = lax.broadcasted_iota(jnp.int32, (1, LANES), 1)
    first = lane < head_size
    key_lane = lax.broadcasted_iota(jnp.int32, (1, keys), 1)

    def rel_bias(head):
        halves = []
        for half in range(keys // LANES):
            at = index_s[:, half * LANES : (half + 1) * LANES]
            low = lax.rem(at, LANES)
            high = lax.div(at, LANES)
            value = jnp.zeros((pad, LANES), F32)
            for chunk in range(chunks):
                line = tablet_s[head, :, chunk * LANES : (chunk + 1) * LANES]
                found = jnp.take_along_axis(
                    jnp.broadcast_to(line, (pad, LANES)), low, axis=1, mode="promise_in_bounds"
                )
                value = jnp.where(high == chunk, found, value)
            halves.append(value)
        return jnp.where(key_lane < rows, jnp.concatenate(halves, axis=1), -1e30)

    def pair_step(pair, carry):
        at = pl.ds(pl.multiple_of(pair * LANES, LANES), LANES)
        query = q_ref[:, at]
        key = k_ref[:, at]
        value = v_ref[:, at]
        outs = []
        for side in range(2):
            head = pair * 2 + side
            own = first if side == 0 else jnp.logical_not(first)
            scores = dot_nt(jnp.where(own, query, jnp.zeros_like(query)), key) + rel_bias(head)
            top = jnp.max(scores, axis=-1, keepdims=True)
            grown = jnp.exp(scores - top)
            probs = (grown / jnp.sum(grown, axis=-1, keepdims=True)).astype(BF16)
            probs_ref[head] = probs
            outs.append(dot_nn(probs, value))
        mixed_ref[:, at] = jnp.where(first, outs[0], outs[1]).astype(BF16)
        return carry

    lax.fori_loop(0, heads // 2, pair_step, 0)
    attended = dot_nn(mixed_ref[...], wproj_ref[...]) + row_of(pbias_ref)
    attended_ref[...] = attended
    hidden = start + row_of(gamma1_ref) * attended
    hidden_ref[...] = hidden
    xhat2, _ = norm_stats(hidden)
    inner_ref[...] = (xhat2 * row_of(gain2_ref) + row_of(bias2_ref)).astype(BF16)


def forward(heads, patches, mask_col, rel_index, token, gain1, bias1, wqkv, qbias, vbias, table,
            wproj, pbias, gamma1, gain2, bias2):
    rows, width = patches.shape[1:]
    pad = mask_col.shape[0]
    keys = round_up(pad, LANES)
    entries = round_up(table.shape[0], LANES)
    outs = (
        shape((pad, width), BF16),
        shape((pad, width), BF16),
        shape((keys, width), BF16),
        shape((keys, width), BF16),
        shape((heads, pad, keys), BF16),
        shape((pad, width), BF16),
        shape((pad, width), F32),
        shape((pad, width), F32),
        shape((pad, width), BF16),
    )
    return call(
        functools.partial(forward_body, heads),
        outs,
        (
            pltpu.VMEM((pad, width), F32),
            pltpu.VMEM((pad, keys), jnp.int32),
            pltpu.VMEM((entries, LANES), F32),
            pltpu.VMEM((heads, 1, entries), F32),
        ),
        flops=10**10,
        moved=2 * 10**7,
    )(patches, mask_col, rel_index, token, gain1, bias1, wqkv, qbias, vbias, table, wproj, pbias,
      gamma1, gain2, bias2)


def mlp_body(
    inner_ref, dbranch_ref, w1a_ref, w1b_ref, w2a_ref, w2b_ref, b1a_ref, b1b_ref,
    acta_ref, actb_ref, dprea_ref, dpreb_ref, branch_ref, dinner_ref, sums_ref,
):
    inner = inner_ref[...]
    dbranch = dbranch_ref[...]
    branch = None
    dinner = None
    for at, (w1, w2, b1, act_out, dpre_out) in enumerate((
        (w1a_ref, w2a_ref, b1a_ref, acta_ref, dprea_ref),
        (w1b_ref, w2b_ref, b1b_ref, actb_ref, dpreb_ref),
    )):
        pre = dot_nn(inner, w1[...]) + row_of(b1).astype(F32)
        phi = 0.5 + 0.5 * lax.erf(pre * (0.5**0.5))
        act = (pre * phi).astype(BF16)
        act_out[...] = act
        slope = phi + pre * (jnp.exp(-0.5 * pre * pre) * 0.3989422804014327)
        dact = dot_nt(dbranch, w2[...])
        dpre = (dact * slope).astype(BF16)
        dpre_out[...] = dpre
        sums_ref[at : at + 1, :] = jnp.sum(dpre.astype(F32), axis=0, keepdims=True)
        this_branch = dot_nn(act, w2[...])
        this_dinner = dot_nt(dpre, w1[...])
        branch = this_branch if branch is None else branch + this_branch
        dinner = this_dinner if dinner is None else dinner + this_dinner
    branch_ref[...] = branch.astype(branch_ref.dtype)
    dinner_ref[...] = dinner.astype(dinner_ref.dtype)


def mlp(inner, dbranch, w1a, w1b, w2a, w2b, b1a, b1b, kind):
    pad, width = inner.shape
    ff = w1a.shape[1]
    outs = (
        shape((pad, ff), BF16),
        shape((pad, ff), BF16),
        shape((pad, ff), BF16),
        shape((pad, ff), BF16),
        shape((pad, width), kind),
        shape((pad, width), kind),
        shape((8, ff), F32),
    )
    return call(mlp_body, outs, flops=10**10, moved=10**7)(
        inner, dbranch, w1a, w1b, w2a, w2b, b1a, b1b
    )


def mlp_grad_body(add, inner0, inner1, dpre0, dpre1, act0, act1, dbr0, dbr1, *rest):
    out_ref = rest[-1]
    for at, (left0, left1, right0, right1) in enumerate(
        ((inner0, inner1, dpre0, dpre1), (dbr0, dbr1, act0, act1))
    ):
        total = dot_tn(left0[...], right0[...]) + dot_tn(left1[...], right1[...])
        if add:
            total = total + rest[0][at].astype(F32)
        out_ref[at] = total.astype(BF16)


def mlp_grad(inner0, inner1, dpre0, dpre1, act0, act1, dbr0, dbr1, other=None):
    width = inner0.shape[1]
    ff = act0.shape[1]
    extra = () if other is None else (other,)
    return call(
        functools.partial(mlp_grad_body, other is not None),
        shape((2, width, ff), BF16),
        flops=10**10,
        moved=10**7,
    )(inner0, inner1, dpre0, dpre1, act0, act1, dbr0, dbr1, *extra)


def backward_body(
    heads,
    rows,
    where_ref,
    dinner0_ref,
    dinner1_ref,
    hidden_ref,
    attended_ref,
    outgrad_ref,
    mask_ref,
    gain2_ref,
    gamma1_ref,
    wproj_ref,
    q_ref,
    k_ref,
    v_ref,
    probs_ref,
    dhidden_ref,
    dattsend_ref,
    dattkeep_ref,
    dqkv_ref,
    dqkvsend_ref,
    dscores_ref,
    sums_ref,
    pad_s,
    dmixed_s,
):
    pad, width = hidden_ref.shape
    head_size = width // heads
    cotangent = load_padded(outgrad_ref, pad_s) * mask_ref[...]
    xhat, root = norm_stats(hidden_ref[...])
    dinner = dinner0_ref[...].astype(F32) + dinner1_ref[...].astype(F32)
    dhidden = cotangent + norm_back(dinner, xhat, root, row_of(gain2_ref))
    dhidden_ref[...] = dhidden
    datt = (row_of(gamma1_ref) * dhidden).astype(BF16)
    high = where_ref[0] > 0
    half = width // 2
    dattsend_ref[...] = jnp.where(high, datt[:, :half], datt[:, half:])
    dattkeep_ref[...] = jnp.where(high, datt[:, half:], datt[:, :half])
    dmixed_s[...] = dot_nt(datt, wproj_ref[...]).astype(BF16)
    sums_ref[0:1, :] = jnp.sum(dinner * xhat, axis=0, keepdims=True)
    sums_ref[1:2, :] = jnp.sum(dinner, axis=0, keepdims=True)
    sums_ref[2:3, :] = jnp.sum(dhidden * attended_ref[...], axis=0, keepdims=True)
    sums_ref[3:4, :] = jnp.sum(datt.astype(F32), axis=0, keepdims=True)

    lane = lax.broadcasted_iota(jnp.int32, (1, LANES), 1)
    first = lane < head_size
    scale = head_size ** (-0.5)

    def pair_step(pair, carry):
        start = pl.multiple_of(pair * LANES, LANES)
        at = pl.ds(start, LANES)
        query = q_ref[:, at]
        key = k_ref[:, at]
        value = v_ref[:, at]
        dmixed = dmixed_s[:, at]
        dq, dk, dv = [], [], []
        for side in range(2):
            head = pair * 2 + side
            own = first if side == 0 else jnp.logical_not(first)
            probs_b = probs_ref[head]
            probs = probs_b.astype(F32)
            dprobs = dot_nt(jnp.where(own, dmixed, jnp.zeros_like(dmixed)), value)
            inside = jnp.sum(probs * dprobs, axis=-1, keepdims=True)
            dscores = (probs * (dprobs - inside)).astype(BF16)
            dscores_ref[head] = dscores
            dq.append(dot_nn(dscores, key))
            dk.append(dot_tn(dscores, query))
            dv.append(dot_tn(probs_b, dmixed))
        dqkv_ref[:, at] = (jnp.where(first, dq[0], dq[1]) * scale).astype(BF16)
        dqkv_ref[:, pl.ds(pl.multiple_of(start + width, LANES), LANES)] = (
            jnp.where(first, dk[0], dk[1])[:pad].astype(BF16)
        )
        dqkv_ref[:, pl.ds(pl.multiple_of(start + 2 * width, LANES), LANES)] = (
            jnp.where(first, dv[0], dv[1])[:pad].astype(BF16)
        )
        return carry

    lax.fori_loop(0, heads // 2, pair_step, 0)
    three = 3 * width // 2
    dqkvsend_ref[...] = jnp.where(high, dqkv_ref[:, :three], dqkv_ref[:, three:])
    sums_ref[4:5, :] = jnp.sum(dqkv_ref[:, :width].astype(F32), axis=0, keepdims=True)
    sums_ref[5:6, :] = jnp.sum(dqkv_ref[:, 2 * width :].astype(F32), axis=0, keepdims=True)
    sums_ref[6:8, :] = jnp.zeros((2, width), F32)


def with_scalars(body, outs, scratch, n_in, flops=10**10, moved=10**7):
    return pl.pallas_call(
        body,
        out_shape=outs,
        in_specs=[pl.BlockSpec(memory_space=pltpu.SMEM)]
        + [pl.BlockSpec(memory_space=pltpu.VMEM)] * n_in,
        scratch_shapes=list(scratch),
        compiler_params=pltpu.CompilerParams(vmem_limit_bytes=VMEM_LIMIT),
        cost_estimate=pl.CostEstimate(flops=flops, bytes_accessed=moved, transcendentals=0),
    )


def backward(heads, where, dinner0, dinner1, hidden, attended, out_grad, mask_col, gain2, gamma1,
             wproj, q, k, v, probs):
    pad, width = hidden.shape
    keys = k.shape[0]
    half, three = width // 2, 3 * width // 2
    outs = (
        shape((pad, width), F32),
        shape((pad, half), BF16),
        shape((pad, half), BF16),
        shape((pad, 3 * width), BF16),
        shape((pad, three), BF16),
        shape((heads, pad, keys), BF16),
        shape((8, width), F32),
    )
    scratch = (pltpu.VMEM((pad, width), F32), pltpu.VMEM((pad, width), BF16))
    return with_scalars(
        functools.partial(backward_body, heads, out_grad.shape[1]), outs, scratch, 13
    )(where, dinner0, dinner1, hidden, attended, out_grad, mask_col, gain2, gamma1, wproj, q, k, v,
      probs)


def first_norm_body(
    patches_ref, mask_ref, token_ref, gain1_ref, dqkv_ref, wqkv_ref, dhidden_ref,
    patchgrad_ref, sums_ref, pad_s,
):
    rows, width = patches_ref.shape[1:]
    mask = mask_ref[...]
    picked = mask > 0
    start = jnp.where(picked, row_of(token_ref), load_padded(patches_ref, pad_s))
    xhat, root = norm_stats(start)
    dnormed = dot_nt(dqkv_ref[...], wqkv_ref[...])
    dstart = dhidden_ref[...] + norm_back(dnormed, xhat, root, row_of(gain1_ref))
    patchgrad_ref[0] = jnp.where(picked, 0.0, dstart)[0:rows]
    sums_ref[0:1, :] = jnp.sum(jnp.where(picked, dstart, 0.0), axis=0, keepdims=True)
    sums_ref[1:2, :] = jnp.sum(dnormed * xhat, axis=0, keepdims=True)
    sums_ref[2:3, :] = jnp.sum(dnormed, axis=0, keepdims=True)
    sums_ref[3:8, :] = jnp.zeros((5, width), F32)


def first_norm(patches, mask_col, token, gain1, dqkv, wqkv, dhidden):
    rows, width = patches.shape[1:]
    pad = mask_col.shape[0]
    outs = (shape((1, rows, width), F32), shape((8, width), F32))
    return call(
        first_norm_body, outs, (pltpu.VMEM((pad, width), F32),), flops=10**9, moved=10**7
    )(patches, mask_col, token, gain1, dqkv, wqkv, dhidden)


def layer_end_body(
    hidden_ref, branch0_ref, branch1_ref, bias_ref, gamma2_ref, outgrad_ref, mask_ref, dbranch_ref,
    out_ref, sums_ref, pad_s,
):
    rows, width = outgrad_ref.shape[1:]
    branch = branch0_ref[...].astype(F32) + branch1_ref[...].astype(F32) + row_of(bias_ref)
    layer = hidden_ref[...] + row_of(gamma2_ref) * branch
    out_ref[0] = layer[0:rows].astype(BF16)
    cotangent = load_padded(outgrad_ref, pad_s) * mask_ref[...]
    sums_ref[0:1, :] = jnp.sum(dbranch_ref[...].astype(F32), axis=0, keepdims=True)
    sums_ref[1:2, :] = jnp.sum(cotangent * branch, axis=0, keepdims=True)
    sums_ref[2:8, :] = jnp.zeros((6, width), F32)


def layer_end(hidden, branch0, branch1, bias, gamma2, out_grad, mask_col, dbranch):
    rows, width = out_grad.shape[1:]
    pad = hidden.shape[0]
    outs = (shape((1, rows, width), BF16), shape((8, width), F32))
    return call(
        layer_end_body, outs, (pltpu.VMEM((pad, width), F32),), flops=10**8, moved=10**7
    )(hidden, branch0, branch1, bias, gamma2, out_grad, mask_col, dbranch)


def table_grad_body(index_ref, ds_ref, out_ref, index_s):
    rows = index_ref.shape[0]
    high_count, head_pad, _ = out_ref.shape
    pad, keys = index_s.shape
    index_s[...] = jnp.zeros_like(index_s)
    index_s[0:rows, 0:rows] = index_ref[...]
    out_ref[...] = jnp.zeros_like(out_ref)
    below = lax.broadcasted_iota(jnp.int32, (LANES, keys), 0)

    def step(group, carry):
        base = pl.multiple_of(group * 8, 8)
        lines = index_s[pl.ds(base, 8), :]
        low = lax.rem(lines, LANES)
        high = lax.div(lines, LANES)
        total = jnp.zeros((high_count * head_pad, LANES), F32)
        for i in range(8):
            onehot = jnp.where(below == low[i : i + 1], 1.0, 0.0).astype(BF16)
            ds = ds_ref[base + i].astype(F32)
            left = jnp.concatenate(
                [jnp.where(high[i : i + 1] == at, ds, 0.0).astype(BF16) for at in range(high_count)],
                axis=0,
            )
            total = total + dot_nt(left, onehot)
        out_ref[...] += total.reshape(high_count, head_pad, LANES)
        return carry

    lax.fori_loop(0, pad // 8, step, 0)


def table_grad(rel_index, dscores, entries):
    pad, head_pad, keys = dscores.shape
    high_count = round_up(entries, LANES) // LANES
    return call(
        table_grad_body,
        shape((high_count, head_pad, LANES), F32),
        (pltpu.VMEM((pad, keys), jnp.int32),),
        flops=10**10,
        moved=10**7,
    )(rel_index, dscores)


def late_grad_body(
    add, where_ref, normed0, normed1, mixed0, mixed1, dqkv_ref, dqkv1_ref, datt0, datt1, *rest
):
    out_ref = rest[-1]
    width = normed0.shape[1]
    half, three = width // 2, 3 * width // 2
    high = where_ref[0] > 0
    core = where_ref[1] > 0
    second = core if add else jnp.logical_not(core)
    own = jnp.where(high, dqkv_ref[:, three:], dqkv_ref[:, :three])
    total0, total1 = None, None
    for normed_ref, mixed_ref, part, datt_ref in (
        (normed0, mixed0, own, datt0),
        (normed1, mixed1, dqkv1_ref[...], datt1),
    ):
        normed = normed_ref[...]
        right0 = jnp.where(second, part[:, width:], part[:, :half])
        left1 = jnp.where(second, mixed_ref[...], normed)
        right1 = jnp.where(second, datt_ref[...], part[:, half:width])
        this0 = dot_tn(normed, right0)
        this1 = dot_tn(left1, right1)
        total0 = this0 if total0 is None else total0 + this0
        total1 = this1 if total1 is None else total1 + this1
    if add:
        total0 = total0 + rest[0][:, :half].astype(F32)
        total1 = total1 + rest[0][:, half:].astype(F32)
    out_ref[:, :half] = total0.astype(BF16)
    out_ref[:, half:] = total1.astype(BF16)


def late_grad(where, normed0, normed1, mixed0, mixed1, dqkv, dqkv1, datt0, datt1, other=None):
    width = normed0.shape[1]
    extra = () if other is None else (other,)
    return with_scalars(
        functools.partial(late_grad_body, other is not None),
        shape((width, width), BF16),
        (),
        8 + len(extra),
    )(where, normed0, normed1, mixed0, mixed1, dqkv, dqkv1, datt0, datt1, *extra)


def on_device(
    dp,
    patches,
    row_mask,
    out_grad,
    rel_index,
    mask_token,
    ln1_gain,
    ln1_bias,
    qkv_weight,
    query_bias,
    value_bias,
    rel_table,
    proj_weight,
    proj_bias,
    gamma1,
    ln2_gain,
    ln2_bias,
    fc1_weight,
    fc1_bias,
    fc2_weight,
    fc2_bias,
    gamma2,
):
    rows, width = patches.shape[1:]
    entries, heads = rel_table.shape
    pad = round_up(rows, 16)
    mp_at = lax.axis_index("mp")
    dp_at = lax.axis_index("dp")
    x_at, core_at, low_at = mp_at // 2, mp_at % 2, dp_at % 2
    where = jnp.stack([x_at, core_at]).astype(jnp.int32)

    def swap(axis, bit):
        count = 4 if axis == "mp" else dp
        pairs = [(at, at ^ bit) for at in range(count)]
        return lambda value: lax.ppermute(value, axis, pairs)

    over_core, over_x = swap("mp", 1), swap("mp", 2)

    mask_col = jnp.pad(
        (row_mask > 0).astype(F32).reshape(rows, 1), ((0, pad - rows), (0, 0))
    )
    dbranch = jnp.pad(
        (gamma2 * (out_grad[0].astype(F32) * mask_col[:rows])).astype(BF16),
        ((0, pad - rows), (0, 0)),
    )
    dbranch1 = over_x(dbranch)
    w1b, w2b, b1b = over_core(fc1_weight), over_core(fc2_weight), over_core(fc1_bias)

    normed, q, k, v, probs, mixed, attended, hidden, inner = forward(
        heads, patches, mask_col, rel_index, mask_token, ln1_gain, ln1_bias, qkv_weight,
        query_bias, value_bias, rel_table, proj_weight, proj_bias, gamma1, ln2_gain, ln2_bias,
    )
    inner1 = over_x(inner)
    weights = (fc1_weight, w1b, fc2_weight, w2b, fc1_bias, b1b)
    acta0, actb0, dprea0, dpreb0, branch0, dinner0, sums0 = mlp(inner, dbranch, *weights, F32)
    acta1, actb1, dprea1, dpreb1, branch1, dinner1, sums1 = mlp(inner1, dbranch1, *weights, BF16)
    dinner_in = over_x(dinner1)
    mixed1 = over_x(mixed)
    normed1 = over_x(normed)
    branch_in = over_x(branch1)

    other = over_core(
        mlp_grad(inner, inner1, dpreb0, dpreb1, actb0, actb1, dbranch, dbranch1)
    )
    fc_grad = mlp_grad(inner, inner1, dprea0, dprea1, acta0, acta1, dbranch, dbranch1, other)

    dhidden, datt_send, datt_keep, dqkv, dqkv_send, dscores, sums_b = backward(
        heads, where, dinner0, dinner_in, hidden, attended, out_grad, mask_col, ln2_gain, gamma1,
        proj_weight, q, k, v, probs,
    )
    datt1 = over_x(datt_send)
    dqkv1 = over_x(dqkv_send)

    patch_grad, sums_n = first_norm(
        patches, mask_col, mask_token, ln1_gain, dqkv, qkv_weight, dhidden
    )
    layer_out, sums_e = layer_end(
        hidden, branch0, branch_in, fc2_bias, gamma2, out_grad, mask_col, dbranch
    )

    late_args = (where, normed, normed1, mixed, mixed1, dqkv, dqkv1, datt_keep, datt1)
    late_other = over_core(late_grad(*late_args))
    late = late_grad(*late_args, late_other)

    block = width // dp
    halves = dp // 2
    over_low = swap("dp", 1)

    def scatter_low(value):
        parts = value.reshape(-1, halves, 2, block, value.shape[-1])
        send = lax.dynamic_index_in_dim(parts, 1 - low_at, 2, False)
        keep = lax.dynamic_index_in_dim(parts, low_at, 2, False)
        return (keep.astype(F32) + over_low(send).astype(F32)).astype(BF16)

    high_at = dp_at // 2

    def scatter_high(value):
        total = lax.dynamic_index_in_dim(value, high_at, 1, False).astype(F32)
        for step in range(1, halves):
            part = lax.dynamic_index_in_dim(value, high_at ^ step, 1, False)
            total = total + swap("dp", 2 * step)(part).astype(F32)
        return total

    fc_own = scatter_high(scatter_low(fc_grad))
    late_own = scatter_high(scatter_low(late))[0].astype(BF16)

    fc1_weight_grad = fc_own[0]
    fc2_weight_grad = fc_own[1].T

    late_x = over_x(late_own)
    pair_core = over_core(jnp.stack([late_own, late_x]))
    on_core = core_at > 0
    on_x = x_at > 0
    mine = jnp.stack([late_own, late_x])
    core0 = jnp.where(on_core, pair_core, mine)
    core1 = jnp.where(on_core, mine, pair_core)
    low0 = jnp.where(on_x, core0[1], core0[0])
    high0 = jnp.where(on_x, core0[0], core0[1])
    low1 = jnp.where(on_x, core1[1], core1[0])
    high1 = jnp.where(on_x, core1[0], core1[1])
    half = width // 2
    qkv_weight_grad = jnp.concatenate(
        [low0, low1[:, :half], high0, high1[:, :half]], axis=1
    ).astype(F32)
    proj_weight_grad = jnp.concatenate([low1[:, half:], high1[:, half:]], axis=1).astype(F32)

    head_pad = 16
    ds = jnp.pad(jnp.transpose(dscores, (1, 0, 2)), ((0, 0), (0, head_pad - heads), (0, 0)))
    table = table_grad(rel_index, ds, entries)

    table_rows = table.reshape(-1, width)
    shared = jnp.concatenate([table_rows, sums_b[:6], sums_n[:3], sums_e[:2]], axis=0)
    shared_rows = shared.shape[0]
    sums = sums0 + sums1
    met = over_core(jnp.concatenate([shared, sums[1:2]], axis=0))
    shared = shared + met[:shared_rows]
    bias_row = sums[0:1] + met[shared_rows:]
    shared = shared + over_x(shared)
    both = jnp.concatenate([shared, bias_row], axis=0)
    bit = 1
    while bit < dp:
        both = both + swap("dp", bit)(both)
        bit *= 2
    n = table_rows.shape[0]
    rel_grad = both[:n].reshape(-1, head_pad, LANES)
    rel_grad = jnp.transpose(rel_grad, (0, 2, 1)).reshape(-1, head_pad)[:entries, :heads]
    (ln2_gain_grad, ln2_bias_grad, gamma1_grad, proj_bias_grad, query_bias_grad, value_bias_grad,
     mask_token_grad, ln1_gain_grad, ln1_bias_grad, fc2_bias_grad, gamma2_grad,
     fc1_bias_grad) = [both[n + at] for at in range(12)]
    return (
        layer_out,
        patch_grad,
        mask_token_grad,
        ln1_gain_grad,
        ln1_bias_grad,
        qkv_weight_grad,
        query_bias_grad,
        value_bias_grad,
        rel_grad,
        proj_weight_grad,
        proj_bias_grad,
        gamma1_grad,
        ln2_gain_grad,
        ln2_bias_grad,
        fc1_weight_grad,
        fc1_bias_grad,
        fc2_weight_grad,
        fc2_bias_grad,
        gamma2_grad,
    )


def solution(mesh):
    rows3 = P(("dp", "mp"), None, None)
    placed = (
        (rows3, P(("dp", "mp"), None), rows3)
        + (P(),) * 13
        + (P(None, "mp"), P("mp"), P("mp", None), P(), P())
    )
    return jax.shard_map(
        functools.partial(on_device, mesh.shape["dp"]),
        mesh=mesh,
        in_specs=placed,
        out_specs=(
            rows3,
            rows3,
            P(),
            P(),
            P(),
            P("dp", None),
            P(),
            P(),
            P(),
            P("dp", None),
            P(),
            P(),
            P(),
            P(),
            P("dp", "mp"),
            P("mp"),
            P("mp", "dp"),
            P(),
            P(),
        ),
        check_vma=False,
    )
```

```python
import functools

import jax
import jax.numpy as jnp
from jax import lax
from jax.experimental import pallas as pl
from jax.experimental.pallas import tpu as pltpu
from jax.sharding import PartitionSpec as P

F32 = jnp.float32
BF16 = jnp.bfloat16
EPS = 1e-06
LANES = 128
COST = dict(pair=0.7, keep=1.5, back=9, norm=4, late=2.6, table=6, mlp=4, end=2, spread=0.7, total=0.5)
UNROLL_F = 6
UNROLL_B = 6
VMEM_LIMIT = 16 * 1024 * 1024


def round_up(value, step):
    return -(-value // step) * step


def dot_nn(left, right):
    return lax.dot_general(left, right, (((1,), (0,)), ((), ())), preferred_element_type=F32)


def dot_nt(left, right):
    return lax.dot_general(left, right, (((1,), (1,)), ((), ())), preferred_element_type=F32)


def dot_tn(left, right):
    return lax.dot_general(left, right, (((0,), (0,)), ((), ())), preferred_element_type=F32)


def row_of(ref):
    return ref[...].reshape(1, ref.shape[0])


def norm_stats(values):
    middle = jnp.mean(values, axis=-1, keepdims=True)
    centred = values - middle
    spread = jnp.mean(centred * centred, axis=-1, keepdims=True)
    root = lax.rsqrt(spread + EPS)
    return centred * root, root


def norm_back(d_out, xhat, root, gain):
    t = d_out * gain
    mean_t = jnp.mean(t, axis=-1, keepdims=True)
    mean_tx = jnp.mean(t * xhat, axis=-1, keepdims=True)
    return root * (t - mean_t - xhat * mean_tx)


SPACES = {
    "h": (pltpu.HBM, pltpu.VMEM),
    "v": (None, pltpu.VMEM),
    "s": (None, pltpu.SMEM),
    "a": (pltpu.HBM, pl.ANY),
}


def call(body, outs, kinds, values, scratch=(), cost=1, deps=(), carry=()):
    specs, given = [], []
    for kind, value in zip(kinds, values, strict=True):
        keep, space = SPACES[kind]
        specs.append(pl.BlockSpec(memory_space=space))
        given.append(value if keep is None else pltpu.with_memory_space_constraint(value, keep))
    outs = outs if isinstance(outs, tuple) else (outs,)
    n_in, n_more, n_out = len(given), len(deps) + len(carry), len(outs)

    def inner(*refs):
        rest = refs[n_in + n_more :]
        body(*refs[:n_in], *rest[:n_out], *rest[n_out + len(carry) :])

    anywhere = pl.BlockSpec(memory_space=pl.ANY)
    out = pl.pallas_call(
        inner,
        name=getattr(body, "func", body).__name__,
        out_shape=outs + tuple(jax.ShapeDtypeStruct(c.shape, c.dtype) for c in carry),
        in_specs=specs + [anywhere] * n_more,
        out_specs=tuple(pl.BlockSpec(memory_space=pltpu.VMEM) for _ in outs)
        + (anywhere,) * len(carry),
        input_output_aliases={n_in + len(deps) + at: n_out + at for at in range(len(carry))},
        scratch_shapes=list(scratch),
        compiler_params=pltpu.CompilerParams(vmem_limit_bytes=VMEM_LIMIT),
        cost_estimate=pl.CostEstimate(
            flops=int(cost * 1e9), bytes_accessed=1000, transcendentals=0
        ),
    )(*given, *deps, *carry)
    return out if len(out) > 1 else out[0]


def shape(dims, kind):
    return pltpu.VMEM(dims, kind)


def shape_out(dims, kind):
    return pltpu.HBM(dims, kind)


def load_padded(source_ref, pad_ref):
    rows = source_ref.shape[1]
    tail = (rows // 8) * 8
    pad_ref[tail:, :] = jnp.zeros_like(pad_ref[tail:, :])
    pad_ref[0:rows, :] = source_ref[0].astype(F32)
    return pad_ref[...]


def mask_column(mask_ref, wide_ref, pad):
    rows = mask_ref.shape[1]
    wide_ref[...] = jnp.zeros_like(wide_ref)
    line = jnp.where(mask_ref[...] > 0, 1.0, 0.0)
    wide_ref[:, 0:rows] = jnp.broadcast_to(line, (LANES, rows))
    return wide_ref[...].T[:pad]


def forward_body(
    heads,
    patches_ref,
    mask_ref,
    index_ref,
    token_ref,
    gain1_ref,
    bias1_ref,
    qbias_ref,
    vbias_ref,
    table_ref,
    pbias_ref,
    gamma1_ref,
    gain2_ref,
    bias2_ref,
    wqkv_hbm,
    wproj_hbm,
    mask_out,
    normed_ref,
    q_ref,
    k_ref,
    v_ref,
    probs_ref,
    mixed_ref,
    attended_ref,
    hidden_ref,
    inner_ref,
    pad_s,
    wide_s,
    index_s,
    table_s,
    bias_s,
    wqkv_ref,
    wproj_ref,
    sems,
):
    rows, width = patches_ref.shape[1:]
    pad = normed_ref.shape[0]
    keys = k_ref.shape[0]
    head_size = width // heads
    copy_qkv = pltpu.make_async_copy(wqkv_hbm, wqkv_ref, sems.at[0])
    copy_qkv.start()
    copy_proj = pltpu.make_async_copy(wproj_hbm, wproj_ref, sems.at[1])
    copy_proj.start()

    index_s[...] = jnp.zeros_like(index_s)
    index_s[0:rows, 0:rows] = index_ref[...]
    entries = table_ref.shape[1]
    chunks = table_s.shape[2] // LANES
    top = jnp.max(jnp.abs(table_ref[...]))
    grow = 32767.0 / jnp.maximum(top, 1e-30)
    shrink = jnp.maximum(top, 1e-30) / 32767.0
    whole = jnp.round(table_ref[...] * grow).astype(jnp.int32)
    table_s[...] = jnp.zeros_like(table_s)
    for pair in range(heads // 2):
        both = whole[2 * pair : 2 * pair + 1] * 65536 + (whole[2 * pair + 1 : 2 * pair + 2] & 65535)
        table_s[pair, :, 0:entries] = jnp.broadcast_to(both, (8, entries))
    key_lane = lax.broadcasted_iota(jnp.int32, (1, LANES), 1)

    def gather_step(tile, carry):
        at_rows = pl.ds(pl.multiple_of(tile * 8, 8), 8)
        for half in range(keys // LANES):
            lanes = slice(half * LANES, (half + 1) * LANES)
            at = index_s[at_rows, lanes]
            low = at & (LANES - 1)
            high = at >> 7
            marks = [high == chunk for chunk in range(chunks)]
            real = key_lane + half * LANES < rows
            for pair in range(heads // 2):
                value = None
                for chunk in range(chunks):
                    line = table_s[pair, :, chunk * LANES : (chunk + 1) * LANES]
                    found = jnp.take_along_axis(line, low, axis=1, mode="promise_in_bounds")
                    value = found if value is None else jnp.where(marks[chunk], found, value)
                one = (value >> 16).astype(F32) * shrink
                two = ((value << 16) >> 16).astype(F32) * shrink
                if (half + 1) * LANES > rows:
                    one = jnp.where(real, one, -1e30)
                    two = jnp.where(real, two, -1e30)
                bias_s[2 * pair, at_rows, lanes] = one
                bias_s[2 * pair + 1, at_rows, lanes] = two
        return carry

    lax.fori_loop(0, pad // 8, gather_step, 0, unroll=2)

    column = mask_column(mask_ref, wide_s, pad)
    mask_out[...] = column
    picked = column[:, 0:1] > 0
    start = jnp.where(picked, row_of(token_ref), load_padded(patches_ref, pad_s))
    pad_s[...] = start
    xhat, _ = norm_stats(start)
    normed = (xhat * row_of(gain1_ref) + row_of(bias1_ref)).astype(BF16)
    normed_ref[...] = normed
    copy_qkv.wait()
    scale = head_size ** (-0.5)
    q_ref[...] = ((dot_nn(normed, wqkv_ref[:, :width]) + row_of(qbias_ref)) * scale).astype(BF16)
    k_ref[0:pad, :] = dot_nn(normed, wqkv_ref[:, width : 2 * width]).astype(BF16)
    k_ref[pad:, :] = jnp.zeros_like(k_ref[pad:, :])
    v_ref[0:pad, :] = (dot_nn(normed, wqkv_ref[:, 2 * width :]) + row_of(vbias_ref)).astype(BF16)
    v_ref[pad:, :] = jnp.zeros_like(v_ref[pad:, :])

    lane = lax.broadcasted_iota(jnp.int32, (1, LANES), 1)
    first = lane < head_size

    def pair_step(pair, carry):
        at = pl.ds(pl.multiple_of(pair * LANES, LANES), LANES)
        query = q_ref[:, at]
        key = k_ref[:, at]
        value = v_ref[:, at]
        outs = []
        for side in range(2):
            head = pair * 2 + side
            own = first if side == 0 else jnp.logical_not(first)
            scores = dot_nt(jnp.where(own, query, jnp.zeros_like(query)), key) + bias_s[head]
            top = jnp.max(scores, axis=-1, keepdims=True)
            grown = jnp.exp(scores - top)
            probs = (grown * (1.0 / jnp.sum(grown, axis=-1, keepdims=True))).astype(BF16)
            probs_ref[head] = probs
            outs.append(dot_nn(probs, value))
        mixed_ref[:, at] = jnp.where(first, outs[0], outs[1]).astype(BF16)
        return carry

    lax.fori_loop(0, heads // 2, pair_step, 0, unroll=UNROLL_F)
    copy_proj.wait()
    attended = dot_nn(mixed_ref[...], wproj_ref[...]) + row_of(pbias_ref)
    attended_ref[...] = attended
    hidden = pad_s[...] + row_of(gamma1_ref) * attended
    hidden_ref[...] = hidden
    xhat2, _ = norm_stats(hidden)
    inner_ref[...] = (xhat2 * row_of(gain2_ref) + row_of(bias2_ref)).astype(BF16)


def forward(heads, pad, patches, row_mask, rel_index, token, gain1, bias1, qbias, vbias, table_t,
            pbias, gamma1, gain2, bias2, wqkv, wproj):
    rows, width = patches.shape[1:]
    keys = round_up(pad, LANES)
    entries = round_up(table_t.shape[1], LANES)
    outs = (
        shape_out((pad, LANES), F32),
        shape_out((pad, width), BF16),
        shape_out((pad, width), BF16),
        shape_out((keys, width), BF16),
        shape_out((keys, width), BF16),
        shape_out((heads, pad, keys), BF16),
        shape_out((pad, width), BF16),
        shape_out((pad, width), F32),
        shape_out((pad, width), F32),
        shape((pad, width), BF16),
    )
    return call(
        functools.partial(forward_body, heads),
        outs,
        "hhhhhhhhhhhhhaa",
        (patches, row_mask, rel_index, token, gain1, bias1, qbias, vbias, table_t, pbias, gamma1,
         gain2, bias2, wqkv, wproj),
        (
            pltpu.VMEM((pad, width), F32),
            pltpu.VMEM((LANES, keys), F32),
            pltpu.VMEM((pad, keys), jnp.int32),
            pltpu.VMEM((heads // 2, 8, entries), jnp.int32),
            pltpu.VMEM((heads, pad, keys), F32),
            pltpu.VMEM(wqkv.shape, BF16),
            pltpu.VMEM(wproj.shape, BF16),
            pltpu.SemaphoreType.DMA((2,)),
        ),
        cost=12,
    )


def mlp_body(
    first, inner_ref, b1a_ref, b1b_ref, w1a_ref, w1b_ref, w2a_ref, w2b_ref, bias_ref, *rest
):
    if first:
        grads, masks, gamma2_ref = rest[0:2], rest[2:4], rest[4]
        rest = rest[5:]
        dbranches, rest = rest[0:2], rest[2:]
        cot_out, rest = rest[0], rest[1:]
        pad_s, wide_s = rest[-2:]
        rest = rest[:-2]
        pad = inner_ref.shape[0]
        for grad_ref, mask_ref, out_ref in zip(grads, masks, dbranches):
            column = mask_column(mask_ref, wide_s, pad)[:, 0:1]
            cotangent = load_padded(grad_ref, pad_s) * column
            out_ref[...] = (row_of(gamma2_ref) * cotangent).astype(BF16)
            if out_ref is dbranches[0]:
                own_cotangent = cotangent
            else:
                cot_out[...] = cotangent
        dbranch = dbranches[0][...]
        cotangent = own_cotangent
    else:
        dbranch, cotangent = rest[0][...], rest[1][...]
        rest = rest[2:]
    acta_ref, actb_ref, dprea_ref, dpreb_ref, branch_ref, dinner_ref, sums_ref = rest
    inner = inner_ref[...]
    branch = None
    dinner = None
    for at, (w1, w2, b1, act_out, dpre_out) in enumerate((
        (w1a_ref, w2a_ref, b1a_ref, acta_ref, dprea_ref),
        (w1b_ref, w2b_ref, b1b_ref, actb_ref, dpreb_ref),
    )):
        pre = dot_nn(inner, w1[...]) + row_of(b1).astype(F32)
        phi = 0.5 + 0.5 * lax.erf(pre * (0.5**0.5))
        act = (pre * phi).astype(BF16)
        act_out[...] = act
        slope = phi + pre * (jnp.exp(-0.5 * pre * pre) * 0.3989422804014327)
        dact = dot_nt(dbranch, w2[...])
        dpre = (dact * slope).astype(BF16)
        dpre_out[...] = dpre
        sums_ref[at : at + 1, :] = jnp.sum(dpre.astype(F32), axis=0, keepdims=True)
        this_branch = dot_nn(act, w2[...])
        this_dinner = dot_nt(dpre, w1[...])
        branch = this_branch if branch is None else branch + this_branch
        dinner = this_dinner if dinner is None else dinner + this_dinner
    if first:
        branch = branch + row_of(bias_ref)
        sums_ref[3:4, :] = jnp.sum(dbranch.astype(F32), axis=0, keepdims=True)
    else:
        sums_ref[3:4, :] = jnp.zeros_like(sums_ref[3:4, :])
    branch_ref[...] = branch.astype(branch_ref.dtype)
    dinner_ref[...] = dinner.astype(dinner_ref.dtype)
    sums_ref[2:3, :] = jnp.sum(cotangent * branch, axis=0, keepdims=True)
    sums_ref[4:8, :] = jnp.zeros_like(sums_ref[4:8, :])


def mlp(inner, weights, bias, given, first, deps=()):
    pad, width = inner.shape
    ff = weights[2].shape[1]
    kind = F32 if first else BF16
    outs = (
        (shape((pad, ff), BF16),) * 4
        + (shape_out((pad, width), kind), shape((pad, width), kind))
        + (shape((8, ff), F32),)
    )
    scratch = ()
    if first:
        outs = (shape((pad, width), BF16),) * 2 + (shape((pad, width), F32),) + outs
        scratch = (pltpu.VMEM((pad, width), F32), pltpu.VMEM((LANES, round_up(pad, LANES)), F32))
    return call(
        functools.partial(mlp_body, first), outs, "vhhvvvvh" + ("hvhvh" if first else "vv"),
        (inner, *weights, bias, *given), scratch, cost=COST["mlp"], deps=deps,
    )


def split_rows(out_send, out_keep, at, total, low, block):
    for step in range(total.shape[0] // (2 * block)):
        even = total[2 * step * block : (2 * step + 1) * block]
        odd = total[(2 * step + 1) * block : (2 * step + 2) * block]
        out_send[at, step] = jnp.where(low, even, odd).astype(BF16)
        out_keep[at, step] = jnp.where(low, odd, even).astype(BF16)


def pair_grad_body(left0, left1, right0, right1, out_ref):
    total = dot_tn(left0[...], right0[...]) + dot_tn(left1[...], right1[...])
    out_ref[...] = total.astype(BF16)


def pair_grad(left0, left1, right0, right1, deps=(), carry=()):
    return call(
        pair_grad_body, shape((left0.shape[1], right0.shape[1]), BF16), "vvvv",
        (left0, left1, right0, right1), cost=COST["pair"], deps=deps, carry=carry,
    )


def fc_keep_body(block, where_ref, *refs):
    send_ref, keep_ref = refs[10:]
    low = where_ref[2] > 0
    for at in range(2):
        left0, left1, right0, right1, other = refs[5 * at : 5 * at + 5]
        total = dot_tn(left0[...], right0[...]) + dot_tn(left1[...], right1[...])
        split_rows(send_ref, keep_ref, at, total + other[...].astype(F32), low, block)


def fc_keep(where, block, one, two, deps=(), carry=()):
    width, ff = one[0].shape[1], one[2].shape[1]
    outs = (shape((2, width // (2 * block), block, ff), BF16),) * 2
    return call(
        functools.partial(fc_keep_body, block), outs, "s" + "v" * 10, (where, *one, *two),
        cost=COST["keep"], deps=deps, carry=carry,
    )


def backward_body(
    heads,
    rows,
    where_ref,
    dinner0_ref,
    dinner1_ref,
    hidden_ref,
    attended_ref,
    outgrad_ref,
    mask_ref,
    gain2_ref,
    gamma1_ref,
    wproj_ref,
    q_ref,
    k_ref,
    v_ref,
    probs_ref,
    dhidden_ref,
    dattkeep_ref,
    dqkv_ref,
    send_ref,
    dscores_ref,
    sums_ref,
    pad_s,
    dmixed_s,
):
    pad, width = hidden_ref.shape
    head_size = width // heads
    cotangent = load_padded(outgrad_ref, pad_s) * mask_ref[:, 0:1]
    xhat, root = norm_stats(hidden_ref[...])
    dinner = dinner0_ref[...].astype(F32) + dinner1_ref[...].astype(F32)
    dhidden = cotangent + norm_back(dinner, xhat, root, row_of(gain2_ref))
    dhidden_ref[...] = dhidden
    datt = (row_of(gamma1_ref) * dhidden).astype(BF16)
    high = where_ref[0] > 0
    half = width // 2
    three = 3 * half
    send_ref[:, three:] = jnp.where(high, datt[:, :half], datt[:, half:])
    dattkeep_ref[...] = jnp.where(high, datt[:, half:], datt[:, :half])
    dmixed_s[...] = dot_nt(datt, wproj_ref[...]).astype(BF16)
    sums_ref[0:1, :] = jnp.sum(dinner * xhat, axis=0, keepdims=True)
    sums_ref[1:2, :] = jnp.sum(dinner, axis=0, keepdims=True)
    sums_ref[2:3, :] = jnp.sum(dhidden * attended_ref[...], axis=0, keepdims=True)
    sums_ref[3:4, :] = jnp.sum(datt.astype(F32), axis=0, keepdims=True)

    lane = lax.broadcasted_iota(jnp.int32, (1, LANES), 1)
    first = lane < head_size
    scale = head_size ** (-0.5)

    def pair_step(pair, carry):
        start = pl.multiple_of(pair * LANES, LANES)
        at = pl.ds(start, LANES)
        query = q_ref[:, at]
        key = k_ref[:, at]
        value = v_ref[:, at]
        dmixed = dmixed_s[:, at]
        dq, dk, dv = [], [], []
        for side in range(2):
            head = pair * 2 + side
            own = first if side == 0 else jnp.logical_not(first)
            probs_b = probs_ref[head]
            probs = probs_b.astype(F32)
            dprobs = dot_nt(jnp.where(own, dmixed, jnp.zeros_like(dmixed)), value)
            inside = jnp.sum(probs * dprobs, axis=-1, keepdims=True)
            dscores = (probs * (dprobs - inside)).astype(BF16)
            dscores_ref[head] = dscores
            dq.append(dot_nn(dscores, key))
            dk.append(dot_tn(dscores, query))
            dv.append(dot_tn(probs_b, dmixed))
        dqkv_ref[:, at] = (jnp.where(first, dq[0], dq[1]) * scale).astype(BF16)
        dqkv_ref[:, pl.ds(pl.multiple_of(start + width, LANES), LANES)] = (
            jnp.where(first, dk[0], dk[1])[:pad].astype(BF16)
        )
        dqkv_ref[:, pl.ds(pl.multiple_of(start + 2 * width, LANES), LANES)] = (
            jnp.where(first, dv[0], dv[1])[:pad].astype(BF16)
        )
        return carry

    lax.fori_loop(0, heads // 2, pair_step, 0, unroll=UNROLL_B)
    send_ref[:, :three] = jnp.where(high, dqkv_ref[:, :three], dqkv_ref[:, three:])
    sums_ref[4:5, :] = jnp.sum(dqkv_ref[:, :width].astype(F32), axis=0, keepdims=True)
    sums_ref[5:6, :] = jnp.sum(dqkv_ref[:, 2 * width :].astype(F32), axis=0, keepdims=True)
    sums_ref[6:8, :] = jnp.zeros((2, width), F32)


def backward(heads, where, dinner0, dinner1, hidden, attended, out_grad, mask_col, gain2, gamma1,
             wproj, q, k, v, probs, deps=()):
    pad, width = hidden.shape
    keys = k.shape[0]
    outs = (
        shape((pad, width), F32),
        shape_out((pad, width // 2), BF16),
        shape_out((pad, 3 * width), BF16),
        shape((pad, 2 * width), BF16),
        shape((heads, pad, keys), BF16),
        shape((8, width), F32),
    )
    return call(
        functools.partial(backward_body, heads, out_grad.shape[1]),
        outs,
        "svvhhhhhhhhhhh",
        (where, dinner0, dinner1, hidden, attended, out_grad, mask_col, gain2, gamma1, wproj, q, k,
         v, probs),
        (pltpu.VMEM((pad, width), F32), pltpu.VMEM((pad, width), BF16)),
        cost=COST["back"],
        deps=deps,
    )


def first_norm_body(
    patches_ref, mask_ref, token_ref, gain1_ref, dqkv_ref, wqkv_ref, dhidden_ref,
    patchgrad_ref, sums_ref, pad_s,
):
    rows, width = patches_ref.shape[1:]
    picked = mask_ref[:, 0:1] > 0
    start = jnp.where(picked, row_of(token_ref), load_padded(patches_ref, pad_s))
    xhat, root = norm_stats(start)
    dnormed = dot_nt(dqkv_ref[...], wqkv_ref[...])
    dstart = dhidden_ref[...] + norm_back(dnormed, xhat, root, row_of(gain1_ref))
    patchgrad_ref[0] = jnp.where(picked, 0.0, dstart)[0:rows]
    sums_ref[0:1, :] = jnp.sum(jnp.where(picked, dstart, 0.0), axis=0, keepdims=True)
    sums_ref[1:2, :] = jnp.sum(dnormed * xhat, axis=0, keepdims=True)
    sums_ref[2:3, :] = jnp.sum(dnormed, axis=0, keepdims=True)
    sums_ref[3:8, :] = jnp.zeros((5, width), F32)


def first_norm(patches, mask_col, token, gain1, dqkv, wqkv, dhidden, deps=()):
    rows, width = patches.shape[1:]
    pad = mask_col.shape[0]
    outs = (shape_out((1, rows, width), F32), shape((8, width), F32))
    return call(
        first_norm_body, outs, "hhhhhhv",
        (patches, mask_col, token, gain1, dqkv, wqkv, dhidden),
        (pltpu.VMEM((pad, width), F32),), cost=COST["norm"], deps=deps,
    )


def layer_end_body(hidden_ref, branch0_ref, branch1_ref, gamma2_ref, out_ref):
    branch = branch0_ref[...] + branch1_ref[...].astype(F32)
    layer = hidden_ref[...] + row_of(gamma2_ref) * branch
    out_ref[0] = layer[0 : out_ref.shape[1]].astype(BF16)


def layer_end(rows, hidden, branch0, branch1, gamma2):
    return call(
        layer_end_body, shape_out((1, rows, hidden.shape[1]), BF16), "hhvh",
        (hidden, branch0, branch1, gamma2), cost=COST["end"],
    )


def table_grad_body(
    where_ref, index_ref, ds_ref, sums_b_ref, sums_n_ref, sums0_ref, sums1_ref, out_ref, index_s,
    total_s,
):
    rows = index_ref.shape[0]
    pad, head_pad, keys = ds_ref.shape
    high_count = total_s.shape[0] // head_pad
    index_s[...] = jnp.zeros_like(index_s)
    index_s[0:rows, 0:rows] = index_ref[...]
    total_s[...] = jnp.zeros_like(total_s)
    below = lax.broadcasted_iota(jnp.int32, (LANES, keys), 0).astype(BF16)
    ones = jnp.ones((LANES, keys), BF16)
    group = 16

    def step(at, carry):
        base = pl.multiple_of(at * group, group)
        lines = index_s[pl.ds(base, group), :]
        low = (lines & (LANES - 1)).astype(F32).astype(BF16)
        high = (lines >> 7).astype(F32).astype(BF16)
        total = None
        for i in range(group):
            onehot = jnp.where(below == low[i : i + 1], ones, jnp.zeros_like(ones))
            ds = ds_ref[base + i]
            left = jnp.concatenate(
                [
                    jnp.where(high[i : i + 1] == jnp.asarray(part, BF16), ds, jnp.zeros_like(ds))
                    for part in range(high_count)
                ],
                axis=0,
            )
            one = dot_nt(left, onehot)
            total = one if total is None else total + one
        total_s[...] += total
        return carry

    lax.fori_loop(0, pad // group, step, 0, unroll=2)
    for part in range(high_count):
        out_ref[0:head_pad, part * LANES : (part + 1) * LANES] = total_s[
            part * head_pad : (part + 1) * head_pad
        ]
    sums = sums0_ref[...] + sums1_ref[...]
    out_ref[head_pad : head_pad + 6, :] = sums_b_ref[0:6, :]
    out_ref[head_pad + 6 : head_pad + 8, :] = sums[2:4]
    out_ref[head_pad + 8 : head_pad + 11, :] = sums_n_ref[0:3, :]
    for part in range(4):
        mine = jnp.where(where_ref[0] == part // 2, 1.0, 0.0)
        own = jnp.where(where_ref[1] == part % 2, sums[0:1], sums[1:2])
        out_ref[head_pad + 11 + part : head_pad + 12 + part, :] = mine * own
    out_ref[head_pad + 15 :, :] = jnp.zeros_like(out_ref[head_pad + 15 :, :])


def table_grad(where, rel_index, dscores, sums_b, sums_n, sums0, sums1, entries, deps=()):
    pad, head_pad, keys = dscores.shape
    high_count = round_up(entries, LANES) // LANES
    width = sums_b.shape[1]
    return call(
        table_grad_body, shape((head_pad + 16, width), F32), "shvvvvv",
        (where, rel_index, dscores, sums_b, sums_n, sums0, sums1),
        (pltpu.VMEM((pad, keys), jnp.int32), pltpu.VMEM((high_count * head_pad, LANES), F32)),
        cost=COST["table"], deps=deps,
    )


def gather_sum_body(count, *refs):
    for at, out_ref in enumerate(refs[count:]):
        total = refs[0][at].astype(F32)
        for ref in refs[1:count]:
            total = total + ref[at].astype(F32)
        out_ref[...] = total.astype(out_ref.dtype)


def gather_sum(parts, kind, deps=(), carry=()):
    count, block, width = parts[0].shape
    make = shape_out if kind == F32 else shape
    return call(
        functools.partial(gather_sum_body, len(parts)), (make((block, width), kind),) * count,
        "v" * len(parts), parts, cost=COST["total"], deps=deps, carry=carry,
    )


def late_grad_body(
    block, where_ref, normed0, normed1, mixed0, mixed1, dqkv_ref, met_ref, datt_ref, *rest
):
    width = normed0.shape[1]
    half, three = width // 2, 3 * width // 2
    high = where_ref[0] > 0
    core = where_ref[1] > 0
    low = where_ref[2] > 0
    second = jnp.logical_not(core) if block is None else core
    own = jnp.where(high, dqkv_ref[:, three:], dqkv_ref[:, :three])
    total0, total1 = None, None
    for normed_ref, mixed_ref, part, datt in (
        (normed0, mixed0, own, datt_ref[...]),
        (normed1, mixed1, met_ref[:, :three], met_ref[:, three:]),
    ):
        normed = normed_ref[...]
        right0 = jnp.where(second, part[:, width:], part[:, :half])
        left1 = jnp.where(second, mixed_ref[...], normed)
        right1 = jnp.where(second, datt, part[:, half:width])
        this0 = dot_tn(normed, right0)
        this1 = dot_tn(left1, right1)
        total0 = this0 if total0 is None else total0 + this0
        total1 = this1 if total1 is None else total1 + this1
    total = jnp.concatenate([total0, total1], axis=1)
    if block is None:
        rest[0][...] = total.astype(BF16)
    else:
        total = total + rest[0][...].astype(F32)
        split_rows(rest[1], rest[2], 0, total, low, block)


def late_grad(where, block, normed0, normed1, mixed0, mixed1, dqkv, met, datt, other=None,
              deps=(), carry=()):
    width = normed0.shape[1]
    values = (where, normed0, normed1, mixed0, mixed1, dqkv, met, datt)
    if other is None:
        block = None
        outs = shape((width, width), BF16)
    else:
        values += (other,)
        outs = (shape((1, width // (2 * block), block, width), BF16),) * 2
    return call(
        functools.partial(late_grad_body, block), outs, "shvhvhvhv"[: len(values)], values,
        cost=COST["late"], deps=deps, carry=carry,
    )


def spread_body(where_ref, keep_ref, met_ref, *outs):
    high = where_ref[3]
    for step, out in enumerate(outs):
        at = high ^ step
        for item in range(keep_ref.shape[0]):
            out[item] = (keep_ref[item, at].astype(F32) + met_ref[item, at].astype(F32)).astype(BF16)


def spread(where, keep, met, deps=(), carry=()):
    count, halves, block, width = keep.shape
    return call(
        spread_body, (shape((count, block, width), BF16),) * halves, "svv", (where, keep, met),
        cost=COST["spread"], deps=deps, carry=carry,
    )


def on_device(
    dp,
    patches,
    row_mask,
    out_grad,
    rel_index,
    mask_token,
    ln1_gain,
    ln1_bias,
    qkv_weight,
    query_bias,
    value_bias,
    rel_table,
    proj_weight,
    proj_bias,
    gamma1,
    ln2_gain,
    ln2_bias,
    fc1_weight,
    fc1_bias,
    fc2_weight,
    fc2_bias,
    gamma2,
):
    rows, width = patches.shape[1:]
    entries, heads = rel_table.shape
    pad = round_up(rows, 16)
    mp_at = lax.axis_index("mp")
    dp_at = lax.axis_index("dp")
    x_at, core_at = mp_at // 2, mp_at % 2
    where = jnp.stack([x_at, core_at, dp_at % 2, dp_at // 2]).astype(jnp.int32)

    def swap(axis, bit):
        count = 4 if axis == "mp" else dp
        pairs = [(at, at ^ bit) for at in range(count)]
        return lambda value: lax.ppermute(value, axis, pairs)

    over_core, over_x, over_low = swap("mp", 1), swap("mp", 2), swap("dp", 1)

    out_grad1, row_mask1 = over_x(out_grad), over_x(row_mask)
    b1b, w1b, w2b = over_core(fc1_bias), over_core(fc1_weight), over_core(fc2_weight)

    mask_col, normed, q, k, v, probs, mixed, attended, hidden, inner = forward(
        heads, pad, patches, row_mask, rel_index, mask_token, ln1_gain, ln1_bias, query_bias,
        value_bias, rel_table.T, proj_bias, gamma1, ln2_gain, ln2_bias, qkv_weight, proj_weight,
    )
    inner1 = over_x(inner)
    weights = (fc1_bias, b1b, fc1_weight, w1b, fc2_weight, w2b)
    dbranch, dbranch1, cot1, acta0, actb0, dprea0, dpreb0, branch0, dinner0, sums0 = mlp(
        inner, weights, fc2_bias, (out_grad, out_grad1, row_mask, row_mask1, gamma2), True
    )
    acta1, actb1, dprea1, dpreb1, branch1, dinner1, sums1 = mlp(
        inner1, weights, fc2_bias, (dbranch1, cot1), False
    )
    dinner_in = over_x(dinner1)

    block = width // dp
    halves = dp // 2
    fence = over_core(sums1)
    fc1_out = pair_grad(inner, inner1, dpreb0, dpreb1, deps=(fence,))
    fc2_out = pair_grad(dbranch, dbranch1, actb0, actb1, deps=(fc1_out,))
    fc1_other, fc2_other = over_core(fc1_out), over_core(fc2_out)
    fc_send, fc_kept, mixed, normed = fc_keep(
        where, block, (inner, inner1, dprea0, dprea1, fc1_other),
        (dbranch, dbranch1, acta0, acta1, fc2_other), carry=(mixed, normed),
    )
    fc_met = over_low(fc_send)
    mixed1 = over_x(mixed)
    normed1 = over_x(normed)

    dhidden, datt, dqkv, send, dscores, sums_b = backward(
        heads, where, dinner0, dinner_in, hidden, attended, out_grad, mask_col, ln2_gain, gamma1,
        proj_weight, q, k, v, probs, deps=(fc_kept,),
    )
    met = over_x(send)

    def cross_high(parts):
        own, *sends = parts
        return (own, *[swap("dp", 2 * (at + 1))(part) for at, part in enumerate(sends)])

    patch_grad, sums_n = first_norm(
        patches, mask_col, mask_token, ln1_gain, dqkv, qkv_weight, dhidden,
        deps=(normed1, mixed1),
    )
    fc_parts = spread(where, fc_kept, fc_met, deps=(sums_n,))
    fc_seen = cross_high(fc_parts)

    late_args = (where, block, normed, normed1, mixed, mixed1, dqkv, met, datt)
    late_out, branch1_late = late_grad(*late_args, deps=(fc_parts[0],), carry=(branch1,))
    late_other = over_core(late_out)
    branch_in = over_x(branch1_late)
    late_send, late_kept = late_grad(*late_args, late_other)
    late_met = over_low(late_send)

    head_pad = 16
    ds = jnp.pad(jnp.transpose(dscores, (1, 0, 2)), ((0, 0), (0, head_pad - heads), (0, 0)))
    small = table_grad(
        where, rel_index, ds, sums_b, sums_n, sums0, sums1, entries, deps=(late_kept,)
    )
    small = small + over_core(small)
    small = small + over_x(small)
    fc1_weight_grad, fc2_weight_grad = gather_sum(fc_seen, F32, deps=(small,))

    *late_parts, small = spread(
        where, late_kept, late_met, deps=(fc1_weight_grad,), carry=(small,)
    )
    late_seen = cross_high(late_parts)
    small = small + over_low(small)
    late_own, small = gather_sum(late_seen, BF16, carry=(small,))

    bit = 2
    while bit < dp:
        small = small + swap("dp", bit)(small)
        bit *= 2

    layer_out = layer_end(rows, hidden, branch0, branch_in, gamma2)

    late_x = over_x(late_own)
    mine = jnp.stack([late_own, late_x])
    pair_core = over_core(mine)
    on_core = core_at > 0
    on_x = x_at > 0
    core0 = jnp.where(on_core, pair_core, mine)
    core1 = jnp.where(on_core, mine, pair_core)
    low0 = jnp.where(on_x, core0[1], core0[0])
    high0 = jnp.where(on_x, core0[0], core0[1])
    low1 = jnp.where(on_x, core1[1], core1[0])
    high1 = jnp.where(on_x, core1[0], core1[1])
    half = width // 2
    qkv_weight_grad = jnp.concatenate(
        [low0, low1[:, :half], high0, high1[:, :half]], axis=1
    ).astype(F32)
    proj_weight_grad = jnp.concatenate([low1[:, half:], high1[:, half:]], axis=1).astype(F32)

    rel_grad = small[:heads, :entries].T
    (ln2_gain_grad, ln2_bias_grad, gamma1_grad, proj_bias_grad, query_bias_grad, value_bias_grad,
     gamma2_grad, fc2_bias_grad, mask_token_grad, ln1_gain_grad, ln1_bias_grad) = [
        small[head_pad + at] for at in range(11)
    ]
    fc1_bias_grad = lax.dynamic_index_in_dim(small, head_pad + 11 + mp_at, 0, False)
    return (
        layer_out,
        patch_grad,
        mask_token_grad,
        ln1_gain_grad,
        ln1_bias_grad,
        qkv_weight_grad,
        query_bias_grad,
        value_bias_grad,
        rel_grad,
        proj_weight_grad,
        proj_bias_grad,
        gamma1_grad,
        ln2_gain_grad,
        ln2_bias_grad,
        fc1_weight_grad,
        fc1_bias_grad,
        fc2_weight_grad.T,
        fc2_bias_grad,
        gamma2_grad,
    )


def solution(mesh):
    rows3 = P(("dp", "mp"), None, None)
    placed = (
        (rows3, P(("dp", "mp"), None), rows3)
        + (P(),) * 13
        + (P(None, "mp"), P("mp"), P("mp", None), P(), P())
    )
    return jax.shard_map(
        functools.partial(on_device, mesh.shape["dp"]),
        mesh=mesh,
        in_specs=placed,
        out_specs=(
            rows3,
            rows3,
            P(),
            P(),
            P(),
            P("dp", None),
            P(),
            P(),
            P(),
            P("dp", None),
            P(),
            P(),
            P(),
            P(),
            P("dp", "mp"),
            P("mp"),
            P("mp", "dp"),
            P(),
            P(),
        ),
        check_vma=False,
    )
```

```python
import functools

import jax
import jax.numpy as jnp
from jax import lax
from jax.experimental import pallas as pl
from jax.experimental.pallas import tpu as pltpu
from jax.sharding import PartitionSpec as P

F32 = jnp.float32
BF16 = jnp.bfloat16
EPS = 1e-06
LANES = 128
SCALE = 1
UNROLL_F = 6
UNROLL_B = 6
VMEM_LIMIT = 16 * 1024 * 1024


def round_up(value, step):
    return -(-value // step) * step


def dot_nn(left, right):
    return lax.dot_general(left, right, (((1,), (0,)), ((), ())), preferred_element_type=F32)


def dot_nt(left, right):
    return lax.dot_general(left, right, (((1,), (1,)), ((), ())), preferred_element_type=F32)


def dot_tn(left, right):
    return lax.dot_general(left, right, (((0,), (0,)), ((), ())), preferred_element_type=F32)


def row_of(ref):
    return ref[...].reshape(1, ref.shape[0])


def norm_stats(values):
    middle = jnp.mean(values, axis=-1, keepdims=True)
    centred = values - middle
    spread = jnp.mean(centred * centred, axis=-1, keepdims=True)
    root = lax.rsqrt(spread + EPS)
    return centred * root, root


def norm_back(d_out, xhat, root, gain):
    t = d_out * gain
    mean_t = jnp.mean(t, axis=-1, keepdims=True)
    mean_tx = jnp.mean(t * xhat, axis=-1, keepdims=True)
    return root * (t - mean_t - xhat * mean_tx)


SPACES = {
    "h": (pltpu.HBM, pltpu.VMEM),
    "v": (None, pltpu.VMEM),
    "s": (None, pltpu.SMEM),
    "a": (pltpu.HBM, pl.ANY),
}


def call(body, outs, kinds, values, scratch=(), cost=1, deps=(), carry=()):
    specs, given = [], []
    for kind, value in zip(kinds, values, strict=True):
        keep, space = SPACES[kind]
        specs.append(pl.BlockSpec(memory_space=space))
        given.append(value if keep is None else pltpu.with_memory_space_constraint(value, keep))
    outs = outs if isinstance(outs, tuple) else (outs,)
    n_in, n_more, n_out = len(given), len(deps) + len(carry), len(outs)

    def inner(*refs):
        rest = refs[n_in + n_more :]
        rest[n_out][...] = jnp.zeros_like(rest[n_out])
        body(*refs[:n_in], *rest[:n_out], *rest[n_out + 1 + len(carry) :])

    anywhere = pl.BlockSpec(memory_space=pl.ANY)
    whole = pl.BlockSpec(memory_space=pltpu.VMEM)
    in_hbm = [value.dtype == BF16 and len(value.shape) == 2 for value in carry]
    out = pl.pallas_call(
        inner,
        name=getattr(body, "func", body).__name__,
        out_shape=outs
        + (pltpu.VMEM((8, LANES), F32),)
        + tuple(
            (pltpu.HBM if pinned else jax.ShapeDtypeStruct)(c.shape, c.dtype)
            for pinned, c in zip(in_hbm, carry)
        ),
        in_specs=specs + [anywhere] * n_more,
        out_specs=(whole,) * (n_out + 1) + (anywhere,) * len(carry),
        input_output_aliases={n_in + len(deps) + at: n_out + 1 + at for at in range(len(carry))},
        scratch_shapes=list(scratch),
        compiler_params=pltpu.CompilerParams(vmem_limit_bytes=VMEM_LIMIT),
        cost_estimate=pl.CostEstimate(
            flops=int(cost * SCALE * 10**9), bytes_accessed=1000, transcendentals=0
        ),
    )(
        *given,
        *deps,
        *(
            pltpu.with_memory_space_constraint(c, pltpu.HBM) if pinned else c
            for pinned, c in zip(in_hbm, carry)
        ),
    )
    results = out[:n_out] + out[n_out + 1 :]
    return (results if len(results) > 1 else results[0]), out[n_out]


def shape(dims, kind):
    return pltpu.VMEM(dims, kind)


def shape_out(dims, kind):
    return pltpu.HBM(dims, kind)


def load_padded(source_ref, pad_ref):
    rows = source_ref.shape[1]
    tail = (rows // 8) * 8
    pad_ref[tail:, :] = jnp.zeros_like(pad_ref[tail:, :])
    pad_ref[0:rows, :] = source_ref[0].astype(F32)
    return pad_ref[...]


def mask_column(mask_ref, wide_ref, pad):
    rows = mask_ref.shape[1]
    wide_ref[...] = jnp.zeros_like(wide_ref)
    line = jnp.where(mask_ref[...] > 0, 1.0, 0.0)
    wide_ref[:, 0:rows] = jnp.broadcast_to(line, (LANES, rows))
    return wide_ref[...].T[:pad]


def place_is(where_ref, step, place):
    high = where_ref[0] == (place >> 1) ^ (step >> 1)
    low = where_ref[1] == (place & 1) ^ (step & 1)
    return jnp.logical_and(high, low)


def forward_body(
    heads,
    where_ref,
    patches_ref,
    mask_ref,
    index_ref,
    token_ref,
    gain1_ref,
    bias1_ref,
    qbias_ref,
    vbias_ref,
    table_ref,
    pbias_ref,
    gamma1_ref,
    gain2_ref,
    bias2_ref,
    wqkv_hbm,
    wproj_hbm,
    mask_out,
    left0_ref,
    left1_ref,
    left2_ref,
    left3_ref,
    q_ref,
    k_ref,
    v_ref,
    probs_ref,
    attended_ref,
    hidden_ref,
    inner_ref,
    pad_s,
    wide_s,
    index_s,
    table_s,
    bias_s,
    wqkv_ref,
    wproj_ref,
    lefts_ref,
    sems,
):
    rows, width = patches_ref.shape[1:]
    pad = q_ref.shape[0]
    keys = k_ref.shape[0]
    head_size = width // heads
    copy_qkv = pltpu.make_async_copy(wqkv_hbm, wqkv_ref, sems.at[0])
    copy_qkv.start()
    copy_proj = pltpu.make_async_copy(wproj_hbm, wproj_ref, sems.at[1])
    copy_proj.start()

    index_s[...] = jnp.zeros_like(index_s)
    index_s[0:rows, 0:rows] = index_ref[...]
    entries = table_ref.shape[1]
    chunks = table_s.shape[2] // LANES
    top = jnp.max(jnp.abs(table_ref[...]))
    grow = 32767.0 / jnp.maximum(top, 1e-30)
    shrink = jnp.maximum(top, 1e-30) / 32767.0
    whole = jnp.round(table_ref[...] * grow).astype(jnp.int32)
    table_s[...] = jnp.zeros_like(table_s)
    for pair in range(heads // 2):
        both = whole[2 * pair : 2 * pair + 1] * 65536 + (whole[2 * pair + 1 : 2 * pair + 2] & 65535)
        table_s[pair, :, 0:entries] = jnp.broadcast_to(both, (8, entries))
    key_lane = lax.broadcasted_iota(jnp.int32, (1, LANES), 1)

    def gather_step(tile, carry):
        at_rows = pl.ds(pl.multiple_of(tile * 8, 8), 8)
        for half in range(keys // LANES):
            lanes = slice(half * LANES, (half + 1) * LANES)
            at = index_s[at_rows, lanes]
            low = at & (LANES - 1)
            high = at >> 7
            marks = [high == chunk for chunk in range(chunks)]
            real = key_lane + half * LANES < rows
            for pair in range(heads // 2):
                value = None
                for chunk in range(chunks):
                    line = table_s[pair, :, chunk * LANES : (chunk + 1) * LANES]
                    found = jnp.take_along_axis(line, low, axis=1, mode="promise_in_bounds")
                    value = found if value is None else jnp.where(marks[chunk], found, value)
                one = (value >> 16).astype(F32) * shrink
                two = ((value << 16) >> 16).astype(F32) * shrink
                if (half + 1) * LANES > rows:
                    one = jnp.where(real, one, -1e30)
                    two = jnp.where(real, two, -1e30)
                bias_s[2 * pair, at_rows, lanes] = one
                bias_s[2 * pair + 1, at_rows, lanes] = two
        return carry

    lax.fori_loop(0, pad // 8, gather_step, 0, unroll=2)

    column = mask_column(mask_ref, wide_s, pad)
    mask_out[...] = column
    picked = column[:, 0:1] > 0
    start = jnp.where(picked, row_of(token_ref), load_padded(patches_ref, pad_s))
    pad_s[...] = start
    xhat, _ = norm_stats(start)
    normed = (xhat * row_of(gain1_ref) + row_of(bias1_ref)).astype(BF16)
    lefts_ref[0] = normed
    copy_qkv.wait()
    scale = head_size ** (-0.5)
    q_ref[...] = ((dot_nn(normed, wqkv_ref[:, :width]) + row_of(qbias_ref)) * scale).astype(BF16)
    k_ref[0:pad, :] = dot_nn(normed, wqkv_ref[:, width : 2 * width]).astype(BF16)
    k_ref[pad:, :] = jnp.zeros_like(k_ref[pad:, :])
    v_ref[0:pad, :] = (dot_nn(normed, wqkv_ref[:, 2 * width :]) + row_of(vbias_ref)).astype(BF16)
    v_ref[pad:, :] = jnp.zeros_like(v_ref[pad:, :])

    lane = lax.broadcasted_iota(jnp.int32, (1, LANES), 1)
    first = lane < head_size

    def pair_step(pair, carry):
        at = pl.ds(pl.multiple_of(pair * LANES, LANES), LANES)
        query = q_ref[:, at]
        key = k_ref[:, at]
        value = v_ref[:, at]
        outs = []
        for side in range(2):
            head = pair * 2 + side
            own = first if side == 0 else jnp.logical_not(first)
            scores = dot_nt(jnp.where(own, query, jnp.zeros_like(query)), key) + bias_s[head]
            top = jnp.max(scores, axis=-1, keepdims=True)
            grown = jnp.exp(scores - top)
            probs = (grown * (1.0 / jnp.sum(grown, axis=-1, keepdims=True))).astype(BF16)
            probs_ref[head] = probs
            outs.append(dot_nn(probs, value))
        lefts_ref[1, :, at] = jnp.where(first, outs[0], outs[1]).astype(BF16)
        return carry

    lax.fori_loop(0, heads // 2, pair_step, 0, unroll=UNROLL_F)
    for at, out_ref in enumerate((left0_ref, left1_ref, left2_ref, left3_ref)):
        out_ref[...] = jnp.where(place_is(where_ref, at, 3), lefts_ref[1], lefts_ref[0])
    copy_proj.wait()
    attended = dot_nn(lefts_ref[1], wproj_ref[...]) + row_of(pbias_ref)
    attended_ref[...] = attended
    hidden = pad_s[...] + row_of(gamma1_ref) * attended
    hidden_ref[...] = hidden
    xhat2, _ = norm_stats(hidden)
    inner_ref[...] = (xhat2 * row_of(gain2_ref) + row_of(bias2_ref)).astype(BF16)


def forward(heads, pad, where, patches, row_mask, rel_index, token, gain1, bias1, qbias, vbias, table_t,
            pbias, gamma1, gain2, bias2, wqkv, wproj, deps=()):
    rows, width = patches.shape[1:]
    keys = round_up(pad, LANES)
    entries = round_up(table_t.shape[1], LANES)
    outs = (
        shape_out((pad, LANES), F32),
        shape_out((pad, width), BF16),
        shape_out((pad, width), BF16),
        shape_out((pad, width), BF16),
        shape_out((pad, width), BF16),
        shape_out((pad, width), BF16),
        shape_out((keys, width), BF16),
        shape_out((keys, width), BF16),
        shape_out((heads, pad, keys), BF16),
        shape_out((pad, width), F32),
        shape_out((pad, width), F32),
        shape((pad, width), BF16),
    )
    return call(
        functools.partial(forward_body, heads),
        outs,
        "shhhhhhhhhhhhhaa",
        (where, patches, row_mask, rel_index, token, gain1, bias1, qbias, vbias, table_t, pbias, gamma1,
         gain2, bias2, wqkv, wproj),
        (
            pltpu.VMEM((pad, width), F32),
            pltpu.VMEM((LANES, keys), F32),
            pltpu.VMEM((pad, keys), jnp.int32),
            pltpu.VMEM((heads // 2, 8, entries), jnp.int32),
            pltpu.VMEM((heads, pad, keys), F32),
            pltpu.VMEM(wqkv.shape, BF16),
            pltpu.VMEM(wproj.shape, BF16),
            pltpu.VMEM((2, pad, width), BF16),
            pltpu.SemaphoreType.DMA((2,)),
        ),
            )


def mlp_body(
    first, inner_ref, b1a_ref, b1b_ref, w1a_ref, w1b_ref, w2a_ref, w2b_ref, bias_ref, *rest
):
    if first:
        grads, masks, gamma2_ref = rest[0:2], rest[2:4], rest[4]
        rest = rest[5:]
        dbranches, rest = rest[0:2], rest[2:]
        cot_out, rest = rest[0], rest[1:]
        pad_s, wide_s = rest[-2:]
        rest = rest[:-2]
        pad = inner_ref.shape[0]
        for grad_ref, mask_ref, out_ref in zip(grads, masks, dbranches):
            column = mask_column(mask_ref, wide_s, pad)[:, 0:1]
            cotangent = load_padded(grad_ref, pad_s) * column
            out_ref[...] = (row_of(gamma2_ref) * cotangent).astype(BF16)
            if out_ref is dbranches[0]:
                own_cotangent = cotangent
            else:
                cot_out[...] = cotangent
        dbranch = dbranches[0][...]
        cotangent = own_cotangent
    else:
        dbranch, rest = rest[0][...], rest[1:]
    acta_ref, actb_ref, dprea_ref, dpreb_ref, dinner_ref, sums_ref, *more = rest
    if first:
        branch_ref = more[0]
    inner = inner_ref[...]
    branch = None
    dinner = None
    for at, (w1, w2, b1, act_out, dpre_out) in enumerate((
        (w1a_ref, w2a_ref, b1a_ref, acta_ref, dprea_ref),
        (w1b_ref, w2b_ref, b1b_ref, actb_ref, dpreb_ref),
    )):
        pre = dot_nn(inner, w1[...]) + row_of(b1).astype(F32)
        phi = 0.5 + 0.5 * lax.erf(pre * (0.5**0.5))
        act = (pre * phi).astype(BF16)
        act_out[...] = act
        slope = phi + pre * (jnp.exp(-0.5 * pre * pre) * 0.3989422804014327)
        dact = dot_nt(dbranch, w2[...])
        dpre = (dact * slope).astype(BF16)
        dpre_out[...] = dpre
        sums_ref[at : at + 1, :] = jnp.sum(dpre.astype(F32), axis=0, keepdims=True)
        this_dinner = dot_nt(dpre, w1[...])
        dinner = this_dinner if dinner is None else dinner + this_dinner
        if first:
            this_branch = dot_nn(act, w2[...])
            branch = this_branch if branch is None else branch + this_branch
    dinner_ref[...] = dinner.astype(dinner_ref.dtype)
    if first:
        branch = branch + row_of(bias_ref)
        branch_ref[...] = branch
        sums_ref[2:3, :] = jnp.sum(cotangent * branch, axis=0, keepdims=True)
        sums_ref[3:4, :] = jnp.sum(dbranch.astype(F32), axis=0, keepdims=True)
    else:
        sums_ref[2:4, :] = jnp.zeros_like(sums_ref[2:4, :])
    sums_ref[4:8, :] = jnp.zeros_like(sums_ref[4:8, :])


def mlp(inner, weights, bias, given, first, deps=(), carry=()):
    pad, width = inner.shape
    ff = weights[2].shape[1]
    kind = F32 if first else BF16
    outs = (
        (shape((pad, ff), BF16),) * 4
        + (shape((pad, width), kind), shape((8, ff), F32))
    )
    scratch = ()
    if first:
        outs = (shape((pad, width), BF16),) * 2 + (shape((pad, width), F32),) + outs
        outs += (shape_out((pad, width), F32),)
        scratch = (pltpu.VMEM((pad, width), F32), pltpu.VMEM((LANES, round_up(pad, LANES)), F32))
    return call(
        functools.partial(mlp_body, first), outs, "vhhvvvvh" + ("hvhvh" if first else "v"),
        (inner, *weights, bias, *given), scratch, cost=5, deps=deps, carry=carry,
    )


def far_branch_body(acta_ref, actb_ref, w2a_ref, w2b_ref, cot_ref, branch_ref, sums_ref):
    branch = dot_nn(acta_ref[...], w2a_ref[...]) + dot_nn(actb_ref[...], w2b_ref[...])
    branch_ref[...] = branch.astype(BF16)
    sums_ref[...] = jnp.zeros_like(sums_ref)
    sums_ref[2:3, :] = jnp.sum(cot_ref[...] * branch, axis=0, keepdims=True)


def far_branch(acta, actb, w2a, w2b, cotangent, deps=()):
    pad, width = cotangent.shape
    return call(
        far_branch_body, (shape_out((pad, width), BF16), shape((8, width), F32)), "vvvvv",
        (acta, actb, w2a, w2b, cotangent), cost=30, deps=deps,
    )


def split_rows(out_send, out_keep, total, low, block):
    for step in range(total.shape[0] // (2 * block)):
        even = total[2 * step * block : (2 * step + 1) * block]
        odd = total[(2 * step + 1) * block : (2 * step + 2) * block]
        out_send[step] = jnp.where(low, even, odd).astype(BF16)
        out_keep[step] = jnp.where(low, odd, even).astype(BF16)


def pair_grad_body(*refs):
    out_ref = refs[-1]
    for at in range(2):
        left0, left1, right0, right1 = refs[4 * at : 4 * at + 4]
        total = dot_tn(left0[...], right0[...]) + dot_tn(left1[...], right1[...])
        out_ref[at] = total.astype(BF16)


def pair_grad(one, two, deps=(), carry=()):
    width, ff = one[0].shape[1], one[2].shape[1]
    return call(
        pair_grad_body, shape((2, width, ff), BF16), "v" * 8, (*one, *two), cost=0.7, deps=deps,
        carry=carry,
    )


def fc_keep_body(block, where_ref, *refs):
    other, send_ref, keep_ref = refs[8:]
    for at in range(2):
        left0, left1, right0, right1 = refs[4 * at : 4 * at + 4]
        total = dot_tn(left0[...], right0[...]) + dot_tn(left1[...], right1[...])
        split_rows(
            send_ref.at[at], keep_ref.at[at], total + other[at].astype(F32), where_ref[2] > 0,
            block,
        )


def fc_keep(where, block, one, two, other, deps=(), carry=()):
    width, ff = one[0].shape[1], one[2].shape[1]
    outs = (shape((2, width // (2 * block), block, ff), BF16),) * 2
    return call(
        functools.partial(fc_keep_body, block), outs, "s" + "v" * 9, (where, *one, *two, other),
        cost=1.2, deps=deps, carry=carry,
    )


def deal_out(where_ref, outs, dqkv_ref, datt):
    third = dqkv_ref.shape[1] // 3
    for step, out_ref in enumerate(outs):
        part = datt
        for place in range(3):
            columns = dqkv_ref[:, place * third : (place + 1) * third]
            part = jnp.where(place_is(where_ref, step, place), columns, part)
        out_ref[...] = part


def heads_back(pairs, first_pair, head_size, q_ref, k_ref, v_ref, probs_ref, dmixed_ref, dqkv_ref,
               dscores_ref):
    pad = q_ref.shape[0]
    third = dqkv_ref.shape[1] // 3
    lane = lax.broadcasted_iota(jnp.int32, (1, LANES), 1)
    first = lane < head_size
    scale = head_size ** (-0.5)

    def pair_step(step, carry):
        at = pl.ds(pl.multiple_of((first_pair + step) * LANES, LANES), LANES)
        query = q_ref[:, at]
        key = k_ref[:, at]
        value = v_ref[:, at]
        dmixed = dmixed_ref[:, at]
        dq, dk, dv = [], [], []
        for side in range(2):
            own = first if side == 0 else jnp.logical_not(first)
            probs_b = probs_ref[2 * (first_pair + step) + side]
            probs = probs_b.astype(F32)
            dprobs = dot_nt(jnp.where(own, dmixed, jnp.zeros_like(dmixed)), value)
            inside = jnp.sum(probs * dprobs, axis=-1, keepdims=True)
            dscores = (probs * (dprobs - inside)).astype(BF16)
            dscores_ref[2 * step + side] = dscores
            dq.append(dot_nn(dscores, key))
            dk.append(dot_tn(dscores, query))
            dv.append(dot_tn(probs_b, dmixed))
        out = pl.multiple_of(step * LANES, LANES)
        dqkv_ref[:, pl.ds(out, LANES)] = (jnp.where(first, dq[0], dq[1]) * scale).astype(BF16)
        dqkv_ref[:, pl.ds(pl.multiple_of(out + third, LANES), LANES)] = (
            jnp.where(first, dk[0], dk[1])[:pad].astype(BF16)
        )
        dqkv_ref[:, pl.ds(pl.multiple_of(out + 2 * third, LANES), LANES)] = (
            jnp.where(first, dv[0], dv[1])[:pad].astype(BF16)
        )
        return carry

    lax.fori_loop(0, pairs, pair_step, 0, unroll=pairs)


def column_sums(out_ref, at, dqkv_ref):
    third = dqkv_ref.shape[1] // 3
    for row, part in ((4, 0), (5, 2)):
        lanes = slice(part * third, (part + 1) * third)
        out_ref[row : row + 1, at * third : (at + 1) * third] = jnp.sum(
            dqkv_ref[:, lanes].astype(F32), axis=0, keepdims=True
        )


def backward_body(
    heads,
    where_ref,
    dinner0_ref,
    dinner1_ref,
    hidden_ref,
    attended_ref,
    outgrad_ref,
    mask_ref,
    gain2_ref,
    gamma1_ref,
    wproj_ref,
    q_ref,
    k_ref,
    v_ref,
    probs_ref,
    dhidden_ref,
    dqkv_ref,
    out0_ref,
    out1_ref,
    out2_ref,
    out3_ref,
    dscores_ref,
    sums_ref,
    pad_s,
    dmixed_ref,
):
    width = hidden_ref.shape[1]
    cotangent = load_padded(outgrad_ref, pad_s) * mask_ref[:, 0:1]
    xhat, root = norm_stats(hidden_ref[...])
    dinner = dinner0_ref[...].astype(F32) + dinner1_ref[...].astype(F32)
    dhidden = cotangent + norm_back(dinner, xhat, root, row_of(gain2_ref))
    dhidden_ref[...] = dhidden
    datt = (row_of(gamma1_ref) * dhidden).astype(BF16)
    dmixed_ref[...] = dot_nt(datt, wproj_ref[...]).astype(BF16)
    sums_ref[0:1, :] = jnp.sum(dinner * xhat, axis=0, keepdims=True)
    sums_ref[1:2, :] = jnp.sum(dinner, axis=0, keepdims=True)
    sums_ref[2:3, :] = jnp.sum(dhidden * attended_ref[...], axis=0, keepdims=True)
    sums_ref[3:4, :] = jnp.sum(datt.astype(F32), axis=0, keepdims=True)
    sums_ref[4:8, :] = jnp.zeros((4, width), F32)
    heads_back(heads // 2, 0, width // heads, q_ref, k_ref, v_ref, probs_ref, dmixed_ref, dqkv_ref,
               dscores_ref)
    deal_out(
        where_ref, (out0_ref, out1_ref, out2_ref, out3_ref), dqkv_ref, datt
    )
    column_sums(sums_ref, 0, dqkv_ref)


def backward(heads, where, dinner0, dinner1, hidden, attended, out_grad, mask_col, gain2, gamma1,
             wproj, q, k, v, probs, deps=()):
    pad, width = hidden.shape
    keys = k.shape[0]
    outs = (
        shape((pad, width), F32),
        shape((pad, 3 * width), BF16),
        shape((pad, width), BF16),
        shape((pad, width), BF16),
        shape((pad, width), BF16),
        shape((pad, width), BF16),
        shape((heads, pad, keys), BF16),
        shape((8, width), F32),
    )
    return call(
        functools.partial(backward_body, heads),
        outs,
        "svvhhhhhhhhhhh",
        (where, dinner0, dinner1, hidden, attended, out_grad, mask_col, gain2, gamma1, wproj, q, k,
         v, probs),
        (pltpu.VMEM((pad, width), F32), pltpu.VMEM((pad, width), BF16)),
        cost=5,
        deps=deps,
    )


def first_norm_body(
    patches_ref, mask_ref, token_ref, gain1_ref, dqkv_ref, wqkv_ref, dhidden_ref,
    patchgrad_ref, sums_ref, pad_s,
):
    rows, width = patches_ref.shape[1:]
    picked = mask_ref[:, 0:1] > 0
    start = jnp.where(picked, row_of(token_ref), load_padded(patches_ref, pad_s))
    xhat, root = norm_stats(start)
    dnormed = dot_nt(dqkv_ref[...], wqkv_ref[...])
    dstart = dhidden_ref[...] + norm_back(dnormed, xhat, root, row_of(gain1_ref))
    patchgrad_ref[0] = jnp.where(picked, 0.0, dstart)[0:rows]
    sums_ref[0:1, :] = jnp.sum(jnp.where(picked, dstart, 0.0), axis=0, keepdims=True)
    sums_ref[1:2, :] = jnp.sum(dnormed * xhat, axis=0, keepdims=True)
    sums_ref[2:3, :] = jnp.sum(dnormed, axis=0, keepdims=True)
    sums_ref[3:8, :] = jnp.zeros((5, width), F32)


def first_norm(patches, mask_col, token, gain1, dqkv, wqkv, dhidden, deps=()):
    rows, width = patches.shape[1:]
    pad = mask_col.shape[0]
    outs = (shape_out((1, rows, width), F32), shape((8, width), F32))
    return call(
        first_norm_body, outs, "hhhhvhv",
        (patches, mask_col, token, gain1, dqkv, wqkv, dhidden),
        (pltpu.VMEM((pad, width), F32),), cost=5, deps=deps,
    )


def layer_end_body(hidden_ref, branch0_ref, branch1_ref, gamma2_ref, out_ref):
    branch = branch0_ref[...] + branch1_ref[...].astype(F32)
    layer = hidden_ref[...] + row_of(gamma2_ref) * branch
    out_ref[0] = layer[0 : out_ref.shape[1]].astype(BF16)


def layer_end(rows, hidden, branch0, branch1, gamma2, deps=(), carry=()):
    return call(
        layer_end_body, shape_out((1, rows, hidden.shape[1]), BF16), "hhvh",
        (hidden, branch0, branch1, gamma2), deps=deps, carry=carry,
    )


def table_grad_body(
    where_ref, index_ref, ds_ref, sums_b_ref, sums_n_ref, sums0_ref, sums1_ref, sums_f_ref, out_ref,
    index_s,
    total_s,
):
    rows = index_ref.shape[0]
    pad, head_pad, keys = ds_ref.shape
    high_count = total_s.shape[0] // head_pad
    index_s[...] = jnp.zeros_like(index_s)
    index_s[0:rows, 0:rows] = index_ref[...]
    total_s[...] = jnp.zeros_like(total_s)
    below = lax.broadcasted_iota(jnp.int32, (LANES, keys), 0).astype(BF16)
    ones = jnp.ones((LANES, keys), BF16)
    group = 16

    def step(at, carry):
        base = pl.multiple_of(at * group, group)
        lines = index_s[pl.ds(base, group), :]
        low = (lines & (LANES - 1)).astype(F32).astype(BF16)
        high = (lines >> 7).astype(F32).astype(BF16)
        total = None
        for i in range(group):
            onehot = jnp.where(below == low[i : i + 1], ones, jnp.zeros_like(ones))
            ds = ds_ref[base + i]
            left = jnp.concatenate(
                [
                    jnp.where(high[i : i + 1] == jnp.asarray(part, BF16), ds, jnp.zeros_like(ds))
                    for part in range(high_count)
                ],
                axis=0,
            )
            one = dot_nt(left, onehot)
            total = one if total is None else total + one
        total_s[...] += total
        return carry

    lax.fori_loop(0, pad // group, step, 0, unroll=2)
    for part in range(high_count):
        out_ref[0:head_pad, part * LANES : (part + 1) * LANES] = total_s[
            part * head_pad : (part + 1) * head_pad
        ]
    sums = sums0_ref[...] + sums1_ref[...] + sums_f_ref[...]
    out_ref[head_pad : head_pad + 6, :] = sums_b_ref[0:6, :]
    out_ref[head_pad + 6 : head_pad + 8, :] = sums[2:4]
    out_ref[head_pad + 8 : head_pad + 11, :] = sums_n_ref[0:3, :]
    for part in range(4):
        mine = jnp.where(where_ref[0] == part // 2, 1.0, 0.0)
        own = jnp.where(where_ref[1] == part % 2, sums[0:1], sums[1:2])
        out_ref[head_pad + 11 + part : head_pad + 12 + part, :] = mine * own
    out_ref[head_pad + 15 :, :] = jnp.zeros_like(out_ref[head_pad + 15 :, :])


def table_grad(where, rel_index, dscores, sums_b, sums_n, sums0, sums1, sums_f, entries, deps=()):
    pad, head_pad, keys = dscores.shape
    high_count = round_up(entries, LANES) // LANES
    width = sums_b.shape[1]
    return call(
        table_grad_body, shape((head_pad + 16, width), F32), "shvvvvvv",
        (where, rel_index, dscores, sums_b, sums_n, sums0, sums1, sums_f),
        (pltpu.VMEM((pad, keys), jnp.int32), pltpu.VMEM((high_count * head_pad, LANES), F32)),
        cost=3.2, deps=deps,
    )


def late_grad_body(block, piece, where_ref, *refs):
    lefts, rights, send_ref, keep_ref = refs[:4], refs[4:8], refs[8], refs[9]
    total = None
    for step in range(4):
        half = rights[step].shape[1] // 2
        one = dot_tn(lefts[step][...], rights[step][:, piece * half : (piece + 1) * half])
        total = one if total is None else total + one
    split_rows(send_ref.at[0], keep_ref.at[0], total, where_ref[2] > 0, block)


def late_grad(where, block, piece, lefts, rights, deps=(), carry=()):
    width = lefts[0].shape[1]
    half = rights[0].shape[1] // 2
    outs = (shape((1, width // (2 * block), block, half), BF16),) * 2
    return call(
        functools.partial(late_grad_body, block, piece), outs, "shvvvvvvv",
        (where, *lefts, *rights), cost=1.2, deps=deps, carry=carry,
    )


def fold_body(bit, where_ref, keep_ref, met_ref, send_out, keep_out):
    low = where_ref[2 + bit] > 0
    for at in range(send_out.shape[0]):
        for step in range(send_out.shape[1]):
            even, odd = (
                keep_ref[at, 2 * step + side].astype(F32) + met_ref[at, 2 * step + side].astype(F32)
                for side in range(2)
            )
            send_out[at, step] = jnp.where(low, even, odd).astype(BF16)
            keep_out[at, step] = jnp.where(low, odd, even).astype(BF16)


def fold(where, bit, keep, met, deps=(), carry=()):
    items, count, block, width = keep.shape
    return call(
        functools.partial(fold_body, bit), (shape((items, count // 2, block, width), BF16),) * 2,
        "svv", (where, keep, met), cost=0.4, deps=deps, carry=carry,
    )


def last_sum_body(keep_ref, met_ref, *outs):
    for at, out_ref in enumerate(outs):
        total = keep_ref[at, 0].astype(F32) + met_ref[at, 0].astype(F32)
        out_ref[...] = total.astype(out_ref.dtype)


def last_sum(keep, met, kind, deps=(), carry=()):
    make = shape_out if kind == F32 else shape
    return call(
        last_sum_body, (make(keep.shape[2:], kind),) * keep.shape[0], "vv", (keep, met), cost=0.4,
        deps=deps, carry=carry,
    )


def join_body(before_ref, keep_ref, met_ref, out_ref):
    half = before_ref.shape[1]
    out_ref[:, :half] = before_ref[...]
    out_ref[:, half:] = (keep_ref[0, 0].astype(F32) + met_ref[0, 0].astype(F32)).astype(BF16)


def join(before, keep, met, deps=(), carry=()):
    block, half = before.shape
    return call(
        join_body, shape((block, 2 * half), BF16), "vvv", (before, keep, met), deps=deps,
        carry=carry,
    )


def assemble_body(where_ref, own_ref, over_x_ref, over_core_ref, qkv_ref, proj_ref):
    width = own_ref.shape[1]
    high = where_ref[0] > 0
    core = where_ref[1] > 0
    own, far = own_ref[...], over_x_ref[...]
    side, corner = over_core_ref[0], over_core_ref[1]
    here = (jnp.where(core, side, own), jnp.where(core, own, side))
    there = (jnp.where(core, corner, far), jnp.where(core, far, corner))
    for at in range(2):
        qkv_ref[:, at * width : (at + 1) * width] = jnp.where(high, there[at], here[at]).astype(F32)
    qkv_ref[:, 2 * width :] = jnp.where(high, here[0], there[0]).astype(F32)
    proj_ref[...] = jnp.where(high, here[1], there[1]).astype(F32)


def assemble(where, own, far, pair, deps=()):
    block, width = own.shape
    return call(
        assemble_body, (shape_out((block, 3 * width), F32), shape_out((block, width), F32)),
        "svvv", (where, own, far, pair), deps=deps,
    )


def on_device(
    dp,
    patches,
    row_mask,
    out_grad,
    rel_index,
    mask_token,
    ln1_gain,
    ln1_bias,
    qkv_weight,
    query_bias,
    value_bias,
    rel_table,
    proj_weight,
    proj_bias,
    gamma1,
    ln2_gain,
    ln2_bias,
    fc1_weight,
    fc1_bias,
    fc2_weight,
    fc2_bias,
    gamma2,
):
    rows, width = patches.shape[1:]
    entries, heads = rel_table.shape
    pad = round_up(rows, 16)
    mp_at = lax.axis_index("mp")
    dp_at = lax.axis_index("dp")
    x_at, core_at = mp_at // 2, mp_at % 2
    bits = dp.bit_length() - 1
    where = jnp.stack(
        [x_at, core_at] + [(dp_at >> bit) & 1 for bit in range(bits)]
    ).astype(jnp.int32)

    def swap(axis, bit):
        count = 4 if axis == "mp" else dp
        pairs = [(at, at ^ bit) for at in range(count)]
        return lambda value: lax.ppermute(value, axis, pairs)

    over_core, over_x = swap("mp", 1), swap("mp", 2)
    over_bit = [swap("dp", 1 << bit) for bit in range(bits)]

    out_grad1, row_mask1 = over_x(out_grad), over_x(row_mask)
    b1b, w1b, w2b = over_core(fc1_bias), over_core(fc1_weight), over_core(fc2_weight)

    before = []

    def step(kernel, *args, deps=(), **more):
        out, token = kernel(*args, deps=tuple(before) + tuple(deps), **more)
        before[:] = [token]
        return out

    mask_col, left0, left1, left2, left3, q, k, v, probs, attended, hidden, inner = step(
        forward, heads, pad, where, patches, row_mask, rel_index, mask_token, ln1_gain, ln1_bias,
        query_bias, value_bias, rel_table.T, proj_bias, gamma1, ln2_gain, ln2_bias, qkv_weight,
        proj_weight,
    )
    inner1 = over_x(inner)
    weights = (fc1_bias, b1b, fc1_weight, w1b, fc2_weight, w2b)
    dbranch, dbranch1, cot1, acta0, actb0, dprea0, dpreb0, dinner0, sums0, branch0, left1 = step(
        mlp, inner, weights, fc2_bias, (out_grad, out_grad1, row_mask, row_mask1, gamma2), True,
        carry=(left1,),
    )
    met_left1 = over_core(left1)
    acta1, actb1, dprea1, dpreb1, dinner1, sums1 = step(
        mlp, inner1, weights, fc2_bias, (dbranch1,), False
    )
    dinner_in = over_x(dinner1)

    block = width // dp

    def middle(keep, met, first, last):
        for bit in range(first, last):
            send, keep = step(fold, where, bit, keep, met)
            met = over_bit[bit](send)
        return keep, met

    fc_other = over_core(
        step(pair_grad, (inner, inner1, dpreb0, dpreb1), (dbranch, dbranch1, actb0, actb1))
    )
    branch1, sums_f = step(far_branch, acta1, actb1, fc2_weight, w2b, cot1)
    fc_send, fc_kept, left2, left3 = step(
        fc_keep, where, block, (inner, inner1, dprea0, dprea1), (dbranch, dbranch1, acta0, acta1),
        fc_other, deps=(met_left1,), carry=(left2, left3),
    )
    fc_met = over_bit[0](fc_send)
    met_left2, met_left3 = over_x(left2), swap("mp", 3)(left3)

    dhidden, dqkv, own, core, far, corner, dscores, sums_b = step(
        backward, heads, where, dinner0, dinner_in, hidden, attended, out_grad, mask_col, ln2_gain,
        gamma1, proj_weight, q, k, v, probs,
    )
    met_far, met_corner, met_core = over_x(far), swap("mp", 3)(corner), over_core(core)
    patch_grad, sums_n = step(
        first_norm, patches, mask_col, mask_token, ln1_gain, dqkv, qkv_weight, dhidden,
        deps=(met_left2, met_left3),
    )
    head_pad = 16
    ds = jnp.pad(jnp.transpose(dscores, (1, 0, 2)), ((0, 0), (0, head_pad - heads), (0, 0)))
    small = step(table_grad, where, rel_index, ds, sums_b, sums_n, sums0, sums1, sums_f,
                 entries)
    small = small + over_core(small)
    fc_kept, fc_met = middle(fc_kept, fc_met, 1, 2)

    late = ((left0, met_left1, met_left2, met_left3), (own, met_core, met_far, met_corner))
    late0_send, late0_keep = step(late_grad, where, block, 0, *late)
    late0_met = over_bit[0](late0_send)
    late1_send, late1_keep = step(late_grad, where, block, 1, *late)
    late1_met = over_bit[0](late1_send)
    small = small + over_x(small)

    late0_send, late0_keep = step(fold, where, 1, late0_keep, late0_met)
    late0_met = over_bit[1](late0_send)
    fc_send, fc_kept, small, branch1 = step(
        fold, where, 2, fc_kept, fc_met, carry=(small, branch1)
    )
    fc_met = over_bit[2](fc_send)
    fc_kept, fc_met = middle(fc_kept, fc_met, 3, bits)
    branch_in = over_x(branch1)
    small = small + over_bit[0](small)
    late1_send, late1_keep = step(fold, where, 1, late1_keep, late1_met)
    late1_met = over_bit[1](late1_send)
    late0_send, late0_keep, small = step(
        fold, where, 2, late0_keep, late0_met, carry=(small,)
    )
    late0_met = over_bit[2](late0_send)
    late0_keep, late0_met = middle(late0_keep, late0_met, 3, bits)
    small = small + over_bit[1](small)
    layer_out, small = step(layer_end, rows, hidden, branch0, branch_in, gamma2, carry=(small,))
    late1_keep, late1_met = middle(late1_keep, late1_met, 2, bits)
    for bit in range(2, bits):
        small = small + over_bit[bit](small)
    fc1_weight_grad, fc2_weight_grad = step(last_sum, fc_kept, fc_met, F32)
    late0_own = step(last_sum, late0_keep, late0_met, BF16)
    late_own = step(join, late0_own, late1_keep, late1_met)
    late_x = over_x(late_own)

    late_pair = over_core(jnp.stack([late_own, late_x]))
    qkv_weight_grad, proj_weight_grad = step(assemble, where, late_own, late_x, late_pair)

    rel_grad = small[:heads, :entries].T
    (ln2_gain_grad, ln2_bias_grad, gamma1_grad, proj_bias_grad, query_bias_grad, value_bias_grad,
     gamma2_grad, fc2_bias_grad, mask_token_grad, ln1_gain_grad, ln1_bias_grad) = [
        small[head_pad + at] for at in range(11)
    ]
    fc1_bias_grad = lax.dynamic_index_in_dim(small, head_pad + 11 + mp_at, 0, False)
    return (
        layer_out,
        patch_grad,
        mask_token_grad,
        ln1_gain_grad,
        ln1_bias_grad,
        qkv_weight_grad,
        query_bias_grad,
        value_bias_grad,
        rel_grad,
        proj_weight_grad,
        proj_bias_grad,
        gamma1_grad,
        ln2_gain_grad,
        ln2_bias_grad,
        fc1_weight_grad,
        fc1_bias_grad,
        fc2_weight_grad.T,
        fc2_bias_grad,
        gamma2_grad,
    )


def solution(mesh):
    rows3 = P(("dp", "mp"), None, None)
    placed = (
        (rows3, P(("dp", "mp"), None), rows3)
        + (P(),) * 13
        + (P(None, "mp"), P("mp"), P("mp", None), P(), P())
    )
    return jax.shard_map(
        functools.partial(on_device, mesh.shape["dp"]),
        mesh=mesh,
        in_specs=placed,
        out_specs=(
            rows3,
            rows3,
            P(),
            P(),
            P(),
            P("dp", None),
            P(),
            P(),
            P(),
            P("dp", None),
            P(),
            P(),
            P(),
            P(),
            P("dp", "mp"),
            P("mp"),
            P("mp", "dp"),
            P(),
            P(),
        ),
        check_vma=False,
    )
```

```python
import functools

import jax
import jax.numpy as jnp
from jax import lax
from jax.experimental import pallas as pl
from jax.experimental.pallas import tpu as pltpu
from jax.sharding import PartitionSpec as P

F32 = jnp.float32
BF16 = jnp.bfloat16
EPS = 1e-06
LANES = 128
SCALE = 1
COST = dict(fwd=1, mlp=5, far=30, pair=0.42, keep=0.6, back=5, norm=5, table=3.2, late=1.2, fold=0.4, last=0.4, end=0.2, join=1)
ORDER = (
    "N", "T", "f1", "A", "B", "x", "a1", "f2@%", "h", "y", "b1", "a2@", "z", "b2", "E@", "w", "F", "S", "J",
)
UNROLL_F = 6
UNROLL_B = 6
VMEM_LIMIT = 16 * 1024 * 1024


def round_up(value, step):
    return -(-value // step) * step


def dot_nn(left, right):
    return lax.dot_general(left, right, (((1,), (0,)), ((), ())), preferred_element_type=F32)


def dot_nt(left, right):
    return lax.dot_general(left, right, (((1,), (1,)), ((), ())), preferred_element_type=F32)


def dot_tn(left, right):
    return lax.dot_general(left, right, (((0,), (0,)), ((), ())), preferred_element_type=F32)


def row_of(ref):
    return ref[...].reshape(1, ref.shape[0])


def norm_stats(values):
    middle = jnp.mean(values, axis=-1, keepdims=True)
    centred = values - middle
    spread = jnp.mean(centred * centred, axis=-1, keepdims=True)
    root = lax.rsqrt(spread + EPS)
    return centred * root, root


def norm_back(d_out, xhat, root, gain):
    t = d_out * gain
    mean_t = jnp.mean(t, axis=-1, keepdims=True)
    mean_tx = jnp.mean(t * xhat, axis=-1, keepdims=True)
    return root * (t - mean_t - xhat * mean_tx)


SPACES = {
    "h": (pltpu.HBM, pltpu.VMEM),
    "v": (None, pltpu.VMEM),
    "s": (None, pltpu.SMEM),
    "a": (pltpu.HBM, pl.ANY),
}


def call(body, outs, kinds, values, scratch=(), cost=1, deps=(), carry=(), hold=()):
    specs, given = [], []
    for kind, value in zip(kinds, values, strict=True):
        keep, space = SPACES[kind]
        specs.append(pl.BlockSpec(memory_space=space))
        given.append(value if keep is None else pltpu.with_memory_space_constraint(value, keep))
    outs = outs if isinstance(outs, tuple) else (outs,)
    passed = tuple(carry) + tuple(hold)
    n_in, n_more, n_out = len(given), len(deps) + len(passed), len(outs)

    def inner(*refs):
        rest = refs[n_in + n_more :]
        rest[n_out][...] = jnp.zeros_like(rest[n_out])
        body(*refs[:n_in], *rest[:n_out], *rest[n_out + 1 + len(passed) :])

    anywhere = pl.BlockSpec(memory_space=pl.ANY)
    whole = pl.BlockSpec(memory_space=pltpu.VMEM)
    in_hbm = [value.dtype == BF16 and len(value.shape) == 2 for value in carry]
    held = tuple(pltpu.with_memory_space_constraint(value, pltpu.VMEM) for value in hold)
    out = pl.pallas_call(
        inner,
        name=getattr(body, "func", body).__name__,
        out_shape=outs
        + (pltpu.VMEM((8, LANES), F32),)
        + tuple(
            (pltpu.HBM if pinned else jax.ShapeDtypeStruct)(c.shape, c.dtype)
            for pinned, c in zip(in_hbm, carry)
        )
        + tuple(pltpu.VMEM(value.shape, value.dtype) for value in hold),
        in_specs=specs + [anywhere] * n_more,
        out_specs=(whole,) * (n_out + 1) + (anywhere,) * len(passed),
        input_output_aliases={n_in + len(deps) + at: n_out + 1 + at for at in range(len(passed))},
        scratch_shapes=list(scratch),
        compiler_params=pltpu.CompilerParams(vmem_limit_bytes=VMEM_LIMIT),
        cost_estimate=pl.CostEstimate(
            flops=int(cost * SCALE * 10**9), bytes_accessed=1000, transcendentals=0
        ),
    )(
        *given,
        *deps,
        *(
            pltpu.with_memory_space_constraint(c, pltpu.HBM) if pinned else c
            for pinned, c in zip(in_hbm, carry)
        ),
        *held,
    )
    results = out[:n_out] + out[n_out + 1 :]
    return (results if len(results) > 1 else results[0]), out[n_out]


def shape(dims, kind):
    return pltpu.VMEM(dims, kind)


def shape_out(dims, kind):
    return pltpu.HBM(dims, kind)


def load_padded(source_ref, pad_ref):
    rows = source_ref.shape[1]
    tail = (rows // 8) * 8
    pad_ref[tail:, :] = jnp.zeros_like(pad_ref[tail:, :])
    pad_ref[0:rows, :] = source_ref[0].astype(F32)
    return pad_ref[...]


def mask_column(mask_ref, wide_ref, pad):
    rows = mask_ref.shape[1]
    wide_ref[...] = jnp.zeros_like(wide_ref)
    line = jnp.where(mask_ref[...] > 0, 1.0, 0.0)
    wide_ref[:, 0:rows] = jnp.broadcast_to(line, (LANES, rows))
    return wide_ref[...].T[:pad]


def place_is(where_ref, step, place):
    high = where_ref[0] == (place >> 1) ^ (step >> 1)
    low = where_ref[1] == (place & 1) ^ (step & 1)
    return jnp.logical_and(high, low)


def forward_body(
    heads,
    where_ref,
    patches_ref,
    mask_ref,
    index_ref,
    token_ref,
    gain1_ref,
    bias1_ref,
    qbias_ref,
    vbias_ref,
    table_ref,
    pbias_ref,
    gamma1_ref,
    gain2_ref,
    bias2_ref,
    wqkv_hbm,
    wproj_hbm,
    mask_out,
    left0_ref,
    left1_ref,
    left2_ref,
    left3_ref,
    q_ref,
    k_ref,
    v_ref,
    probs_ref,
    attended_ref,
    hidden_ref,
    inner_ref,
    pad_s,
    wide_s,
    index_s,
    table_s,
    bias_s,
    wqkv_ref,
    wproj_ref,
    lefts_ref,
    sems,
):
    rows, width = patches_ref.shape[1:]
    pad = q_ref.shape[0]
    keys = k_ref.shape[0]
    head_size = width // heads
    copy_qkv = pltpu.make_async_copy(wqkv_hbm, wqkv_ref, sems.at[0])
    copy_qkv.start()
    copy_proj = pltpu.make_async_copy(wproj_hbm, wproj_ref, sems.at[1])
    copy_proj.start()

    index_s[...] = jnp.zeros_like(index_s)
    index_s[0:rows, 0:rows] = index_ref[...]
    entries = table_ref.shape[1]
    chunks = table_s.shape[2] // LANES
    top = jnp.max(jnp.abs(table_ref[...]))
    grow = 32767.0 / jnp.maximum(top, 1e-30)
    shrink = jnp.maximum(top, 1e-30) / 32767.0
    whole = jnp.round(table_ref[...] * grow).astype(jnp.int32)
    table_s[...] = jnp.zeros_like(table_s)
    for pair in range(heads // 2):
        both = whole[2 * pair : 2 * pair + 1] * 65536 + (whole[2 * pair + 1 : 2 * pair + 2] & 65535)
        table_s[pair, :, 0:entries] = jnp.broadcast_to(both, (8, entries))
    key_lane = lax.broadcasted_iota(jnp.int32, (1, LANES), 1)

    def gather_step(tile, carry):
        at_rows = pl.ds(pl.multiple_of(tile * 8, 8), 8)
        for half in range(keys // LANES):
            lanes = slice(half * LANES, (half + 1) * LANES)
            at = index_s[at_rows, lanes]
            low = at & (LANES - 1)
            high = at >> 7
            marks = [high == chunk for chunk in range(chunks)]
            real = key_lane + half * LANES < rows
            for pair in range(heads // 2):
                value = None
                for chunk in range(chunks):
                    line = table_s[pair, :, chunk * LANES : (chunk + 1) * LANES]
                    found = jnp.take_along_axis(line, low, axis=1, mode="promise_in_bounds")
                    value = found if value is None else jnp.where(marks[chunk], found, value)
                one = (value >> 16).astype(F32) * shrink
                two = ((value << 16) >> 16).astype(F32) * shrink
                if (half + 1) * LANES > rows:
                    one = jnp.where(real, one, -1e30)
                    two = jnp.where(real, two, -1e30)
                bias_s[2 * pair, at_rows, lanes] = one
                bias_s[2 * pair + 1, at_rows, lanes] = two
        return carry

    lax.fori_loop(0, pad // 8, gather_step, 0, unroll=2)

    column = mask_column(mask_ref, wide_s, pad)
    mask_out[...] = column
    picked = column[:, 0:1] > 0
    start = jnp.where(picked, row_of(token_ref), load_padded(patches_ref, pad_s))
    pad_s[...] = start
    xhat, _ = norm_stats(start)
    normed = (xhat * row_of(gain1_ref) + row_of(bias1_ref)).astype(BF16)
    lefts_ref[0] = normed
    copy_qkv.wait()
    scale = head_size ** (-0.5)
    q_ref[...] = ((dot_nn(normed, wqkv_ref[:, :width]) + row_of(qbias_ref)) * scale).astype(BF16)
    k_ref[0:pad, :] = dot_nn(normed, wqkv_ref[:, width : 2 * width]).astype(BF16)
    k_ref[pad:, :] = jnp.zeros_like(k_ref[pad:, :])
    v_ref[0:pad, :] = (dot_nn(normed, wqkv_ref[:, 2 * width :]) + row_of(vbias_ref)).astype(BF16)
    v_ref[pad:, :] = jnp.zeros_like(v_ref[pad:, :])

    lane = lax.broadcasted_iota(jnp.int32, (1, LANES), 1)
    first = lane < head_size

    def pair_step(pair, carry):
        at = pl.ds(pl.multiple_of(pair * LANES, LANES), LANES)
        query = q_ref[:, at]
        key = k_ref[:, at]
        value = v_ref[:, at]
        outs = []
        for side in range(2):
            head = pair * 2 + side
            own = first if side == 0 else jnp.logical_not(first)
            scores = dot_nt(jnp.where(own, query, jnp.zeros_like(query)), key) + bias_s[head]
            top = jnp.max(scores, axis=-1, keepdims=True)
            grown = jnp.exp(scores - top)
            probs = (grown * (1.0 / jnp.sum(grown, axis=-1, keepdims=True))).astype(BF16)
            probs_ref[head] = probs
            outs.append(dot_nn(probs, value))
        lefts_ref[1, :, at] = jnp.where(first, outs[0], outs[1]).astype(BF16)
        return carry

    lax.fori_loop(0, heads // 2, pair_step, 0, unroll=UNROLL_F)
    for at, out_ref in enumerate((left0_ref, left1_ref, left2_ref, left3_ref)):
        out_ref[...] = jnp.where(place_is(where_ref, at, 3), lefts_ref[1], lefts_ref[0])
    copy_proj.wait()
    attended = dot_nn(lefts_ref[1], wproj_ref[...]) + row_of(pbias_ref)
    attended_ref[...] = attended
    hidden = pad_s[...] + row_of(gamma1_ref) * attended
    hidden_ref[...] = hidden
    xhat2, _ = norm_stats(hidden)
    inner_ref[...] = (xhat2 * row_of(gain2_ref) + row_of(bias2_ref)).astype(BF16)


def forward(heads, pad, where, patches, row_mask, rel_index, token, gain1, bias1, qbias, vbias, table_t,
            pbias, gamma1, gain2, bias2, wqkv, wproj, deps=()):
    rows, width = patches.shape[1:]
    keys = round_up(pad, LANES)
    entries = round_up(table_t.shape[1], LANES)
    outs = (
        shape_out((pad, LANES), F32),
        shape_out((pad, width), BF16),
        shape_out((pad, width), BF16),
        shape_out((pad, width), BF16),
        shape_out((pad, width), BF16),
        shape_out((pad, width), BF16),
        shape((keys, width), BF16),
        shape((keys, width), BF16),
        shape((heads, pad, keys), BF16),
        shape((pad, width), F32),
        shape_out((pad, width), F32),
        shape((pad, width), BF16),
    )
    return call(
        functools.partial(forward_body, heads),
        outs,
        "shhhhhhhhhhhhhaa",
        (where, patches, row_mask, rel_index, token, gain1, bias1, qbias, vbias, table_t, pbias, gamma1,
         gain2, bias2, wqkv, wproj),
        (
            pltpu.VMEM((pad, width), F32),
            pltpu.VMEM((LANES, keys), F32),
            pltpu.VMEM((pad, keys), jnp.int32),
            pltpu.VMEM((heads // 2, 8, entries), jnp.int32),
            pltpu.VMEM((heads, pad, keys), F32),
            pltpu.VMEM(wqkv.shape, BF16),
            pltpu.VMEM(wproj.shape, BF16),
            pltpu.VMEM((2, pad, width), BF16),
            pltpu.SemaphoreType.DMA((2,)),
        ),
            )


def mlp_body(
    first, inner_ref, b1a_ref, b1b_ref, w1a_ref, w1b_ref, w2a_ref, w2b_ref, bias_ref, *rest
):
    if first:
        grads, masks, gamma2_ref = rest[0:2], rest[2:4], rest[4]
        rest = rest[5:]
        dbranches, rest = rest[0:2], rest[2:]
        cot_out, rest = rest[0], rest[1:]
        pad_s, wide_s = rest[-2:]
        rest = rest[:-2]
        pad = inner_ref.shape[0]
        for grad_ref, mask_ref, out_ref in zip(grads, masks, dbranches):
            column = mask_column(mask_ref, wide_s, pad)[:, 0:1]
            cotangent = load_padded(grad_ref, pad_s) * column
            out_ref[...] = (row_of(gamma2_ref) * cotangent).astype(BF16)
            if out_ref is dbranches[0]:
                own_cotangent = cotangent
            else:
                cot_out[...] = cotangent
        dbranch = dbranches[0][...]
        cotangent = own_cotangent
    else:
        dbranch, rest = rest[0][...], rest[1:]
    acta_ref, actb_ref, dprea_ref, dpreb_ref, dinner_ref, sums_ref, *more = rest
    if first:
        branch_ref = more[0]
    inner = inner_ref[...]
    branch = None
    dinner = None
    for at, (w1, w2, b1, act_out, dpre_out) in enumerate((
        (w1a_ref, w2a_ref, b1a_ref, acta_ref, dprea_ref),
        (w1b_ref, w2b_ref, b1b_ref, actb_ref, dpreb_ref),
    )):
        pre = dot_nn(inner, w1[...]) + row_of(b1).astype(F32)
        phi = 0.5 + 0.5 * lax.erf(pre * (0.5**0.5))
        act = (pre * phi).astype(BF16)
        act_out[...] = act
        slope = phi + pre * (jnp.exp(-0.5 * pre * pre) * 0.3989422804014327)
        dact = dot_nt(dbranch, w2[...])
        dpre = (dact * slope).astype(BF16)
        dpre_out[...] = dpre
        sums_ref[at : at + 1, :] = jnp.sum(dpre.astype(F32), axis=0, keepdims=True)
        this_dinner = dot_nt(dpre, w1[...])
        dinner = this_dinner if dinner is None else dinner + this_dinner
        if first:
            this_branch = dot_nn(act, w2[...])
            branch = this_branch if branch is None else branch + this_branch
    dinner_ref[...] = dinner.astype(dinner_ref.dtype)
    if first:
        branch = branch + row_of(bias_ref)
        branch_ref[...] = branch
        sums_ref[2:3, :] = jnp.sum(cotangent * branch, axis=0, keepdims=True)
        sums_ref[3:4, :] = jnp.sum(dbranch.astype(F32), axis=0, keepdims=True)
    else:
        sums_ref[2:4, :] = jnp.zeros_like(sums_ref[2:4, :])
    sums_ref[4:8, :] = jnp.zeros_like(sums_ref[4:8, :])


def mlp(inner, weights, bias, given, first, deps=(), carry=(), hold=()):
    pad, width = inner.shape
    ff = weights[2].shape[1]
    kind = F32 if first else BF16
    outs = (
        (shape((pad, ff), BF16),) * 4
        + (shape((pad, width), kind), shape((8, ff), F32))
    )
    scratch = ()
    if first:
        outs = (shape((pad, width), BF16),) * 2 + (shape((pad, width), F32),) + outs
        outs += (shape_out((pad, width), F32),)
        scratch = (pltpu.VMEM((pad, width), F32), pltpu.VMEM((LANES, round_up(pad, LANES)), F32))
    return call(
        functools.partial(mlp_body, first), outs, "vhhvvvvh" + ("hvhvh" if first else "v"),
        (inner, *weights, bias, *given), scratch, cost=COST["mlp"], deps=deps, carry=carry, hold=hold,
    )


def far_branch_body(acta_ref, actb_ref, w2a_ref, w2b_ref, cot_ref, branch_ref, sums_ref):
    branch = dot_nn(acta_ref[...], w2a_ref[...]) + dot_nn(actb_ref[...], w2b_ref[...])
    branch_ref[...] = branch.astype(BF16)
    sums_ref[...] = jnp.zeros_like(sums_ref)
    sums_ref[2:3, :] = jnp.sum(cot_ref[...] * branch, axis=0, keepdims=True)


def far_branch(acta, actb, w2a, w2b, cotangent, deps=(), hold=()):
    pad, width = cotangent.shape
    return call(
        far_branch_body, (shape_out((pad, width), BF16), shape((8, width), F32)), "vvvvv",
        (acta, actb, w2a, w2b, cotangent), cost=COST["far"], deps=deps, hold=hold,
    )


def split_rows(out_send, out_keep, total, low, block):
    for step in range(total.shape[0] // (2 * block)):
        even = total[2 * step * block : (2 * step + 1) * block]
        odd = total[(2 * step + 1) * block : (2 * step + 2) * block]
        out_send[step] = jnp.where(low, even, odd).astype(BF16)
        out_keep[step] = jnp.where(low, odd, even).astype(BF16)


def pair_grad_body(*refs):
    out_ref = refs[-1]
    for at in range(2):
        left0, left1, right0, right1 = refs[4 * at : 4 * at + 4]
        total = dot_tn(left0[...], right0[...]) + dot_tn(left1[...], right1[...])
        out_ref[at] = total.astype(BF16)


def pair_grad(one, two, deps=(), carry=(), hold=()):
    width, ff = one[0].shape[1], one[2].shape[1]
    return call(
        pair_grad_body, shape((2, width, ff), BF16), "v" * 8, (*one, *two), cost=COST["pair"], deps=deps,
        carry=carry, hold=hold,
    )


def fc_keep_body(block, where_ref, *refs):
    other, send_ref, keep_ref = refs[8:]
    for at in range(2):
        left0, left1, right0, right1 = refs[4 * at : 4 * at + 4]
        total = dot_tn(left0[...], right0[...]) + dot_tn(left1[...], right1[...])
        split_rows(
            send_ref.at[at], keep_ref.at[at], total + other[at].astype(F32), where_ref[2] > 0,
            block,
        )


def fc_keep(where, block, one, two, other, deps=(), carry=(), hold=()):
    width, ff = one[0].shape[1], one[2].shape[1]
    outs = (shape((2, width // (2 * block), block, ff), BF16),) * 2
    return call(
        functools.partial(fc_keep_body, block), outs, "s" + "v" * 9, (where, *one, *two, other),
        cost=COST["keep"], deps=deps, carry=carry, hold=hold,
    )


def deal_out(where_ref, outs, dqkv_ref, datt):
    third = dqkv_ref.shape[1] // 3
    for step, out_ref in enumerate(outs):
        part = datt
        for place in range(3):
            columns = dqkv_ref[:, place * third : (place + 1) * third]
            part = jnp.where(place_is(where_ref, step, place), columns, part)
        out_ref[...] = part


def heads_back(pairs, first_pair, head_size, q_ref, k_ref, v_ref, probs_ref, dmixed_ref, dqkv_ref,
               dscores_ref):
    pad = q_ref.shape[0]
    third = dqkv_ref.shape[1] // 3
    lane = lax.broadcasted_iota(jnp.int32, (1, LANES), 1)
    first = lane < head_size
    scale = head_size ** (-0.5)

    def pair_step(step, carry):
        at = pl.ds(pl.multiple_of((first_pair + step) * LANES, LANES), LANES)
        query = q_ref[:, at]
        key = k_ref[:, at]
        value = v_ref[:, at]
        dmixed = dmixed_ref[:, at]
        dq, dk, dv = [], [], []
        for side in range(2):
            own = first if side == 0 else jnp.logical_not(first)
            probs_b = probs_ref[2 * (first_pair + step) + side]
            probs = probs_b.astype(F32)
            dprobs = dot_nt(jnp.where(own, dmixed, jnp.zeros_like(dmixed)), value)
            inside = jnp.sum(probs * dprobs, axis=-1, keepdims=True)
            dscores = (probs * (dprobs - inside)).astype(BF16)
            dscores_ref[2 * step + side] = dscores
            dq.append(dot_nn(dscores, key))
            dk.append(dot_tn(dscores, query))
            dv.append(dot_tn(probs_b, dmixed))
        out = pl.multiple_of(step * LANES, LANES)
        dqkv_ref[:, pl.ds(out, LANES)] = (jnp.where(first, dq[0], dq[1]) * scale).astype(BF16)
        dqkv_ref[:, pl.ds(pl.multiple_of(out + third, LANES), LANES)] = (
            jnp.where(first, dk[0], dk[1])[:pad].astype(BF16)
        )
        dqkv_ref[:, pl.ds(pl.multiple_of(out + 2 * third, LANES), LANES)] = (
            jnp.where(first, dv[0], dv[1])[:pad].astype(BF16)
        )
        return carry

    lax.fori_loop(0, pairs, pair_step, 0, unroll=pairs)


def column_sums(out_ref, at, dqkv_ref):
    third = dqkv_ref.shape[1] // 3
    for row, part in ((4, 0), (5, 2)):
        lanes = slice(part * third, (part + 1) * third)
        out_ref[row : row + 1, at * third : (at + 1) * third] = jnp.sum(
            dqkv_ref[:, lanes].astype(F32), axis=0, keepdims=True
        )


def backward_body(
    heads,
    where_ref,
    dinner0_ref,
    dinner1_ref,
    hidden_ref,
    attended_ref,
    outgrad_ref,
    mask_ref,
    gain2_ref,
    gamma1_ref,
    wproj_ref,
    q_ref,
    k_ref,
    v_ref,
    probs_ref,
    dhidden_ref,
    dqkv_ref,
    out0_ref,
    out1_ref,
    out2_ref,
    out3_ref,
    dscores_ref,
    sums_ref,
    pad_s,
    dmixed_ref,
):
    width = hidden_ref.shape[1]
    cotangent = load_padded(outgrad_ref, pad_s) * mask_ref[:, 0:1]
    xhat, root = norm_stats(hidden_ref[...])
    dinner = dinner0_ref[...].astype(F32) + dinner1_ref[...].astype(F32)
    dhidden = cotangent + norm_back(dinner, xhat, root, row_of(gain2_ref))
    dhidden_ref[...] = dhidden
    datt = (row_of(gamma1_ref) * dhidden).astype(BF16)
    dmixed_ref[...] = dot_nt(datt, wproj_ref[...]).astype(BF16)
    sums_ref[0:1, :] = jnp.sum(dinner * xhat, axis=0, keepdims=True)
    sums_ref[1:2, :] = jnp.sum(dinner, axis=0, keepdims=True)
    sums_ref[2:3, :] = jnp.sum(dhidden * attended_ref[...], axis=0, keepdims=True)
    sums_ref[3:4, :] = jnp.sum(datt.astype(F32), axis=0, keepdims=True)
    sums_ref[4:8, :] = jnp.zeros((4, width), F32)
    heads_back(heads // 2, 0, width // heads, q_ref, k_ref, v_ref, probs_ref, dmixed_ref, dqkv_ref,
               dscores_ref)
    deal_out(
        where_ref, (out0_ref, out1_ref, out2_ref, out3_ref), dqkv_ref, datt
    )
    column_sums(sums_ref, 0, dqkv_ref)


def backward(heads, where, dinner0, dinner1, hidden, attended, out_grad, mask_col, gain2, gamma1,
             wproj, q, k, v, probs, deps=()):
    pad, width = hidden.shape
    keys = k.shape[0]
    outs = (
        shape((pad, width), F32),
        shape((pad, 3 * width), BF16),
        shape((pad, width), BF16),
        shape((pad, width), BF16),
        shape((pad, width), BF16),
        shape((pad, width), BF16),
        shape((heads, pad, keys), BF16),
        shape((8, width), F32),
    )
    return call(
        functools.partial(backward_body, heads),
        outs,
        "svvhvhhhhhhvvv",
        (where, dinner0, dinner1, hidden, attended, out_grad, mask_col, gain2, gamma1, wproj, q, k,
         v, probs),
        (pltpu.VMEM((pad, width), F32), pltpu.VMEM((pad, width), BF16)),
        cost=COST["back"],
        deps=deps,
    )


def first_norm_body(
    patches_ref, mask_ref, token_ref, gain1_ref, dqkv_ref, wqkv_ref, dhidden_ref,
    patchgrad_ref, sums_ref, pad_s,
):
    rows, width = patches_ref.shape[1:]
    picked = mask_ref[:, 0:1] > 0
    start = jnp.where(picked, row_of(token_ref), load_padded(patches_ref, pad_s))
    xhat, root = norm_stats(start)
    dnormed = dot_nt(dqkv_ref[...], wqkv_ref[...])
    dstart = dhidden_ref[...] + norm_back(dnormed, xhat, root, row_of(gain1_ref))
    patchgrad_ref[0] = jnp.where(picked, 0.0, dstart)[0:rows]
    sums_ref[0:1, :] = jnp.sum(jnp.where(picked, dstart, 0.0), axis=0, keepdims=True)
    sums_ref[1:2, :] = jnp.sum(dnormed * xhat, axis=0, keepdims=True)
    sums_ref[2:3, :] = jnp.sum(dnormed, axis=0, keepdims=True)
    sums_ref[3:8, :] = jnp.zeros((5, width), F32)


def first_norm(patches, mask_col, token, gain1, dqkv, wqkv, dhidden, deps=(), carry=()):
    rows, width = patches.shape[1:]
    pad = mask_col.shape[0]
    outs = (shape_out((1, rows, width), F32), shape((8, width), F32))
    return call(
        first_norm_body, outs, "hhhhvhv",
        (patches, mask_col, token, gain1, dqkv, wqkv, dhidden),
        (pltpu.VMEM((pad, width), F32),), cost=COST["norm"], deps=deps, carry=carry,
    )


def layer_end_body(hidden_ref, branch0_ref, branch1_ref, gamma2_ref, out_ref):
    branch = branch0_ref[...] + branch1_ref[...].astype(F32)
    layer = hidden_ref[...] + row_of(gamma2_ref) * branch
    out_ref[0] = layer[0 : out_ref.shape[1]].astype(BF16)


def layer_end(rows, hidden, branch0, branch1, gamma2, deps=(), carry=()):
    return call(
        layer_end_body, shape_out((1, rows, hidden.shape[1]), BF16), "hhvh",
        (hidden, branch0, branch1, gamma2), cost=COST["end"], deps=deps, carry=carry,
    )


def table_grad_body(
    where_ref, index_ref, ds_ref, sums_b_ref, sums_n_ref, sums0_ref, sums1_ref, sums_f_ref, out_ref,
    index_s,
    total_s,
):
    rows = index_ref.shape[0]
    pad, head_pad, keys = ds_ref.shape
    high_count = total_s.shape[0] // head_pad
    index_s[...] = jnp.zeros_like(index_s)
    index_s[0:rows, 0:rows] = index_ref[...]
    total_s[...] = jnp.zeros_like(total_s)
    below = lax.broadcasted_iota(jnp.int32, (LANES, keys), 0).astype(BF16)
    ones = jnp.ones((LANES, keys), BF16)
    group = 16

    def step(at, carry):
        base = pl.multiple_of(at * group, group)
        lines = index_s[pl.ds(base, group), :]
        low = (lines & (LANES - 1)).astype(F32).astype(BF16)
        high = (lines >> 7).astype(F32).astype(BF16)
        total = None
        for i in range(group):
            onehot = jnp.where(below == low[i : i + 1], ones, jnp.zeros_like(ones))
            ds = ds_ref[base + i]
            left = jnp.concatenate(
                [
                    jnp.where(high[i : i + 1] == jnp.asarray(part, BF16), ds, jnp.zeros_like(ds))
                    for part in range(high_count)
                ],
                axis=0,
            )
            one = dot_nt(left, onehot)
            total = one if total is None else total + one
        total_s[...] += total
        return carry

    lax.fori_loop(0, pad // group, step, 0, unroll=2)
    for part in range(high_count):
        out_ref[0:head_pad, part * LANES : (part + 1) * LANES] = total_s[
            part * head_pad : (part + 1) * head_pad
        ]
    sums = sums0_ref[...] + sums1_ref[...] + sums_f_ref[...]
    out_ref[head_pad : head_pad + 6, :] = sums_b_ref[0:6, :]
    out_ref[head_pad + 6 : head_pad + 8, :] = sums[2:4]
    out_ref[head_pad + 8 : head_pad + 11, :] = sums_n_ref[0:3, :]
    for part in range(4):
        mine = jnp.where(where_ref[0] == part // 2, 1.0, 0.0)
        own = jnp.where(where_ref[1] == part % 2, sums[0:1], sums[1:2])
        out_ref[head_pad + 11 + part : head_pad + 12 + part, :] = mine * own
    out_ref[head_pad + 15 :, :] = jnp.zeros_like(out_ref[head_pad + 15 :, :])


def table_grad(where, rel_index, dscores, sums_b, sums_n, sums0, sums1, sums_f, entries, deps=()):
    pad, head_pad, keys = dscores.shape
    high_count = round_up(entries, LANES) // LANES
    width = sums_b.shape[1]
    return call(
        table_grad_body, shape((head_pad + 16, width), F32), "shvvvvvv",
        (where, rel_index, dscores, sums_b, sums_n, sums0, sums1, sums_f),
        (pltpu.VMEM((pad, keys), jnp.int32), pltpu.VMEM((high_count * head_pad, LANES), F32)),
        cost=COST["table"], deps=deps,
    )


def late_grad_body(block, piece, where_ref, *refs):
    lefts, rights, send_ref, keep_ref = refs[:4], refs[4:8], refs[8], refs[9]
    total = None
    for step in range(4):
        half = rights[step].shape[1] // 2
        one = dot_tn(lefts[step][...], rights[step][:, piece * half : (piece + 1) * half])
        total = one if total is None else total + one
    split_rows(send_ref.at[0], keep_ref.at[0], total, where_ref[2] > 0, block)


def late_grad(where, block, piece, lefts, rights, deps=(), carry=()):
    width = lefts[0].shape[1]
    half = rights[0].shape[1] // 2
    outs = (shape((1, width // (2 * block), block, half), BF16),) * 2
    return call(
        functools.partial(late_grad_body, block, piece), outs, "shvvvvvvv",
        (where, *lefts, *rights), cost=COST["late"], deps=deps, carry=carry,
    )


def fold_body(bit, where_ref, keep_ref, met_ref, send_out, keep_out):
    low = where_ref[2 + bit] > 0
    for at in range(send_out.shape[0]):
        for step in range(send_out.shape[1]):
            even, odd = (
                keep_ref[at, 2 * step + side].astype(F32) + met_ref[at, 2 * step + side].astype(F32)
                for side in range(2)
            )
            send_out[at, step] = jnp.where(low, even, odd).astype(BF16)
            keep_out[at, step] = jnp.where(low, odd, even).astype(BF16)


def fold(where, bit, keep, met, deps=(), carry=()):
    items, count, block, width = keep.shape
    return call(
        functools.partial(fold_body, bit), (shape((items, count // 2, block, width), BF16),) * 2,
        "svv", (where, keep, met), cost=COST["fold"], deps=deps, carry=carry,
    )


def last_sum_body(keep_ref, met_ref, *outs):
    for at, out_ref in enumerate(outs):
        total = keep_ref[at, 0].astype(F32) + met_ref[at, 0].astype(F32)
        out_ref[...] = total.astype(out_ref.dtype)


def last_sum(keep, met, kind, deps=(), carry=()):
    make = shape_out if kind == F32 else shape
    return call(
        last_sum_body, (make(keep.shape[2:], kind),) * keep.shape[0], "vv", (keep, met), cost=COST["last"],
        deps=deps, carry=carry,
    )


def join_body(before_ref, keep_ref, met_ref, out_ref):
    half = before_ref.shape[1]
    out_ref[:, :half] = before_ref[...]
    out_ref[:, half:] = (keep_ref[0, 0].astype(F32) + met_ref[0, 0].astype(F32)).astype(BF16)


def join(before, keep, met, deps=(), carry=()):
    block, half = before.shape
    return call(
        join_body, shape((block, 2 * half), BF16), "vvv", (before, keep, met), cost=COST["join"], deps=deps,
        carry=carry,
    )


def assemble_body(where_ref, own_ref, over_x_ref, over_core_ref, qkv_ref, proj_ref):
    width = own_ref.shape[1]
    high = where_ref[0] > 0
    core = where_ref[1] > 0
    own, far = own_ref[...], over_x_ref[...]
    side, corner = over_core_ref[0], over_core_ref[1]
    here = (jnp.where(core, side, own), jnp.where(core, own, side))
    there = (jnp.where(core, corner, far), jnp.where(core, far, corner))
    for at in range(2):
        qkv_ref[:, at * width : (at + 1) * width] = jnp.where(high, there[at], here[at]).astype(F32)
    qkv_ref[:, 2 * width :] = jnp.where(high, here[0], there[0]).astype(F32)
    proj_ref[...] = jnp.where(high, here[1], there[1]).astype(F32)


def assemble(where, own, far, pair, deps=()):
    block, width = own.shape
    return call(
        assemble_body, (shape_out((block, 3 * width), F32), shape_out((block, width), F32)),
        "svvv", (where, own, far, pair), deps=deps,
    )


def on_device(
    dp,
    patches,
    row_mask,
    out_grad,
    rel_index,
    mask_token,
    ln1_gain,
    ln1_bias,
    qkv_weight,
    query_bias,
    value_bias,
    rel_table,
    proj_weight,
    proj_bias,
    gamma1,
    ln2_gain,
    ln2_bias,
    fc1_weight,
    fc1_bias,
    fc2_weight,
    fc2_bias,
    gamma2,
):
    rows, width = patches.shape[1:]
    entries, heads = rel_table.shape
    pad = round_up(rows, 16)
    mp_at = lax.axis_index("mp")
    dp_at = lax.axis_index("dp")
    x_at, core_at = mp_at // 2, mp_at % 2
    bits = dp.bit_length() - 1
    where = jnp.stack(
        [x_at, core_at] + [(dp_at >> bit) & 1 for bit in range(bits)]
    ).astype(jnp.int32)

    def swap(axis, bit):
        count = 4 if axis == "mp" else dp
        pairs = [(at, at ^ bit) for at in range(count)]
        return lambda value: lax.ppermute(value, axis, pairs)

    over_core, over_x = swap("mp", 1), swap("mp", 2)
    over_bit = [swap("dp", 1 << bit) for bit in range(bits)]

    out_grad1, row_mask1 = over_x(out_grad), over_x(row_mask)
    b1b, w1b, w2b = over_core(fc1_bias), over_core(fc1_weight), over_core(fc2_weight)

    before = []

    def step(kernel, *args, deps=(), **more):
        out, token = kernel(*args, deps=tuple(before) + tuple(deps), **more)
        before[:] = [token]
        return out

    mask_col, left0, left1, left2, left3, q, k, v, probs, attended, hidden, inner = step(
        forward, heads, pad, where, patches, row_mask, rel_index, mask_token, ln1_gain, ln1_bias,
        query_bias, value_bias, rel_table.T, proj_bias, gamma1, ln2_gain, ln2_bias, qkv_weight,
        proj_weight,
    )
    held = [k, v, probs, attended]

    def holding(kernel, *args, **more):
        out = step(kernel, *args, hold=tuple(held), **more)
        count = len(held)
        held[:] = out[-count:]
        out = tuple(out[:-count])
        return out if len(out) > 1 else out[0]

    inner1 = over_x(inner)
    weights = (fc1_bias, b1b, fc1_weight, w1b, fc2_weight, w2b)
    dbranch, dbranch1, cot1, acta0, actb0, dprea0, dpreb0, dinner0, sums0, branch0, left1 = holding(
        mlp, inner, weights, fc2_bias, (out_grad, out_grad1, row_mask, row_mask1, gamma2), True,
        carry=(left1,),
    )
    met_left1 = over_core(left1)
    acta1, actb1, dprea1, dpreb1, dinner1, sums1 = holding(
        mlp, inner1, weights, fc2_bias, (dbranch1,), False
    )
    dinner_in = over_x(dinner1)

    block = width // dp

    def middle(keep, met, first, last):
        for bit in range(first, last):
            send, keep = step(fold, where, bit, keep, met)
            met = over_bit[bit](send)
        return keep, met

    fc_other = over_core(
        holding(pair_grad, (inner, inner1, dpreb0, dpreb1), (dbranch, dbranch1, actb0, actb1))
    )
    branch1, sums_f = holding(far_branch, acta1, actb1, fc2_weight, w2b, cot1)
    fc_send, fc_kept, left2, left3 = holding(
        fc_keep, where, block, (inner, inner1, dprea0, dprea1), (dbranch, dbranch1, acta0, acta1),
        fc_other, deps=(met_left1,), carry=(left2, left3),
    )
    fc_met = over_bit[0](fc_send)
    met_left2, met_left3 = over_x(left2), swap("mp", 3)(left3)
    k, v, probs, attended = held

    dhidden, dqkv, own, core, far, corner, dscores, sums_b = step(
        backward, heads, where, dinner0, dinner_in, hidden, attended, out_grad, mask_col, ln2_gain,
        gamma1, proj_weight, q, k, v, probs,
    )
    met_far, met_corner, met_core = over_x(far), swap("mp", 3)(corner), over_core(core)
    head_pad = 16
    late = ((left0, met_left1, met_left2, met_left3), (own, met_core, met_far, met_corner))
    keep, met, made = {"f": fc_kept}, {"f": fc_met}, {}
    state = {"small": None, "branch": branch1, "own": None}

    def tailed(mark, kernel, *args, **more):
        names = [name for sign, name in (("@", "small"), ("%", "branch"), ("!", "own")) if sign in mark]
        carried = tuple(state[name] for name in names)
        out = step(kernel, *args, carry=carried, **more)
        if not names:
            return out
        state.update(zip(names, out[-len(names) :]))
        out = tuple(out[: -len(names)])
        return out if len(out) > 1 else out[0]

    def spread_on(name, mark, first, last):
        for bit in range(first, last):
            send, keep[name] = tailed(mark if bit == first else "", fold, where, bit, keep[name], met[name])
            met[name] = over_bit[bit](send)

    def hop(swaps):
        for swapped in swaps:
            state["small"] = state["small"] + swapped(state["small"])

    for item in ORDER:
        name, mark = item.rstrip("@%!"), item[len(item.rstrip("@%!")) :]
        if name == "N":
            made["patch"], made["sums"] = tailed(
                mark, first_norm, patches, mask_col, mask_token, ln1_gain, dqkv, qkv_weight, dhidden,
                deps=(met_left2, met_left3),
            )
        elif name == "T":
            ds = jnp.pad(
                jnp.transpose(dscores, (1, 0, 2)), ((0, 0), (0, head_pad - heads), (0, 0))
            )
            state["small"] = step(
                table_grad, where, rel_index, ds, sums_b, made["sums"], sums0, sums1, sums_f, entries
            )
            hop([over_core])
        elif name in ("A", "B"):
            send, keep[name] = tailed(mark, late_grad, where, block, "AB".index(name), *late)
            met[name] = over_bit[0](send)
        elif name in ("f1", "a1", "b1"):
            spread_on(name[0].upper() if name[0] != "f" else "f", mark, 1, 2)
        elif name in ("f2", "a2", "b2"):
            spread_on(name[0].upper() if name[0] != "f" else "f", mark, 2, bits)
        elif name == "x":
            hop([over_x])
        elif name == "y":
            hop([over_bit[0]])
        elif name == "z":
            hop([over_bit[1]])
        elif name == "w":
            hop(over_bit[2:])
        elif name == "h":
            made["branch"] = over_x(state["branch"])
        elif name == "E":
            made["layer"] = tailed(mark, layer_end, rows, hidden, branch0, made["branch"], gamma2)
        elif name == "F":
            made["fc"] = tailed(mark, last_sum, keep["f"], met["f"], F32)
        elif name == "S":
            made["A"] = tailed(mark, last_sum, keep["A"], met["A"], BF16)
        elif name == "J":
            state["own"] = tailed(mark, join, made["A"], keep["B"], met["B"])
            late_x = over_x(state["own"])
    small, late_own = state["small"], state["own"]
    patch_grad, layer_out = made["patch"], made["layer"]
    fc1_weight_grad, fc2_weight_grad = made["fc"]
    late_pair = over_core(jnp.stack([late_own, late_x]))
    qkv_weight_grad, proj_weight_grad = step(assemble, where, late_own, late_x, late_pair)

    rel_grad = small[:heads, :entries].T
    (ln2_gain_grad, ln2_bias_grad, gamma1_grad, proj_bias_grad, query_bias_grad, value_bias_grad,
     gamma2_grad, fc2_bias_grad, mask_token_grad, ln1_gain_grad, ln1_bias_grad) = [
        small[head_pad + at] for at in range(11)
    ]
    fc1_bias_grad = lax.dynamic_index_in_dim(small, head_pad + 11 + mp_at, 0, False)
    return (
        layer_out,
        patch_grad,
        mask_token_grad,
        ln1_gain_grad,
        ln1_bias_grad,
        qkv_weight_grad,
        query_bias_grad,
        value_bias_grad,
        rel_grad,
        proj_weight_grad,
        proj_bias_grad,
        gamma1_grad,
        ln2_gain_grad,
        ln2_bias_grad,
        fc1_weight_grad,
        fc1_bias_grad,
        fc2_weight_grad.T,
        fc2_bias_grad,
        gamma2_grad,
    )


def solution(mesh):
    rows3 = P(("dp", "mp"), None, None)
    placed = (
        (rows3, P(("dp", "mp"), None), rows3)
        + (P(),) * 13
        + (P(None, "mp"), P("mp"), P("mp", None), P(), P())
    )
    return jax.shard_map(
        functools.partial(on_device, mesh.shape["dp"]),
        mesh=mesh,
        in_specs=placed,
        out_specs=(
            rows3,
            rows3,
            P(),
            P(),
            P(),
            P("dp", None),
            P(),
            P(),
            P(),
            P("dp", None),
            P(),
            P(),
            P(),
            P(),
            P("dp", "mp"),
            P("mp"),
            P("mp", "dp"),
            P(),
            P(),
        ),
        check_vma=False,
    )
```

```python
import functools

import jax
import jax.numpy as jnp
from jax import lax
from jax.experimental import pallas as pl
from jax.experimental.pallas import tpu as pltpu
from jax.sharding import PartitionSpec as P

F32 = jnp.float32
BF16 = jnp.bfloat16
EPS = 1e-06
LANES = 128
SCALE = 1
COST = dict(fwd=1, mlp=5, far=30, pair=0.42, keep=0.6, back=5, norm=5, table=3.2, late=1.2, fold=0.4, last=0.4, end=0.2, join=1)
ORDER = (
    "N", "T", "f1", "A", "B", "a1", "x", "f2@%", "h", "y", "b1", "a2@", "z", "b2", "E@", "w", "S", "F", "J",
)
UNROLL_F = 6
UNROLL_B = 6
VMEM_LIMIT = 16 * 1024 * 1024


def round_up(value, step):
    return -(-value // step) * step


def dot_nn(left, right):
    return lax.dot_general(left, right, (((1,), (0,)), ((), ())), preferred_element_type=F32)


def dot_nt(left, right):
    return lax.dot_general(left, right, (((1,), (1,)), ((), ())), preferred_element_type=F32)


def dot_tn(left, right):
    return lax.dot_general(left, right, (((0,), (0,)), ((), ())), preferred_element_type=F32)


def row_of(ref):
    return ref[...].reshape(1, ref.shape[0])


def norm_stats(values):
    middle = jnp.mean(values, axis=-1, keepdims=True)
    centred = values - middle
    spread = jnp.mean(centred * centred, axis=-1, keepdims=True)
    root = lax.rsqrt(spread + EPS)
    return centred * root, root


def norm_back(d_out, xhat, root, gain):
    t = d_out * gain
    mean_t = jnp.mean(t, axis=-1, keepdims=True)
    mean_tx = jnp.mean(t * xhat, axis=-1, keepdims=True)
    return root * (t - mean_t - xhat * mean_tx)


SPACES = {
    "h": (pltpu.HBM, pltpu.VMEM),
    "v": (None, pltpu.VMEM),
    "s": (None, pltpu.SMEM),
    "a": (pltpu.HBM, pl.ANY),
}


def call(body, outs, kinds, values, scratch=(), cost=1, deps=(), carry=(), hold=()):
    specs, given = [], []
    for kind, value in zip(kinds, values, strict=True):
        keep, space = SPACES[kind]
        specs.append(pl.BlockSpec(memory_space=space))
        given.append(value if keep is None else pltpu.with_memory_space_constraint(value, keep))
    outs = outs if isinstance(outs, tuple) else (outs,)
    passed = tuple(carry) + tuple(hold)
    n_in, n_more, n_out = len(given), len(deps) + len(passed), len(outs)

    def inner(*refs):
        rest = refs[n_in + n_more :]
        rest[n_out][...] = jnp.zeros_like(rest[n_out])
        body(*refs[:n_in], *rest[:n_out], *rest[n_out + 1 + len(passed) :])

    anywhere = pl.BlockSpec(memory_space=pl.ANY)
    whole = pl.BlockSpec(memory_space=pltpu.VMEM)
    in_hbm = [value.dtype == BF16 and len(value.shape) == 2 for value in carry]
    held = tuple(pltpu.with_memory_space_constraint(value, pltpu.VMEM) for value in hold)
    out = pl.pallas_call(
        inner,
        name=getattr(body, "func", body).__name__,
        out_shape=outs
        + (pltpu.VMEM((8, LANES), F32),)
        + tuple(
            (pltpu.HBM if pinned else jax.ShapeDtypeStruct)(c.shape, c.dtype)
            for pinned, c in zip(in_hbm, carry)
        )
        + tuple(pltpu.VMEM(value.shape, value.dtype) for value in hold),
        in_specs=specs + [anywhere] * n_more,
        out_specs=(whole,) * (n_out + 1) + (anywhere,) * len(passed),
        input_output_aliases={n_in + len(deps) + at: n_out + 1 + at for at in range(len(passed))},
        scratch_shapes=list(scratch),
        compiler_params=pltpu.CompilerParams(vmem_limit_bytes=VMEM_LIMIT),
        cost_estimate=pl.CostEstimate(
            flops=int(cost * SCALE * 10**9), bytes_accessed=1000, transcendentals=0
        ),
    )(
        *given,
        *deps,
        *(
            pltpu.with_memory_space_constraint(c, pltpu.HBM) if pinned else c
            for pinned, c in zip(in_hbm, carry)
        ),
        *held,
    )
    results = out[:n_out] + out[n_out + 1 :]
    return (results if len(results) > 1 else results[0]), out[n_out]


def shape(dims, kind):
    return pltpu.VMEM(dims, kind)


def shape_out(dims, kind):
    return pltpu.HBM(dims, kind)


def load_padded(source_ref, pad_ref):
    rows = source_ref.shape[1]
    tail = (rows // 8) * 8
    pad_ref[tail:, :] = jnp.zeros_like(pad_ref[tail:, :])
    pad_ref[0:rows, :] = source_ref[0].astype(F32)
    return pad_ref[...]


def mask_column(mask_ref, wide_ref, pad):
    rows = mask_ref.shape[1]
    wide_ref[...] = jnp.zeros_like(wide_ref)
    line = jnp.where(mask_ref[...] > 0, 1.0, 0.0)
    wide_ref[:, 0:rows] = jnp.broadcast_to(line, (LANES, rows))
    return wide_ref[...].T[:pad]


def place_is(where_ref, step, place):
    high = where_ref[0] == (place >> 1) ^ (step >> 1)
    low = where_ref[1] == (place & 1) ^ (step & 1)
    return jnp.logical_and(high, low)


def forward_body(
    heads,
    where_ref,
    patches_ref,
    mask_ref,
    index_ref,
    token_ref,
    gain1_ref,
    bias1_ref,
    qbias_ref,
    vbias_ref,
    table_ref,
    pbias_ref,
    gamma1_ref,
    gain2_ref,
    bias2_ref,
    wqkv_hbm,
    wproj_hbm,
    mask_out,
    left0_ref,
    left1_ref,
    left2_ref,
    left3_ref,
    q_ref,
    k_ref,
    v_ref,
    probs_ref,
    attended_ref,
    hidden_ref,
    inner_ref,
    pad_s,
    wide_s,
    index_s,
    table_s,
    bias_s,
    wqkv_ref,
    wproj_ref,
    lefts_ref,
    sems,
):
    rows, width = patches_ref.shape[1:]
    pad = q_ref.shape[0]
    keys = k_ref.shape[0]
    head_size = width // heads
    copy_qkv = pltpu.make_async_copy(wqkv_hbm, wqkv_ref, sems.at[0])
    copy_qkv.start()
    copy_proj = pltpu.make_async_copy(wproj_hbm, wproj_ref, sems.at[1])
    copy_proj.start()

    index_s[...] = jnp.zeros_like(index_s)
    index_s[0:rows, 0:rows] = index_ref[...]
    entries = table_ref.shape[1]
    chunks = table_s.shape[2] // LANES
    top = jnp.max(jnp.abs(table_ref[...]))
    grow = 32767.0 / jnp.maximum(top, 1e-30)
    shrink = jnp.maximum(top, 1e-30) / 32767.0
    whole = jnp.round(table_ref[...] * grow).astype(jnp.int32)
    table_s[...] = jnp.zeros_like(table_s)
    for pair in range(heads // 2):
        both = whole[2 * pair : 2 * pair + 1] * 65536 + (whole[2 * pair + 1 : 2 * pair + 2] & 65535)
        table_s[pair, :, 0:entries] = jnp.broadcast_to(both, (8, entries))
    key_lane = lax.broadcasted_iota(jnp.int32, (1, LANES), 1)

    def gather_step(tile, carry):
        at_rows = pl.ds(pl.multiple_of(tile * 8, 8), 8)
        for half in range(keys // LANES):
            lanes = slice(half * LANES, (half + 1) * LANES)
            at = index_s[at_rows, lanes]
            low = at & (LANES - 1)
            high = at >> 7
            marks = [high == chunk for chunk in range(chunks)]
            real = key_lane + half * LANES < rows
            for pair in range(heads // 2):
                value = None
                for chunk in range(chunks):
                    line = table_s[pair, :, chunk * LANES : (chunk + 1) * LANES]
                    found = jnp.take_along_axis(line, low, axis=1, mode="promise_in_bounds")
                    value = found if value is None else jnp.where(marks[chunk], found, value)
                one = (value >> 16).astype(F32) * shrink
                two = ((value << 16) >> 16).astype(F32) * shrink
                if (half + 1) * LANES > rows:
                    one = jnp.where(real, one, -1e30)
                    two = jnp.where(real, two, -1e30)
                bias_s[2 * pair, at_rows, lanes] = one
                bias_s[2 * pair + 1, at_rows, lanes] = two
        return carry

    lax.fori_loop(0, pad // 8, gather_step, 0, unroll=2)

    column = mask_column(mask_ref, wide_s, pad)
    mask_out[...] = column
    picked = column[:, 0:1] > 0
    start = jnp.where(picked, row_of(token_ref), load_padded(patches_ref, pad_s))
    pad_s[...] = start
    xhat, _ = norm_stats(start)
    normed = (xhat * row_of(gain1_ref) + row_of(bias1_ref)).astype(BF16)
    lefts_ref[0] = normed
    copy_qkv.wait()
    scale = head_size ** (-0.5)
    q_ref[...] = ((dot_nn(normed, wqkv_ref[:, :width]) + row_of(qbias_ref)) * scale).astype(BF16)
    k_ref[0:pad, :] = dot_nn(normed, wqkv_ref[:, width : 2 * width]).astype(BF16)
    k_ref[pad:, :] = jnp.zeros_like(k_ref[pad:, :])
    v_ref[0:pad, :] = (dot_nn(normed, wqkv_ref[:, 2 * width :]) + row_of(vbias_ref)).astype(BF16)
    v_ref[pad:, :] = jnp.zeros_like(v_ref[pad:, :])

    lane = lax.broadcasted_iota(jnp.int32, (1, LANES), 1)
    first = lane < head_size

    def pair_step(pair, carry):
        at = pl.ds(pl.multiple_of(pair * LANES, LANES), LANES)
        query = q_ref[:, at]
        key = k_ref[:, at]
        value = v_ref[:, at]
        outs = []
        for side in range(2):
            head = pair * 2 + side
            own = first if side == 0 else jnp.logical_not(first)
            scores = dot_nt(jnp.where(own, query, jnp.zeros_like(query)), key) + bias_s[head]
            top = jnp.max(scores, axis=-1, keepdims=True)
            grown = jnp.exp(scores - top)
            probs = (grown * (1.0 / jnp.sum(grown, axis=-1, keepdims=True))).astype(BF16)
            probs_ref[head] = probs
            outs.append(dot_nn(probs, value))
        lefts_ref[1, :, at] = jnp.where(first, outs[0], outs[1]).astype(BF16)
        return carry

    lax.fori_loop(0, heads // 2, pair_step, 0, unroll=UNROLL_F)
    for at, out_ref in enumerate((left0_ref, left1_ref, left2_ref, left3_ref)):
        out_ref[...] = jnp.where(place_is(where_ref, at, 3), lefts_ref[1], lefts_ref[0])
    copy_proj.wait()
    attended = dot_nn(lefts_ref[1], wproj_ref[...]) + row_of(pbias_ref)
    attended_ref[...] = attended
    hidden = pad_s[...] + row_of(gamma1_ref) * attended
    hidden_ref[...] = hidden
    xhat2, _ = norm_stats(hidden)
    inner_ref[...] = (xhat2 * row_of(gain2_ref) + row_of(bias2_ref)).astype(BF16)


def forward(heads, pad, where, patches, row_mask, rel_index, token, gain1, bias1, qbias, vbias, table_t,
            pbias, gamma1, gain2, bias2, wqkv, wproj, deps=()):
    rows, width = patches.shape[1:]
    keys = round_up(pad, LANES)
    entries = round_up(table_t.shape[1], LANES)
    outs = (
        shape_out((pad, LANES), F32),
        shape_out((pad, width), BF16),
        shape_out((pad, width), BF16),
        shape_out((pad, width), BF16),
        shape_out((pad, width), BF16),
        shape_out((pad, width), BF16),
        shape((keys, width), BF16),
        shape((keys, width), BF16),
        shape((heads, pad, keys), BF16),
        shape((pad, width), F32),
        shape_out((pad, width), F32),
        shape((pad, width), BF16),
    )
    return call(
        functools.partial(forward_body, heads),
        outs,
        "shhhhhhhhhhhhhaa",
        (where, patches, row_mask, rel_index, token, gain1, bias1, qbias, vbias, table_t, pbias, gamma1,
         gain2, bias2, wqkv, wproj),
        (
            pltpu.VMEM((pad, width), F32),
            pltpu.VMEM((LANES, keys), F32),
            pltpu.VMEM((pad, keys), jnp.int32),
            pltpu.VMEM((heads // 2, 8, entries), jnp.int32),
            pltpu.VMEM((heads, pad, keys), F32),
            pltpu.VMEM(wqkv.shape, BF16),
            pltpu.VMEM(wproj.shape, BF16),
            pltpu.VMEM((2, pad, width), BF16),
            pltpu.SemaphoreType.DMA((2,)),
        ),
            )


def mlp_body(
    first, inner_ref, b1a_ref, b1b_ref, w1a_ref, w1b_ref, w2a_ref, w2b_ref, bias_ref, *rest
):
    if first:
        grads, masks, gamma2_ref = rest[0:2], rest[2:4], rest[4]
        rest = rest[5:]
        dbranches, rest = rest[0:2], rest[2:]
        cot_out, rest = rest[0], rest[1:]
        pad_s, wide_s = rest[-2:]
        rest = rest[:-2]
        pad = inner_ref.shape[0]
        for grad_ref, mask_ref, out_ref in zip(grads, masks, dbranches):
            column = mask_column(mask_ref, wide_s, pad)[:, 0:1]
            cotangent = load_padded(grad_ref, pad_s) * column
            out_ref[...] = (row_of(gamma2_ref) * cotangent).astype(BF16)
            if out_ref is dbranches[0]:
                own_cotangent = cotangent
            else:
                cot_out[...] = cotangent
        dbranch = dbranches[0][...]
        cotangent = own_cotangent
    else:
        dbranch, rest = rest[0][...], rest[1:]
    acta_ref, actb_ref, dprea_ref, dpreb_ref, dinner_ref, sums_ref, *more = rest
    if first:
        branch_ref = more[0]
    inner = inner_ref[...]
    branch = None
    dinner = None
    for at, (w1, w2, b1, act_out, dpre_out) in enumerate((
        (w1a_ref, w2a_ref, b1a_ref, acta_ref, dprea_ref),
        (w1b_ref, w2b_ref, b1b_ref, actb_ref, dpreb_ref),
    )):
        pre = dot_nn(inner, w1[...]) + row_of(b1).astype(F32)
        phi = 0.5 + 0.5 * lax.erf(pre * (0.5**0.5))
        act = (pre * phi).astype(BF16)
        act_out[...] = act
        slope = phi + pre * (jnp.exp(-0.5 * pre * pre) * 0.3989422804014327)
        dact = dot_nt(dbranch, w2[...])
        dpre = (dact * slope).astype(BF16)
        dpre_out[...] = dpre
        sums_ref[at : at + 1, :] = jnp.sum(dpre.astype(F32), axis=0, keepdims=True)
        this_dinner = dot_nt(dpre, w1[...])
        dinner = this_dinner if dinner is None else dinner + this_dinner
        if first:
            this_branch = dot_nn(act, w2[...])
            branch = this_branch if branch is None else branch + this_branch
    dinner_ref[...] = dinner.astype(dinner_ref.dtype)
    if first:
        branch = branch + row_of(bias_ref)
        branch_ref[...] = branch
        sums_ref[2:3, :] = jnp.sum(cotangent * branch, axis=0, keepdims=True)
        sums_ref[3:4, :] = jnp.sum(dbranch.astype(F32), axis=0, keepdims=True)
    else:
        sums_ref[2:4, :] = jnp.zeros_like(sums_ref[2:4, :])
    sums_ref[4:8, :] = jnp.zeros_like(sums_ref[4:8, :])


def mlp(inner, weights, bias, given, first, deps=(), carry=(), hold=()):
    pad, width = inner.shape
    ff = weights[2].shape[1]
    kind = F32 if first else BF16
    outs = (
        (shape((pad, ff), BF16),) * 4
        + (shape((pad, width), kind), shape((8, ff), F32))
    )
    scratch = ()
    if first:
        outs = (shape((pad, width), BF16),) * 2 + (shape((pad, width), F32),) + outs
        outs += (shape_out((pad, width), F32),)
        scratch = (pltpu.VMEM((pad, width), F32), pltpu.VMEM((LANES, round_up(pad, LANES)), F32))
    return call(
        functools.partial(mlp_body, first), outs, "vhhvvvvh" + ("hvhvh" if first else "v"),
        (inner, *weights, bias, *given), scratch, cost=COST["mlp"], deps=deps, carry=carry, hold=hold,
    )


def far_branch_body(acta_ref, actb_ref, w2a_ref, w2b_ref, cot_ref, branch_ref, sums_ref):
    branch = dot_nn(acta_ref[...], w2a_ref[...]) + dot_nn(actb_ref[...], w2b_ref[...])
    branch_ref[...] = branch.astype(BF16)
    sums_ref[...] = jnp.zeros_like(sums_ref)
    sums_ref[2:3, :] = jnp.sum(cot_ref[...] * branch, axis=0, keepdims=True)


def far_branch(acta, actb, w2a, w2b, cotangent, deps=(), hold=()):
    pad, width = cotangent.shape
    return call(
        far_branch_body, (shape_out((pad, width), BF16), shape((8, width), F32)), "vvvvv",
        (acta, actb, w2a, w2b, cotangent), cost=COST["far"], deps=deps, hold=hold,
    )


def split_rows(out_send, out_keep, total, low, block):
    for step in range(total.shape[0] // (2 * block)):
        even = total[2 * step * block : (2 * step + 1) * block]
        odd = total[(2 * step + 1) * block : (2 * step + 2) * block]
        out_send[step] = jnp.where(low, even, odd).astype(BF16)
        out_keep[step] = jnp.where(low, odd, even).astype(BF16)


def pair_grad_body(*refs):
    out_ref = refs[-1]
    for at in range(2):
        left0, left1, right0, right1 = refs[4 * at : 4 * at + 4]
        total = dot_tn(left0[...], right0[...]) + dot_tn(left1[...], right1[...])
        out_ref[at] = total.astype(BF16)


def pair_grad(one, two, deps=(), carry=(), hold=()):
    width, ff = one[0].shape[1], one[2].shape[1]
    return call(
        pair_grad_body, shape((2, width, ff), BF16), "v" * 8, (*one, *two), cost=COST["pair"], deps=deps,
        carry=carry, hold=hold,
    )


def fc_keep_body(block, where_ref, *refs):
    other, send_ref, keep_ref = refs[8:]
    for at in range(2):
        left0, left1, right0, right1 = refs[4 * at : 4 * at + 4]
        total = dot_tn(left0[...], right0[...]) + dot_tn(left1[...], right1[...])
        split_rows(
            send_ref.at[at], keep_ref.at[at], total + other[at].astype(F32), where_ref[2] > 0,
            block,
        )


def fc_keep(where, block, one, two, other, deps=(), carry=(), hold=()):
    width, ff = one[0].shape[1], one[2].shape[1]
    outs = (shape((2, width // (2 * block), block, ff), BF16),) * 2
    return call(
        functools.partial(fc_keep_body, block), outs, "s" + "v" * 9, (where, *one, *two, other),
        cost=COST["keep"], deps=deps, carry=carry, hold=hold,
    )


def deal_out(where_ref, outs, dqkv_ref, datt):
    third = dqkv_ref.shape[1] // 3
    for step, out_ref in enumerate(outs):
        part = datt
        for place in range(3):
            columns = dqkv_ref[:, place * third : (place + 1) * third]
            part = jnp.where(place_is(where_ref, step, place), columns, part)
        out_ref[...] = part


def heads_back(pairs, first_pair, head_size, q_ref, k_ref, v_ref, probs_ref, dmixed_ref, dqkv_ref,
               dscores_ref):
    pad = q_ref.shape[0]
    third = dqkv_ref.shape[1] // 3
    lane = lax.broadcasted_iota(jnp.int32, (1, LANES), 1)
    first = lane < head_size
    scale = head_size ** (-0.5)

    def pair_step(step, carry):
        at = pl.ds(pl.multiple_of((first_pair + step) * LANES, LANES), LANES)
        query = q_ref[:, at]
        key = k_ref[:, at]
        value = v_ref[:, at]
        dmixed = dmixed_ref[:, at]
        dq, dk, dv = [], [], []
        for side in range(2):
            own = first if side == 0 else jnp.logical_not(first)
            probs_b = probs_ref[2 * (first_pair + step) + side]
            probs = probs_b.astype(F32)
            dprobs = dot_nt(jnp.where(own, dmixed, jnp.zeros_like(dmixed)), value)
            inside = jnp.sum(probs * dprobs, axis=-1, keepdims=True)
            dscores = (probs * (dprobs - inside)).astype(BF16)
            dscores_ref[2 * step + side] = dscores
            dq.append(dot_nn(dscores, key))
            dk.append(dot_tn(dscores, query))
            dv.append(dot_tn(probs_b, dmixed))
        out = pl.multiple_of(step * LANES, LANES)
        dqkv_ref[:, pl.ds(out, LANES)] = (jnp.where(first, dq[0], dq[1]) * scale).astype(BF16)
        dqkv_ref[:, pl.ds(pl.multiple_of(out + third, LANES), LANES)] = (
            jnp.where(first, dk[0], dk[1])[:pad].astype(BF16)
        )
        dqkv_ref[:, pl.ds(pl.multiple_of(out + 2 * third, LANES), LANES)] = (
            jnp.where(first, dv[0], dv[1])[:pad].astype(BF16)
        )
        return carry

    lax.fori_loop(0, pairs, pair_step, 0, unroll=pairs)


def column_sums(out_ref, at, dqkv_ref):
    third = dqkv_ref.shape[1] // 3
    for row, part in ((4, 0), (5, 2)):
        lanes = slice(part * third, (part + 1) * third)
        out_ref[row : row + 1, at * third : (at + 1) * third] = jnp.sum(
            dqkv_ref[:, lanes].astype(F32), axis=0, keepdims=True
        )


def backward_body(
    heads,
    where_ref,
    dinner0_ref,
    dinner1_ref,
    hidden_ref,
    attended_ref,
    outgrad_ref,
    mask_ref,
    gain2_ref,
    gamma1_ref,
    wproj_ref,
    q_ref,
    k_ref,
    v_ref,
    probs_ref,
    dhidden_ref,
    dqkv_ref,
    out0_ref,
    out1_ref,
    out2_ref,
    out3_ref,
    dscores_ref,
    sums_ref,
    pad_s,
    dmixed_ref,
):
    width = hidden_ref.shape[1]
    cotangent = load_padded(outgrad_ref, pad_s) * mask_ref[:, 0:1]
    xhat, root = norm_stats(hidden_ref[...])
    dinner = dinner0_ref[...].astype(F32) + dinner1_ref[...].astype(F32)
    dhidden = cotangent + norm_back(dinner, xhat, root, row_of(gain2_ref))
    dhidden_ref[...] = dhidden
    datt = (row_of(gamma1_ref) * dhidden).astype(BF16)
    dmixed_ref[...] = dot_nt(datt, wproj_ref[...]).astype(BF16)
    sums_ref[0:1, :] = jnp.sum(dinner * xhat, axis=0, keepdims=True)
    sums_ref[1:2, :] = jnp.sum(dinner, axis=0, keepdims=True)
    sums_ref[2:3, :] = jnp.sum(dhidden * attended_ref[...], axis=0, keepdims=True)
    sums_ref[3:4, :] = jnp.sum(datt.astype(F32), axis=0, keepdims=True)
    sums_ref[4:8, :] = jnp.zeros((4, width), F32)
    heads_back(heads // 2, 0, width // heads, q_ref, k_ref, v_ref, probs_ref, dmixed_ref, dqkv_ref,
               dscores_ref)
    deal_out(
        where_ref, (out0_ref, out1_ref, out2_ref, out3_ref), dqkv_ref, datt
    )
    column_sums(sums_ref, 0, dqkv_ref)


def backward(heads, where, dinner0, dinner1, hidden, attended, out_grad, mask_col, gain2, gamma1,
             wproj, q, k, v, probs, deps=()):
    pad, width = hidden.shape
    keys = k.shape[0]
    outs = (
        shape((pad, width), F32),
        shape((pad, 3 * width), BF16),
        shape((pad, width), BF16),
        shape((pad, width), BF16),
        shape((pad, width), BF16),
        shape((pad, width), BF16),
        shape((heads, pad, keys), BF16),
        shape((8, width), F32),
    )
    return call(
        functools.partial(backward_body, heads),
        outs,
        "svvhvhhhhhhvvv",
        (where, dinner0, dinner1, hidden, attended, out_grad, mask_col, gain2, gamma1, wproj, q, k,
         v, probs),
        (pltpu.VMEM((pad, width), F32), pltpu.VMEM((pad, width), BF16)),
        cost=COST["back"],
        deps=deps,
    )


def first_norm_body(
    patches_ref, mask_ref, token_ref, gain1_ref, dqkv_ref, wqkv_ref, dhidden_ref,
    patchgrad_ref, sums_ref, pad_s,
):
    rows, width = patches_ref.shape[1:]
    picked = mask_ref[:, 0:1] > 0
    start = jnp.where(picked, row_of(token_ref), load_padded(patches_ref, pad_s))
    xhat, root = norm_stats(start)
    dnormed = dot_nt(dqkv_ref[...], wqkv_ref[...])
    dstart = dhidden_ref[...] + norm_back(dnormed, xhat, root, row_of(gain1_ref))
    patchgrad_ref[0] = jnp.where(picked, 0.0, dstart)[0:rows]
    sums_ref[0:1, :] = jnp.sum(jnp.where(picked, dstart, 0.0), axis=0, keepdims=True)
    sums_ref[1:2, :] = jnp.sum(dnormed * xhat, axis=0, keepdims=True)
    sums_ref[2:3, :] = jnp.sum(dnormed, axis=0, keepdims=True)
    sums_ref[3:8, :] = jnp.zeros((5, width), F32)


def first_norm(patches, mask_col, token, gain1, dqkv, wqkv, dhidden, deps=(), carry=()):
    rows, width = patches.shape[1:]
    pad = mask_col.shape[0]
    outs = (shape_out((1, rows, width), F32), shape((8, width), F32))
    return call(
        first_norm_body, outs, "hhhhvhv",
        (patches, mask_col, token, gain1, dqkv, wqkv, dhidden),
        (pltpu.VMEM((pad, width), F32),), cost=COST["norm"], deps=deps, carry=carry,
    )


def layer_end_body(hidden_ref, branch0_ref, branch1_ref, gamma2_ref, out_ref):
    branch = branch0_ref[...] + branch1_ref[...].astype(F32)
    layer = hidden_ref[...] + row_of(gamma2_ref) * branch
    out_ref[0] = layer[0 : out_ref.shape[1]].astype(BF16)


def layer_end(rows, hidden, branch0, branch1, gamma2, deps=(), carry=()):
    return call(
        layer_end_body, shape_out((1, rows, hidden.shape[1]), BF16), "hhvh",
        (hidden, branch0, branch1, gamma2), cost=COST["end"], deps=deps, carry=carry,
    )


def table_grad_body(
    where_ref, index_ref, ds_ref, sums_b_ref, sums_n_ref, sums0_ref, sums1_ref, sums_f_ref, out_ref,
    index_s,
    total_s,
):
    rows = index_ref.shape[0]
    pad, head_pad, keys = ds_ref.shape
    high_count = total_s.shape[0] // head_pad
    index_s[...] = jnp.zeros_like(index_s)
    index_s[0:rows, 0:rows] = index_ref[...]
    total_s[...] = jnp.zeros_like(total_s)
    below = lax.broadcasted_iota(jnp.int32, (LANES, keys), 0).astype(BF16)
    ones = jnp.ones((LANES, keys), BF16)
    group = 16

    def step(at, carry):
        base = pl.multiple_of(at * group, group)
        lines = index_s[pl.ds(base, group), :]
        low = (lines & (LANES - 1)).astype(F32).astype(BF16)
        high = (lines >> 7).astype(F32).astype(BF16)
        total = None
        for i in range(group):
            onehot = jnp.where(below == low[i : i + 1], ones, jnp.zeros_like(ones))
            ds = ds_ref[base + i]
            left = jnp.concatenate(
                [
                    jnp.where(high[i : i + 1] == jnp.asarray(part, BF16), ds, jnp.zeros_like(ds))
                    for part in range(high_count)
                ],
                axis=0,
            )
            one = dot_nt(left, onehot)
            total = one if total is None else total + one
        total_s[...] += total
        return carry

    lax.fori_loop(0, pad // group, step, 0, unroll=2)
    for part in range(high_count):
        out_ref[0:head_pad, part * LANES : (part + 1) * LANES] = total_s[
            part * head_pad : (part + 1) * head_pad
        ]
    sums = sums0_ref[...] + sums1_ref[...] + sums_f_ref[...]
    out_ref[head_pad : head_pad + 6, :] = sums_b_ref[0:6, :]
    out_ref[head_pad + 6 : head_pad + 8, :] = sums[2:4]
    out_ref[head_pad + 8 : head_pad + 11, :] = sums_n_ref[0:3, :]
    for part in range(4):
        mine = jnp.where(where_ref[0] == part // 2, 1.0, 0.0)
        own = jnp.where(where_ref[1] == part % 2, sums[0:1], sums[1:2])
        out_ref[head_pad + 11 + part : head_pad + 12 + part, :] = mine * own
    out_ref[head_pad + 15 :, :] = jnp.zeros_like(out_ref[head_pad + 15 :, :])


def table_grad(where, rel_index, dscores, sums_b, sums_n, sums0, sums1, sums_f, entries, deps=()):
    pad, head_pad, keys = dscores.shape
    high_count = round_up(entries, LANES) // LANES
    width = sums_b.shape[1]
    return call(
        table_grad_body, shape((head_pad + 16, width), F32), "shvvvvvv",
        (where, rel_index, dscores, sums_b, sums_n, sums0, sums1, sums_f),
        (pltpu.VMEM((pad, keys), jnp.int32), pltpu.VMEM((high_count * head_pad, LANES), F32)),
        cost=COST["table"], deps=deps,
    )


def late_grad_body(block, piece, where_ref, *refs):
    lefts, rights, send_ref, keep_ref = refs[:4], refs[4:8], refs[8], refs[9]
    total = None
    for step in range(4):
        half = rights[step].shape[1] // 2
        one = dot_tn(lefts[step][...], rights[step][:, piece * half : (piece + 1) * half])
        total = one if total is None else total + one
    split_rows(send_ref.at[0], keep_ref.at[0], total, where_ref[2] > 0, block)


def late_grad(where, block, piece, lefts, rights, deps=(), carry=()):
    width = lefts[0].shape[1]
    half = rights[0].shape[1] // 2
    outs = (shape((1, width // (2 * block), block, half), BF16),) * 2
    return call(
        functools.partial(late_grad_body, block, piece), outs, "shvvvvvvv",
        (where, *lefts, *rights), cost=COST["late"], deps=deps, carry=carry,
    )


def fold_body(bit, where_ref, keep_ref, met_ref, send_out, keep_out):
    low = where_ref[2 + bit] > 0
    for at in range(send_out.shape[0]):
        for step in range(send_out.shape[1]):
            even, odd = (
                keep_ref[at, 2 * step + side].astype(F32) + met_ref[at, 2 * step + side].astype(F32)
                for side in range(2)
            )
            send_out[at, step] = jnp.where(low, even, odd).astype(BF16)
            keep_out[at, step] = jnp.where(low, odd, even).astype(BF16)


def fold(where, bit, keep, met, deps=(), carry=()):
    items, count, block, width = keep.shape
    return call(
        functools.partial(fold_body, bit), (shape((items, count // 2, block, width), BF16),) * 2,
        "svv", (where, keep, met), cost=COST["fold"], deps=deps, carry=carry,
    )


def last_sum_body(keep_ref, met_ref, *outs):
    for at, out_ref in enumerate(outs):
        total = keep_ref[at, 0].astype(F32) + met_ref[at, 0].astype(F32)
        out_ref[...] = total.astype(out_ref.dtype)


def last_sum(keep, met, kind, deps=(), carry=()):
    make = shape_out if kind == F32 else shape
    return call(
        last_sum_body, (make(keep.shape[2:], kind),) * keep.shape[0], "vv", (keep, met), cost=COST["last"],
        deps=deps, carry=carry,
    )


def join_body(before_ref, keep_ref, met_ref, out_ref):
    half = before_ref.shape[1]
    out_ref[:, :half] = before_ref[...]
    out_ref[:, half:] = (keep_ref[0, 0].astype(F32) + met_ref[0, 0].astype(F32)).astype(BF16)


def join(before, keep, met, deps=(), carry=()):
    block, half = before.shape
    return call(
        join_body, shape((block, 2 * half), BF16), "vvv", (before, keep, met), cost=COST["join"], deps=deps,
        carry=carry,
    )


def assemble_body(where_ref, own_ref, over_x_ref, over_core_ref, qkv_ref, proj_ref):
    width = own_ref.shape[1]
    high = where_ref[0] > 0
    core = where_ref[1] > 0
    own, far = own_ref[...], over_x_ref[...]
    side, corner = over_core_ref[0], over_core_ref[1]
    here = (jnp.where(core, side, own), jnp.where(core, own, side))
    there = (jnp.where(core, corner, far), jnp.where(core, far, corner))
    for at in range(2):
        qkv_ref[:, at * width : (at + 1) * width] = jnp.where(high, there[at], here[at]).astype(F32)
    qkv_ref[:, 2 * width :] = jnp.where(high, here[0], there[0]).astype(F32)
    proj_ref[...] = jnp.where(high, here[1], there[1]).astype(F32)


def assemble(where, own, far, pair, deps=()):
    block, width = own.shape
    return call(
        assemble_body, (shape_out((block, 3 * width), F32), shape_out((block, width), F32)),
        "svvv", (where, own, far, pair), deps=deps,
    )


def on_device(
    dp,
    patches,
    row_mask,
    out_grad,
    rel_index,
    mask_token,
    ln1_gain,
    ln1_bias,
    qkv_weight,
    query_bias,
    value_bias,
    rel_table,
    proj_weight,
    proj_bias,
    gamma1,
    ln2_gain,
    ln2_bias,
    fc1_weight,
    fc1_bias,
    fc2_weight,
    fc2_bias,
    gamma2,
):
    rows, width = patches.shape[1:]
    entries, heads = rel_table.shape
    pad = round_up(rows, 16)
    mp_at = lax.axis_index("mp")
    dp_at = lax.axis_index("dp")
    x_at, core_at = mp_at // 2, mp_at % 2
    bits = dp.bit_length() - 1
    where = jnp.stack(
        [x_at, core_at] + [(dp_at >> bit) & 1 for bit in range(bits)]
    ).astype(jnp.int32)

    def swap(axis, bit):
        count = 4 if axis == "mp" else dp
        pairs = [(at, at ^ bit) for at in range(count)]
        return lambda value: lax.ppermute(value, axis, pairs)

    over_core, over_x = swap("mp", 1), swap("mp", 2)
    over_bit = [swap("dp", 1 << bit) for bit in range(bits)]

    out_grad1, row_mask1 = over_x(out_grad), over_x(row_mask)
    b1b, w1b, w2b = over_core(fc1_bias), over_core(fc1_weight), over_core(fc2_weight)

    before = []

    def step(kernel, *args, deps=(), **more):
        out, token = kernel(*args, deps=tuple(before) + tuple(deps), **more)
        before[:] = [token]
        return out

    mask_col, left0, left1, left2, left3, q, k, v, probs, attended, hidden, inner = step(
        forward, heads, pad, where, patches, row_mask, rel_index, mask_token, ln1_gain, ln1_bias,
        query_bias, value_bias, rel_table.T, proj_bias, gamma1, ln2_gain, ln2_bias, qkv_weight,
        proj_weight,
    )
    held = [k, v, probs, attended]

    def holding(kernel, *args, **more):
        out = step(kernel, *args, hold=tuple(held), **more)
        count = len(held)
        held[:] = out[-count:]
        out = tuple(out[:-count])
        return out if len(out) > 1 else out[0]

    inner1 = over_x(inner)
    weights = (fc1_bias, b1b, fc1_weight, w1b, fc2_weight, w2b)
    dbranch, dbranch1, cot1, acta0, actb0, dprea0, dpreb0, dinner0, sums0, branch0, left1 = holding(
        mlp, inner, weights, fc2_bias, (out_grad, out_grad1, row_mask, row_mask1, gamma2), True,
        carry=(left1,),
    )
    met_left1 = over_core(left1)
    acta1, actb1, dprea1, dpreb1, dinner1, sums1 = holding(
        mlp, inner1, weights, fc2_bias, (dbranch1,), False
    )
    dinner_in = over_x(dinner1)

    block = width // dp

    def middle(keep, met, first, last):
        for bit in range(first, last):
            send, keep = step(fold, where, bit, keep, met)
            met = over_bit[bit](send)
        return keep, met

    fc_other = over_core(
        holding(pair_grad, (inner, inner1, dpreb0, dpreb1), (dbranch, dbranch1, actb0, actb1))
    )
    branch1, sums_f = holding(far_branch, acta1, actb1, fc2_weight, w2b, cot1)
    fc_send, fc_kept, left2, left3 = holding(
        fc_keep, where, block, (inner, inner1, dprea0, dprea1), (dbranch, dbranch1, acta0, acta1),
        fc_other, deps=(met_left1,), carry=(left2, left3),
    )
    fc_met = over_bit[0](fc_send)
    met_left2, met_left3 = over_x(left2), swap("mp", 3)(left3)
    k, v, probs, attended = held

    dhidden, dqkv, own, core, far, corner, dscores, sums_b = step(
        backward, heads, where, dinner0, dinner_in, hidden, attended, out_grad, mask_col, ln2_gain,
        gamma1, proj_weight, q, k, v, probs,
    )
    met_far, met_corner, met_core = over_x(far), swap("mp", 3)(corner), over_core(core)
    head_pad = 16
    late = ((left0, met_left1, met_left2, met_left3), (own, met_core, met_far, met_corner))
    keep, met, made = {"f": fc_kept}, {"f": fc_met}, {}
    state = {"small": None, "branch": branch1, "own": None}

    def tailed(mark, kernel, *args, **more):
        names = [name for sign, name in (("@", "small"), ("%", "branch"), ("!", "own")) if sign in mark]
        carried = tuple(state[name] for name in names)
        out = step(kernel, *args, carry=carried, **more)
        if not names:
            return out
        state.update(zip(names, out[-len(names) :]))
        out = tuple(out[: -len(names)])
        return out if len(out) > 1 else out[0]

    def spread_on(name, mark, first, last):
        for bit in range(first, last):
            send, keep[name] = tailed(mark if bit == first else "", fold, where, bit, keep[name], met[name])
            met[name] = over_bit[bit](send)

    def hop(swaps):
        for swapped in swaps:
            state["small"] = state["small"] + swapped(state["small"])

    for item in ORDER:
        name, mark = item.rstrip("@%!"), item[len(item.rstrip("@%!")) :]
        if name == "N":
            made["patch"], made["sums"] = tailed(
                mark, first_norm, patches, mask_col, mask_token, ln1_gain, dqkv, qkv_weight, dhidden,
                deps=(met_left2, met_left3),
            )
        elif name == "T":
            ds = jnp.pad(
                jnp.transpose(dscores, (1, 0, 2)), ((0, 0), (0, head_pad - heads), (0, 0))
            )
            state["small"] = step(
                table_grad, where, rel_index, ds, sums_b, made["sums"], sums0, sums1, sums_f, entries
            )
            hop([over_core])
        elif name in ("A", "B"):
            send, keep[name] = tailed(mark, late_grad, where, block, "AB".index(name), *late)
            met[name] = over_bit[0](send)
        elif name in ("f1", "a1", "b1"):
            spread_on(name[0].upper() if name[0] != "f" else "f", mark, 1, 2)
        elif name in ("f2", "a2", "b2"):
            spread_on(name[0].upper() if name[0] != "f" else "f", mark, 2, bits)
        elif name == "x":
            hop([over_x])
        elif name == "y":
            hop([over_bit[0]])
        elif name == "z":
            hop([over_bit[1]])
        elif name == "w":
            hop(over_bit[2:])
        elif name == "h":
            made["branch"] = over_x(state["branch"])
        elif name == "E":
            made["layer"] = tailed(mark, layer_end, rows, hidden, branch0, made["branch"], gamma2)
        elif name == "F":
            made["fc"] = tailed(mark, last_sum, keep["f"], met["f"], F32)
        elif name == "S":
            made["A"] = tailed(mark, last_sum, keep["A"], met["A"], BF16)
        elif name == "J":
            state["own"] = tailed(mark, join, made["A"], keep["B"], met["B"])
            late_x = over_x(state["own"])
    small, late_own = state["small"], state["own"]
    patch_grad, layer_out = made["patch"], made["layer"]
    fc1_weight_grad, fc2_weight_grad = made["fc"]
    late_pair = over_core(jnp.stack([late_own, late_x]))
    qkv_weight_grad, proj_weight_grad = step(assemble, where, late_own, late_x, late_pair)

    rel_grad = small[:heads, :entries].T
    (ln2_gain_grad, ln2_bias_grad, gamma1_grad, proj_bias_grad, query_bias_grad, value_bias_grad,
     gamma2_grad, fc2_bias_grad, mask_token_grad, ln1_gain_grad, ln1_bias_grad) = [
        small[head_pad + at] for at in range(11)
    ]
    fc1_bias_grad = lax.dynamic_index_in_dim(small, head_pad + 11 + mp_at, 0, False)
    return (
        layer_out,
        patch_grad,
        mask_token_grad,
        ln1_gain_grad,
        ln1_bias_grad,
        qkv_weight_grad,
        query_bias_grad,
        value_bias_grad,
        rel_grad,
        proj_weight_grad,
        proj_bias_grad,
        gamma1_grad,
        ln2_gain_grad,
        ln2_bias_grad,
        fc1_weight_grad,
        fc1_bias_grad,
        fc2_weight_grad.T,
        fc2_bias_grad,
        gamma2_grad,
    )


def solution(mesh):
    rows3 = P(("dp", "mp"), None, None)
    placed = (
        (rows3, P(("dp", "mp"), None), rows3)
        + (P(),) * 13
        + (P(None, "mp"), P("mp"), P("mp", None), P(), P())
    )
    return jax.shard_map(
        functools.partial(on_device, mesh.shape["dp"]),
        mesh=mesh,
        in_specs=placed,
        out_specs=(
            rows3,
            rows3,
            P(),
            P(),
            P(),
            P("dp", None),
            P(),
            P(),
            P(),
            P("dp", None),
            P(),
            P(),
            P(),
            P(),
            P("dp", "mp"),
            P("mp"),
            P("mp", "dp"),
            P(),
            P(),
        ),
        check_vma=False,
    )
```
